32 devices in a mesh: dp: 4 (over z), blk: 4 (over x, core), head: 2 (over y).
Axes of the slice: x: 2, y: 2, z: 4, core: 2. Of those that a mesh axis runs over, the one named last changes fastest.
Arguments:
- tokens: bfloat16 [8, 1024, 2048], P('dp', ('blk', 'head')), may hold values from -6 to 6
- segments: int32 [8, 1024], P('dp'), may hold values from 0 to 3, never falling along the last dimension, each value on 1 to 512 neighbouring positions
- routes: int32 [8, 1024, 8], P('dp', ('blk', 'head')), may hold values from 0 to 31, all different within a row; in each aligned block of 128 rows (0 to 127, 128 to 255, ..., all dimensions but the last counted through in order) at most 36 rows name the same one
- cotangent: bfloat16 [8, 1024, 2048], P('dp', ('blk', 'head')), may hold values from -6 to 6
- attn_gain: float32 [2048], replicated, may hold values from 0.25 to 1.75
- qkv_weight: bfloat16 [2048, 5120], P('dp'), may hold values from -0.125 to 0.125
- q_gain: float32 [128], replicated, may hold values from 0.25 to 1.75
- k_gain: float32 [128], replicated, may hold values from 0.25 to 1.75
- out_weight: bfloat16 [2048, 4096], P('dp'), may hold values from -0.75 to 0.75
- ffn_gain: float32 [2048], replicated, may hold values from 0.25 to 1.75
- router_weight: bfloat16 [2048, 32], replicated, may hold values from -0.0625 to 0.0625
- gate_weight: bfloat16 [32, 2048, 768], P(('dp', 'blk', 'head')), may hold values from -0.125 to 0.125
- up_weight: bfloat16 [32, 2048, 768], P(('dp', 'blk', 'head')), may hold values from -0.125 to 0.125
- down_weight: bfloat16 [32, 768, 2048], P(('dp', 'blk', 'head')), may hold values from -0.875 to 0.875
Outputs:
- layer_out: bfloat16 [8, 1024, 2048], P('dp', ('blk', 'head'))
- input_grad: bfloat16 [8, 1024, 2048], P('dp', ('blk', 'head'))
- attn_gain_grad: float32 [2048], P(('dp', 'blk', 'head'))
- qkv_grad: float32 [2048, 5120], P(('dp', 'blk', 'head'))
- q_gain_grad: float32 [128], P(('dp', 'blk', 'head'))
- k_gain_grad: float32 [128], P(('dp', 'blk', 'head'))
- out_grad: float32 [2048, 4096], P(('dp', 'blk', 'head'))
- ffn_gain_grad: float32 [2048], P(('dp', 'blk', 'head'))
- router_grad: float32 [2048, 32], P(('dp', 'blk', 'head'))
- gate_grad: float32 [32, 2048, 768], P(('dp', 'blk', 'head'))
- up_grad: float32 [32, 2048, 768], P(('dp', 'blk', 'head'))
- down_grad: float32 [32, 768, 2048], P(('dp', 'blk', 'head'))
The draws below stay inside these ranges and needn't reach their ends.
Inputs may be any that keep to these rules, and one draw needn't show every extreme that they name: `segments`: within each sequence the document numbers never fall; every document covers 1 to 512 consecutive positions and one covers exactly 512. `routes`: each position names 8 different experts. In each aligned block of 128 positions of a sequence (the positions of one device) no expert is named more than 36 times, and in some blocks an expert is named exactly 36 times.
All inputs are finite; a program needn't handle non-finite values.
Results may differ from the reference program's by a relative error of at most 0.029.
Values may be sent and summed in bfloat16 or wider, within the bound.
No kernel may reach another device: no remote copies, remote signals or barrier semaphores. Data moves between devices by JAX's collectives and lax.ppermute only.
A program may use at most 384 MiB of HBM per device.

```python
import math
import jax
import jax.numpy as jnp
import numpy as np
from jax import lax

D = 2048
Q_HEADS = 32
KV_HEADS = 4
HEAD_DIM = 128
EXPERT_FF = 768
TOPK = 8
TOK_DEV = 128
QD = 4096
KVD = 512
QKV = 5120
LEN = 1024
SEQS = 8
EXPERTS = 32
CAP = 36
DOC_MOST = 512
DOCS = 4


def shard_levels(stream_key, extent, shards, least, high):
    level, own = 1.0, jax.random.fold_in(stream_key, 6)
    for dim, parts in shards:
        steps = jnp.exp(jax.random.uniform(jax.random.fold_in(own, dim), (parts,), jnp.float32, least / len(shards), high / len(shards)))
        level = level * jnp.repeat(steps, extent[dim] // parts).reshape([-1 if axis == dim else 1 for axis in range(len(extent))])
    return level


def length_profile(count, total, bound, slope):
    weights = [(1 << 20) // math.isqrt(standing ** slope) + 1 for standing in range(2, count + 1)]
    spare, counts = total - bound - (count - 1), [1] * (count - 1)
    while spare > 0:
        movable = [i for i in range(count - 1) if counts[i] < bound]
        whole, budget = sum([weights[i] for i in movable]), spare
        for i in movable:
            extra = min(bound - counts[i], max(1, budget * weights[i] // whole), spare)
            counts[i] = counts[i] + extra
            spare = spare - extra
    return np.array([bound] + counts)


def ragged(key, number_of, total, most, slope):
    if number_of == 2:
        one = jax.random.randint(key, (), max(1, total - most), min(most, total - 1) + 1)
        return jnp.stack([one, total - one])
    tallies = jnp.asarray(length_profile(number_of, total, most, slope), jnp.int32)
    twos = (number_of - 1) // 2
    source_of, receiver = tallies[1:1 + 2 * twos:2], tallies[2:2 + 2 * twos:2]
    slack = jnp.minimum(source_of - 1, most - receiver)
    passed = jax.random.randint(jax.random.fold_in(key, 1), (twos,), 0, 1 << 20) % (slack + 1)
    tallies = tallies.at[1:1 + 2 * twos:2].set(source_of - passed).at[2:2 + 2 * twos:2].set(receiver + passed)
    return tallies[jax.random.permutation(jax.random.fold_in(key, 2), number_of)]


def routed_block(key, own, number, rows, amount, top, reach, slope):
    ranking = jax.random.permutation(key, amount)
    crowded, ordinary = shares(amount, rows * top, reach, slope, True), shares(amount, rows * top, reach, slope, False)
    places = jnp.arange(amount)

    def named(lengths, turn):
        used = int((lengths > 0).sum())
        fixed = max(1, used // 4)
        moved = fixed + (places - fixed + turn * (used - fixed)) % max(1, amount - fixed)
        return jnp.zeros((amount,), jnp.int32).at[ranking[jnp.where(places < fixed, places, moved)]].set(jnp.asarray(lengths, jnp.int32))

    lengths = jnp.where(number % 4 == 0, named(crowded, number // 4), named(ordinary, number - number // 4 - 1))
    mixed = jax.random.permutation(jax.random.fold_in(own, 3), amount)
    source_of, receiver = mixed[0:amount // 2 * 2:2], mixed[1:amount // 2 * 2:2]
    margin = jnp.minimum(lengths[source_of] - 1, reach - lengths[receiver]) // 2
    margin = jnp.where((source_of == ranking[0]) | (receiver == ranking[0]) | (lengths[receiver] == 0), 0, jnp.maximum(margin, 0))
    moved = jax.random.randint(jax.random.fold_in(own, 4), (amount // 2,), 0, 1 << 20) % (margin + 1)
    lengths = lengths.at[source_of].add(-moved).at[receiver].add(moved)
    members = jnp.searchsorted(jnp.cumsum(lengths), jnp.arange(rows * top), side="right").astype(jnp.int32)
    grid = members.reshape(top, rows).T
    grid = grid[jax.random.permutation(jax.random.fold_in(own, 1), rows)]
    turn = jax.random.randint(jax.random.fold_in(own, 2), (rows, 1), 0, top)
    return jnp.take_along_axis(grid, (jnp.arange(top)[None, :] + turn) % top, axis=1)


def shares(count, total, reach, skew, full):
    weights = [(1 << 20) // math.isqrt(rank ** skew) + 1 for rank in range(1, count + 1)]
    largest = reach if full else min(reach, max(-(-total // count), total * weights[0] // sum(weights)))
    least = 1 if total - largest >= count - 1 else 0
    counts, spare = [largest] + [least] * (count - 1), total - largest - least * (count - 1)
    while spare > 0:
        candidates = [i for i in range(1, count) if counts[i] < largest] or [i for i in range(1, count) if counts[i] < reach]
        whole, left = sum([weights[i] for i in candidates]), spare
        for i in candidates:
            extra = min(reach - counts[i], max(1, left * weights[i] // whole), spare)
            counts[i] = counts[i] + extra
            spare = spare - extra
    return np.array(counts)


def centred(rng, shape, deviation, bound, shards=(), held_as=jnp.bfloat16):
    drawn = jax.random.normal(rng, shape, jnp.float32) * deviation
    if len(shards) > 0:
        drawn = shard_levels(rng, shape, shards, -0.22, 0.18) * drawn
    return jnp.clip(drawn, min=-bound, max=bound).astype(held_as)


def setup_inputs(seed: int = 0) -> dict:
    key_of = jax.random.split(jax.random.key(seed), 15)
    tokens = centred(key_of[0], (SEQS, LEN, D), 1.0, 6.0, ((0, 4), (1, 8)))
    segments = jax.vmap(lambda own: jnp.searchsorted(jnp.cumsum(ragged(own, DOCS, LEN, DOC_MOST, 2)), jnp.arange(LEN), side="right"))(jax.random.split(key_of[1], SEQS)).reshape((SEQS, LEN)).astype(jnp.int32)
    routes_keys = jax.random.split(jax.random.fold_in(key_of[2], 1), SEQS * LEN // TOK_DEV)
    routes_turns = jax.random.permutation(jax.random.fold_in(key_of[2], 3), SEQS * LEN // TOK_DEV)
    routes = jax.vmap(lambda own, number: routed_block(jax.random.fold_in(key_of[2], 2), own, number, TOK_DEV, EXPERTS, TOPK, CAP, 1))(routes_keys, routes_turns).reshape((SEQS, LEN, TOPK))
    cotangent = centred(key_of[3], (SEQS, LEN, D), 1.0, 6.0, ((0, 4), (1, 8)))
    attn_gain = jnp.clip(1.0 + 0.15 * jax.random.normal(key_of[4], (D,), jnp.float32), 0.25, 1.75)
    qkv_weight = centred(key_of[5], (D, QKV), D ** -0.5, 0.125, ((0, 4),))
    q_gain = jnp.clip(1.0 + 0.15 * jax.random.normal(key_of[6], (HEAD_DIM,), jnp.float32), 0.25, 1.75)
    k_gain = jnp.clip(1.0 + 0.15 * jax.random.normal(key_of[7], (HEAD_DIM,), jnp.float32), 0.25, 1.75)
    out_weight = centred(key_of[8], (D, QD), (QD // 64) ** -0.5, 0.75, ((0, 4),))
    ffn_gain = jnp.clip(1.0 + 0.15 * jax.random.normal(key_of[9], (D,), jnp.float32), 0.25, 1.75)
    router_weight = centred(key_of[10], (D, EXPERTS), (4 * D) ** -0.5, 0.0625)
    gate_weight = centred(key_of[11], (EXPERTS, D, EXPERT_FF), D ** -0.5, 0.125, ((0, 32),))
    up_weight = centred(key_of[12], (EXPERTS, D, EXPERT_FF), D ** -0.5, 0.125, ((0, 32),))
    down_weight = centred(key_of[13], (EXPERTS, EXPERT_FF, D), (EXPERT_FF // 16) ** -0.5, 0.875, ((0, 32),))
    return {"tokens": tokens, "segments": segments, "routes": routes, "cotangent": cotangent, "attn_gain": attn_gain, "qkv_weight": qkv_weight, "q_gain": q_gain, "k_gain": k_gain, "out_weight": out_weight, "ffn_gain": ffn_gain, "router_weight": router_weight, "gate_weight": gate_weight, "up_weight": up_weight, "down_weight": down_weight}


@jax.custom_vjp
def low(v):
    return lax.optimization_barrier(v.astype(jnp.bfloat16)).astype(jnp.float32)

@jax.custom_vjp
def low_back(v):
    return v

def low_keep(v):
    return (low(v), None)

def low_pass(kept, grad):
    return (grad,)

def back_keep(v):
    return (v, None)

def back_low(kept, grad):
    return (low(grad),)
low.defvjp(low_keep, low_pass)
low_back.defvjp(back_keep, back_low)
EPSILON = 1e-06
HIGHEST = lax.Precision.HIGHEST

def rms_scale(values, gain_vec):
    return values * lax.rsqrt(lax.optimization_barrier(jnp.mean(values * values, axis=-1, keepdims=True)) + EPSILON) * gain_vec

def rotary_tables(positions, head_width):
    half_width = head_width // 2
    frequency = 1000000.0 ** (-2.0 * jnp.arange(half_width, dtype=jnp.float32) / head_width)
    angles = positions.astype(jnp.float32)[:, None] * frequency[None, :]
    angles = jnp.concatenate([angles, angles], axis=-1)
    return (jnp.cos(angles), jnp.sin(angles))

def rotate(values, cosines, sines):
    half_width = values.shape[-1] // 2
    turned = jnp.concatenate([-values[..., half_width:], values[..., :half_width]], axis=-1)
    return values * cosines + turned * sines

def softmax_rows(scores):
    shifted = jnp.exp(scores - lax.optimization_barrier(jnp.max(scores, axis=-1, keepdims=True)))
    return shifted / lax.optimization_barrier(jnp.sum(shifted, axis=-1, keepdims=True))

def layer(layer_in, attn_gain, qkv_weight, q_gain, k_gain, out_weight, ffn_gain, router_weight, gate_weight, up_weight, down_weight, segment, route):
    seq_rows = layer_in.shape[0]
    group_size = Q_HEADS // KV_HEADS
    normed = low(rms_scale(layer_in, attn_gain))
    qkv_rows = low_back(jnp.dot(normed, qkv_weight, precision=HIGHEST))
    queries = qkv_rows[:, :QD].reshape(seq_rows, Q_HEADS, HEAD_DIM)
    keys_pre = qkv_rows[:, QD:QD + KVD].reshape(seq_rows, KV_HEADS, HEAD_DIM)
    values_all = low(low_back(qkv_rows[:, QD + KVD:].reshape(seq_rows, KV_HEADS, HEAD_DIM)))
    positions = jnp.arange(seq_rows, dtype=jnp.int32)
    cosines, sines = rotary_tables(positions, HEAD_DIM)
    queries = low(low_back(rotate(rms_scale(queries, q_gain), cosines[:, None], sines[:, None])))
    keys_all = low(low_back(rotate(rms_scale(keys_pre, k_gain), cosines[:, None], sines[:, None])))
    query_block = 512 if seq_rows % 512 == 0 else seq_rows
    block_count = seq_rows // query_block
    grouped = queries.reshape(block_count, query_block, KV_HEADS, group_size, HEAD_DIM)
    score_scale = 1.0 / math.sqrt(HEAD_DIM)

    def attend(inputs):
        query_rows, row_pos, row_seg = inputs
        scores = low_back(jnp.einsum('qhgd,khd->hgqk', query_rows, keys_all, precision=HIGHEST) * score_scale)
        allowed = (positions[None, :] <= row_pos[:, None]) & (segment[None, :] == row_seg[:, None])
        scores = jnp.where(allowed[None, None], scores, -jnp.inf)
        probs = low(softmax_rows(scores))
        return jnp.einsum('hgqk,khd->qhgd', probs, values_all, precision=HIGHEST)
    mixed = lax.map(jax.checkpoint(attend), (grouped, positions.reshape(block_count, query_block), segment.reshape(block_count, query_block)))
    attn_rows = low(low_back(mixed.reshape(seq_rows, QD)))
    middle = layer_in + low_back(jnp.dot(attn_rows, out_weight.T, precision=HIGHEST))
    normed2 = low(rms_scale(middle, ffn_gain))
    logits = low_back(jnp.dot(normed2, router_weight, precision=HIGHEST))
    gates = softmax_rows(jnp.take_along_axis(logits, route, axis=1))
    source_blocks = seq_rows // TOK_DEV
    flat_routes = route.reshape(source_blocks, TOK_DEV * TOPK)
    onehot = (flat_routes[:, :, None] == jnp.arange(EXPERTS, dtype=jnp.int32)[None, None, :]).astype(jnp.int32)
    earlier = (jnp.cumsum(onehot, axis=1).astype(jnp.int32) - onehot) * onehot
    ranks = lax.optimization_barrier(jnp.sum(earlier, axis=2)).astype(jnp.int32)
    slots = (ranks + jnp.arange(source_blocks, dtype=jnp.int32)[:, None] * CAP).reshape(-1).astype(jnp.int32)
    experts_of = route.reshape(-1).astype(jnp.int32)
    copies = low_back(jnp.broadcast_to(normed2[:, None, :], (seq_rows, TOPK, D))).reshape(seq_rows * TOPK, D)
    buffer = jnp.zeros((EXPERTS, source_blocks * CAP, D), jnp.float32).at[experts_of, slots].set(copies)
    gate_pre = low_back(jnp.einsum('erd,edf->erf', buffer, gate_weight, precision=HIGHEST))
    up_pre = low_back(jnp.einsum('erd,edf->erf', buffer, up_weight, precision=HIGHEST))
    hidden = low(low_back(gate_pre / (1.0 + jnp.exp(-gate_pre)) * up_pre))
    produced = low(low_back(jnp.einsum('erf,efd->erd', hidden, down_weight, precision=HIGHEST)))
    returned = produced[experts_of, slots].reshape(seq_rows, TOPK, D)
    return middle + lax.optimization_barrier(jnp.sum(gates[:, :, None] * returned, axis=1))

def reference(tokens, segments, routes, cotangent, attn_gain, qkv_weight, q_gain, k_gain, out_weight, ffn_gain, router_weight, gate_weight, up_weight, down_weight):
    params = (attn_gain.astype(jnp.float32), qkv_weight.astype(jnp.float32), q_gain.astype(jnp.float32), k_gain.astype(jnp.float32), out_weight.astype(jnp.float32), ffn_gain.astype(jnp.float32), router_weight.astype(jnp.float32), gate_weight.astype(jnp.float32), up_weight.astype(jnp.float32), down_weight.astype(jnp.float32))

    def one_sequence(totals, inputs):
        seq_tokens, seq_segment, seq_route, seq_cot = inputs

        def forward(layer_in, *weights):
            return layer(layer_in, *weights, seq_segment, seq_route)
        result, pull = jax.vjp(forward, seq_tokens.astype(jnp.float32), *params)
        grads = pull(seq_cot.astype(jnp.float32))
        totals = tuple((total + grad for total, grad in zip(totals, grads[1:])))
        return (totals, (result.astype(jnp.bfloat16), grads[0].astype(jnp.bfloat16)))
    zeros = tuple((jnp.zeros(weight.shape, jnp.float32) for weight in params))
    totals, outputs = lax.scan(one_sequence, zeros, (tokens, segments, routes, cotangent))
    return (outputs[0], outputs[1], totals[0], totals[1], totals[2], totals[3], totals[4], totals[5], totals[6], totals[7], totals[8], totals[9])
```

```python
import functools
import math

import jax
import jax.numpy as jnp
from jax import lax
from jax.experimental import pallas as pl
from jax.experimental.pallas import tpu as pltpu
from jax.sharding import PartitionSpec as P

Q_HEADS = 32
KV_HEADS = 4
HEAD_DIM = 128
EPSILON = 1e-06
NEG_FILL = -1e30
PLANE = ("blk", "head")
EVERY = ("dp", "blk", "head")
F32 = jnp.float32
BF16 = jnp.bfloat16


def dot_nn(a, b):
    return jnp.dot(a, b, preferred_element_type=F32)


def dot_nt(a, b):
    return lax.dot_general(a, b, (((1,), (1,)), ((), ())), preferred_element_type=F32)


def dot_tn(a, b):
    return lax.dot_general(a, b, (((0,), (0,)), ((), ())), preferred_element_type=F32)


def rms_parts(values):
    scale = lax.rsqrt(jnp.mean(values * values, axis=-1, keepdims=True) + EPSILON)
    return values * scale, scale


def rms_back(grad, unit, scale, gain_vec):
    scaled = grad * gain_vec
    return scale * (scaled - unit * jnp.mean(scaled * unit, axis=-1, keepdims=True))


def turn_head(unit, cosines, sines):
    return unit * cosines + pltpu.roll(unit, HEAD_DIM // 2, 1) * sines


def turn_back(grad, cosines, sines):
    return grad * cosines + pltpu.roll(grad * sines, HEAD_DIM // 2, 1)


def head_forward(raw, gain_row, cosines, sines):
    unit, scale = rms_parts(raw)
    return turn_head(unit * gain_row, cosines, sines), unit, scale


def fill_keys(heads, order_ref, qkv_ref, cos_ref, sin_ref, k_gain_ref, k_scr, v_scr):
    start = heads * HEAD_DIM

    def one(block, carry):
        place = order_ref[block]
        raw = qkv_ref[place, :, start : start + HEAD_DIM]
        turned, _, _ = head_forward(raw, k_gain_ref[...], cos_ref[block], sin_ref[block])
        k_scr[block] = turned.astype(BF16)
        v_scr[block] = qkv_ref[place, :, start + HEAD_DIM : start + 2 * HEAD_DIM].astype(BF16)
        return carry

    lax.fori_loop(0, qkv_ref.shape[0], one, 0)


def allowed_keys(row_seg, key_seg, row_block, key_block, heads):
    rows = lax.broadcasted_iota(jnp.int32, (row_seg.shape[0], key_seg.shape[1]), 0)
    cols = lax.broadcasted_iota(jnp.int32, (row_seg.shape[0], key_seg.shape[1]), 1)
    rows = rows + (row_block - key_block) * row_seg.shape[0]
    keep = jnp.where((row_seg == key_seg) & (cols <= rows), 0.0, NEG_FILL)
    return jnp.concatenate([keep] * heads, axis=0)


def attend_kernel(
    heads,
    score_scale,
    order_ref,
    low_ref,
    qkv_ref,
    cos_ref,
    sin_ref,
    q_gain_ref,
    k_gain_ref,
    seg_row_ref,
    seg_col_ref,
    attn_ref,
    stat_ref,
    k_scr,
    v_scr,
):
    block = pl.program_id(0)

    @pl.when(block == 0)
    def _():
        fill_keys(heads, order_ref, qkv_ref, cos_ref, sin_ref, k_gain_ref, k_scr, v_scr)

    place = order_ref[block]
    cosines, sines = cos_ref[block], sin_ref[block]
    rows = []
    for h in range(heads):
        raw = qkv_ref[place, :, h * HEAD_DIM : (h + 1) * HEAD_DIM]
        rows.append(head_forward(raw, q_gain_ref[...], cosines, sines)[0].astype(BF16))
    queries = jnp.concatenate(rows, axis=0)
    count = queries.shape[0]
    row_seg = seg_col_ref[block]

    def step(key_block, carry):
        top, total, acc = carry
        scores = dot_nt(queries, k_scr[key_block]) * score_scale
        scores = scores + allowed_keys(row_seg, seg_row_ref[key_block], block, key_block, heads)
        new_top = jnp.maximum(top, jnp.max(scores, axis=1, keepdims=True))
        shrink = jnp.exp(top - new_top)
        weights = jnp.exp(scores - new_top)
        total = total * shrink + jnp.sum(weights, axis=1, keepdims=True)
        acc = acc * shrink + dot_nn(weights.astype(BF16), v_scr[key_block])
        return new_top, total, acc

    first = step(
        block,
        (
            jnp.full((count, 1), NEG_FILL, F32),
            jnp.zeros((count, 1), F32),
            jnp.zeros((count, HEAD_DIM), F32),
        ),
    )
    top, total, acc = lax.fori_loop(low_ref[block], block, step, first)
    acc = acc / total
    size = attn_ref.shape[1]
    for h in range(heads):
        attn_ref[0, :, h * HEAD_DIM : (h + 1) * HEAD_DIM] = acc[h * size : (h + 1) * size].astype(
            BF16
        )
    stat_ref[0] = jnp.broadcast_to(top + jnp.log(total), (count, HEAD_DIM))


def attend_back_kernel(
    heads,
    score_scale,
    order_ref,
    low_ref,
    qkv_ref,
    cos_ref,
    sin_ref,
    q_gain_ref,
    k_gain_ref,
    seg_row_ref,
    seg_col_ref,
    attn_ref,
    grad_ref,
    stat_ref,
    out_ref,
    gain_ref,
    k_scr,
    v_scr,
    dk_scr,
    dv_scr,
):
    block = pl.program_id(0)
    blocks = pl.num_programs(0)
    start = heads * HEAD_DIM

    @pl.when(block == 0)
    def _():
        fill_keys(heads, order_ref, qkv_ref, cos_ref, sin_ref, k_gain_ref, k_scr, v_scr)
        dk_scr[...] = jnp.zeros_like(dk_scr)
        dv_scr[...] = jnp.zeros_like(dv_scr)
        gain_ref[...] = jnp.zeros_like(gain_ref)

    place = order_ref[block]
    cosines, sines = cos_ref[block], sin_ref[block]
    rows, units, scales, grads, deltas = [], [], [], [], []
    for h in range(heads):
        raw = qkv_ref[place, :, h * HEAD_DIM : (h + 1) * HEAD_DIM]
        turned, unit, scale = head_forward(raw, q_gain_ref[...], cosines, sines)
        rows.append(turned.astype(BF16))
        units.append(unit)
        scales.append(scale)
        grad = grad_ref[0, :, h * HEAD_DIM : (h + 1) * HEAD_DIM]
        grads.append(grad)
        attn = attn_ref[0, :, h * HEAD_DIM : (h + 1) * HEAD_DIM]
        deltas.append(jnp.sum(grad.astype(F32) * attn.astype(F32), axis=1, keepdims=True))
    queries = jnp.concatenate(rows, axis=0)
    grad_rows = jnp.concatenate(grads, axis=0)
    delta = jnp.concatenate(deltas, axis=0)
    stat = stat_ref[0]
    row_seg = seg_col_ref[block]
    count = queries.shape[0]

    def step(key_block, acc):
        keys, values = k_scr[key_block], v_scr[key_block]
        scores = dot_nt(queries, keys) * score_scale
        scores = scores + allowed_keys(row_seg, seg_row_ref[key_block], block, key_block, heads)
        probs = jnp.exp(scores - stat)
        grad_probs = dot_nt(grad_rows, values)
        grad_scores = (probs * (grad_probs - delta)).astype(BF16)
        dk_scr[key_block] += dot_tn(grad_scores, queries)
        dv_scr[key_block] += dot_tn(probs.astype(BF16), grad_rows)
        return acc + dot_nn(grad_scores, keys)

    acc = lax.fori_loop(
        low_ref[block], block + 1, step, jnp.zeros((count, HEAD_DIM), F32)
    )
    acc = acc * score_scale
    size = grad_ref.shape[1]
    gain_sum = jnp.zeros((1, HEAD_DIM), F32)
    for h in range(heads):
        grad = turn_back(acc[h * size : (h + 1) * size], cosines, sines)
        gain_sum = gain_sum + jnp.sum(grad * units[h], axis=0, keepdims=True)
        out_ref[place, :, h * HEAD_DIM : (h + 1) * HEAD_DIM] = rms_back(
            grad, units[h], scales[h], q_gain_ref[...]
        ).astype(BF16)
    gain_ref[0:1, :] += gain_sum

    @pl.when(block == blocks - 1)
    def _():
        def one(key_block, carry):
            spot = order_ref[key_block]
            raw = qkv_ref[spot, :, start : start + HEAD_DIM]
            unit, scale = rms_parts(raw)
            grad = turn_back(dk_scr[key_block] * score_scale, cos_ref[key_block], sin_ref[key_block])
            out_ref[spot, :, start : start + HEAD_DIM] = rms_back(
                grad, unit, scale, k_gain_ref[...]
            ).astype(BF16)
            out_ref[spot, :, start + HEAD_DIM : start + 2 * HEAD_DIM] = dv_scr[key_block].astype(
                BF16
            )
            return carry + jnp.sum(grad * unit, axis=0, keepdims=True)

        gain_ref[1:2, :] += lax.fori_loop(0, blocks, one, jnp.zeros((1, HEAD_DIM), F32))


def whole_block(shape):
    zeros = (0,) * len(shape)
    return pl.BlockSpec(shape, lambda block, order, low: zeros)


def row_block(shape):
    return pl.BlockSpec(shape, lambda block, order, low: (order[block], 0, 0))


def attention_inputs(qkv, tables, gains, segment):
    blocks, size, _ = qkv.shape
    rows = segment.reshape(blocks, 1, size)
    cols = segment.reshape(blocks, size, 1)
    arrays = (qkv, *tables, *gains, rows, cols)
    return arrays, [whole_block(a.shape) for a in arrays]


def attend(qkv, tables, gains, segment, order, low, heads):
    blocks, size, _ = qkv.shape
    arrays, specs = attention_inputs(qkv, tables, gains, segment)
    return pl.pallas_call(
        functools.partial(attend_kernel, heads, 1.0 / math.sqrt(HEAD_DIM)),
        grid_spec=pltpu.PrefetchScalarGridSpec(
            num_scalar_prefetch=2,
            grid=(blocks,),
            in_specs=specs,
            out_specs=[
                row_block((1, size, heads * HEAD_DIM)),
                row_block((1, heads * size, HEAD_DIM)),
            ],
            scratch_shapes=[pltpu.VMEM((blocks, size, HEAD_DIM), BF16)] * 2,
        ),
        out_shape=[
            jax.ShapeDtypeStruct((blocks, size, heads * HEAD_DIM), BF16),
            jax.ShapeDtypeStruct((blocks, heads * size, HEAD_DIM), F32),
        ],
        compiler_params=pltpu.CompilerParams(vmem_limit_bytes=48 * 2**20),
    )(order, low, *arrays)


def attend_back(qkv, tables, gains, segment, order, low, heads, attn, grad, stat):
    blocks, size, width = qkv.shape
    arrays, specs = attention_inputs(qkv, tables, gains, segment)
    return pl.pallas_call(
        functools.partial(attend_back_kernel, heads, 1.0 / math.sqrt(HEAD_DIM)),
        grid_spec=pltpu.PrefetchScalarGridSpec(
            num_scalar_prefetch=2,
            grid=(blocks,),
            in_specs=specs
            + [
                row_block((1, size, heads * HEAD_DIM)),
                row_block((1, size, heads * HEAD_DIM)),
                row_block((1, heads * size, HEAD_DIM)),
            ],
            out_specs=[whole_block((blocks, size, width)), whole_block((8, HEAD_DIM))],
            scratch_shapes=[pltpu.VMEM((blocks, size, HEAD_DIM), BF16)] * 2
            + [pltpu.VMEM((blocks, size, HEAD_DIM), F32)] * 2,
        ),
        out_shape=[
            jax.ShapeDtypeStruct((blocks, size, width), BF16),
            jax.ShapeDtypeStruct((8, HEAD_DIM), F32),
        ],
        compiler_params=pltpu.CompilerParams(vmem_limit_bytes=56 * 2**20),
    )(order, low, *arrays, attn, grad, stat)


def ring_steps(ways):
    ring = list(range(1, ways, 2)) + list(range(0, ways, 2))[::-1]
    return [(ring[i], ring[(i + 1) % ways]) for i in range(ways)]


def line_gather(rows, ways):
    held, out = rows, [rows]
    for _ in range(ways - 1):
        held = lax.ppermute(held, "dp", ring_steps(ways))
        out.append(held)
    return jnp.concatenate(out, axis=0)


def line_reduce(parts, ways):
    size = parts.shape[0] // ways
    back = [(b, a) for a, b in ring_steps(ways)]
    acc = parts[(ways - 1) * size :]
    for k in range(ways - 2, -1, -1):
        acc = lax.ppermute(acc, "dp", back)
        acc = (acc.astype(F32) + parts[k * size : (k + 1) * size].astype(F32)).astype(BF16)
    return acc


def paired(blk_ways, head_ways):
    return blk_ways == 4 and head_ways == 2


def flips(bit):
    return [(i, i ^ bit) for i in range(8)]


def plane_flips(turn):
    return (flips(4), flips(1)) if turn % 2 == 0 else (flips(1), flips(4))


def plane_gather(rows, turn, pair):
    if not pair:
        return lax.all_gather(rows, PLANE, axis=0, tiled=False)
    first, second = plane_flips(turn)
    two = jnp.stack([rows, lax.ppermute(rows, PLANE, first)])
    four = jnp.concatenate([two, lax.ppermute(two, PLANE, second)])
    return jnp.concatenate([four, lax.ppermute(four, PLANE, flips(2))])


def plane_order(plane_index, plane_ways, turn, pair):
    blocks = jnp.arange(plane_ways, dtype=jnp.int32)
    if not pair:
        return blocks
    away = blocks ^ plane_index
    x, core, y = (away >> 2) & 1, (away >> 1) & 1, away & 1
    near, far = (x, y) if turn % 2 == 0 else (y, x)
    return (core * 4 + far * 2 + near).astype(jnp.int32)


def plane_reduce(parts, turn, pair):
    if not pair:
        return lax.psum_scatter(parts, PLANE, scatter_dimension=0, tiled=False)
    first, second = plane_flips(turn)
    for half, move in ((4, flips(2)), (2, second), (1, first)):
        came = lax.ppermute(parts[half:], PLANE, move)
        parts = (parts[:half].astype(F32) + came.astype(F32)).astype(BF16)
    return parts[0]


def plane_exchange(rows):
    return lax.all_to_all(rows, PLANE, split_axis=0, concat_axis=0, tiled=True)


def body(
    tokens,
    segments,
    routes,
    cotangent,
    attn_gain,
    qkv_weight,
    q_gain,
    k_gain,
    out_weight,
    ffn_gain,
    router_weight,
    gate_weight,
    up_weight,
    down_weight,
):
    seqs, size, width = tokens.shape
    dp_ways = lax.axis_size("dp")
    blk_ways = lax.axis_size("blk")
    head_ways = lax.axis_size("head")
    plane_ways = blk_ways * head_ways
    pair = paired(blk_ways, head_ways)
    dp_index = lax.axis_index("dp")
    plane_index = lax.axis_index("blk") * head_ways + lax.axis_index("head")
    seq_total = segments.shape[1]
    experts = router_weight.shape[1]
    top_count = routes.shape[2]
    capacity = (9 * size * top_count + 8 * experts - 1) // (8 * experts)
    query_dim = Q_HEADS * HEAD_DIM
    kv_dim = KV_HEADS * HEAD_DIM
    heads = Q_HEADS // plane_ways
    share = plane_ways // KV_HEADS
    kv_index = plane_index // share
    local_dim = heads * HEAD_DIM
    extra = -(-2 * experts // 128) * 128

    weight_rows = qkv_weight.shape[0]

    def columns(weight, start, count):
        return lax.dynamic_slice(weight, (0, start), (weight_rows, count))

    qkv_local = lax.all_gather(
        jnp.concatenate(
            [
                columns(qkv_weight, plane_index * local_dim, local_dim),
                columns(qkv_weight, query_dim + kv_index * HEAD_DIM, HEAD_DIM),
                columns(qkv_weight, query_dim + kv_dim + kv_index * HEAD_DIM, HEAD_DIM),
            ],
            axis=1,
        ),
        "dp",
        axis=0,
        tiled=True,
    )
    out_local = lax.all_gather(
        columns(out_weight, plane_index * local_dim, local_dim), "dp", axis=0, tiled=True
    )

    half = HEAD_DIM // 2
    frequency = 1000000.0 ** (-2.0 * jnp.arange(half, dtype=F32) / HEAD_DIM)
    angles = jnp.arange(seq_total, dtype=jnp.int32).astype(F32)[:, None] * frequency[None, :]
    cosines, sines = jnp.cos(angles), jnp.sin(angles)
    tables = (
        jnp.concatenate([cosines, cosines], axis=1).reshape(plane_ways, size, HEAD_DIM),
        jnp.concatenate([-sines, sines], axis=1).reshape(plane_ways, size, HEAD_DIM),
    )
    gains = (q_gain[None], k_gain[None])
    attn_gain_row, ffn_gain_row = attn_gain[None], ffn_gain[None]

    expert_ids = dp_index * plane_ways + jnp.arange(plane_ways, dtype=jnp.int32)
    before = (
        jnp.arange(size, dtype=jnp.int32)[:, None] > jnp.arange(size, dtype=jnp.int32)[None, :]
    ).astype(BF16)
    slot_ids = jnp.arange(dp_ways * capacity, dtype=jnp.int32)

    def picks_of(route):
        line_routes = line_gather(route, dp_ways)
        chosen = jnp.any(line_routes[:, :, None] == expert_ids[None, None, :], axis=1)
        chosen = chosen.reshape(dp_ways, size, plane_ways)
        ranks = jnp.einsum(
            "ij,zje->zie", before, chosen.astype(BF16), preferred_element_type=F32
        ).astype(jnp.int32)
        ranks = ranks + jnp.arange(dp_ways, dtype=jnp.int32)[:, None, None] * capacity
        keys = jnp.where(chosen, ranks, -1).reshape(dp_ways * size, plane_ways).T
        picks = (keys[:, None, :] == slot_ids[None, :, None]).astype(BF16)
        return picks.reshape(plane_ways * dp_ways * capacity, dp_ways * size)

    picks = [picks_of(routes[s]) for s in range(seqs)]

    def dispatch(rows, s):
        return plane_exchange(dot_nn(picks[s], line_gather(rows, dp_ways)).astype(BF16))

    def collect(rows, s):
        return line_reduce(dot_tn(picks[s], plane_exchange(rows)).astype(BF16), dp_ways)

    orders, lows = [], []
    for s in range(seqs):
        blocks = segments[s].reshape(plane_ways, size)
        lows.append(
            jnp.sum(
                (blocks[None, :, size - 1] < blocks[:, None, 0]).astype(jnp.int32), axis=1
            ).astype(jnp.int32)
        )
        orders.append(plane_order(plane_index, plane_ways, s, pair))

    inputs, units, scales, spread = [], [], [], []
    for s in range(seqs):
        rows = tokens[s].astype(F32)
        unit, scale = rms_parts(rows)
        inputs.append(rows)
        units.append(unit)
        scales.append(scale)
        spread.append(plane_gather((unit * attn_gain_row).astype(BF16), s, pair))
    cot_rows = [dispatch(cotangent[s], s) for s in range(seqs)]
    projected, attended, stats, middles = [], [], [], []
    for s in range(seqs):
        qkv = dot_nn(spread[s].reshape(seq_total, width), qkv_local)
        qkv = qkv.reshape(plane_ways, size, local_dim + 2 * HEAD_DIM)
        attn, stat = attend(qkv, tables, gains, segments[s], orders[s], lows[s], heads)
        mixed = dot_nt(attn.reshape(seq_total, local_dim), out_local).astype(BF16)
        mixed = plane_reduce(mixed.reshape(plane_ways, size, width), s, pair)
        projected.append(qkv)
        attended.append(attn)
        stats.append(stat)
        middles.append(inputs[s] + mixed.astype(F32))

    normed2s, mid_units, mid_scales, gate_tables, came = [], [], [], [], []
    for s in range(seqs):
        unit, scale = rms_parts(middles[s])
        normed2 = (unit * ffn_gain_row).astype(BF16)
        logits = dot_nn(normed2, router_weight)
        chosen = jnp.any(
            routes[s][:, :, None] == jnp.arange(experts, dtype=jnp.int32)[None, None, :], axis=1
        )
        top = jnp.max(jnp.where(chosen, logits, -jnp.inf), axis=1, keepdims=True)
        powers = jnp.where(chosen, jnp.exp(jnp.where(chosen, logits - top, 0.0)), 0.0)
        gates = powers / jnp.sum(powers, axis=1, keepdims=True)
        coarse = gates.astype(BF16)
        fine = (gates - coarse.astype(F32)).astype(BF16)
        payload = [normed2, coarse, fine]
        if extra > 2 * experts:
            payload.append(jnp.zeros((size, extra - 2 * experts), BF16))
        normed2s.append(normed2)
        mid_units.append(unit)
        mid_scales.append(scale)
        gate_tables.append(gates)
        came.append(dispatch(jnp.concatenate(payload, axis=1), s))

    gate_w, up_w, down_w = gate_weight[0], up_weight[0], down_weight[0]
    expert_id = dp_index * plane_ways + plane_index
    extra_ids = jnp.arange(extra, dtype=jnp.int32)
    mine_coarse = (extra_ids == expert_id).astype(F32)[None, :]
    mine_fine = (extra_ids == experts + expert_id).astype(F32)[None, :]
    mine = mine_coarse + mine_fine
    kept = []
    grad_backs, out_backs = [], []
    for s in range(seqs):
        rows = came[s][:, :width]
        gate = jnp.sum(came[s][:, width:].astype(F32) * mine, axis=1, keepdims=True)
        gate_pre = dot_nn(rows, gate_w)
        up_pre = dot_nn(rows, up_w)
        pulled = dot_nt(cot_rows[s], down_w)
        sigma = 1.0 / (1.0 + jnp.exp(-gate_pre))
        hidden = (gate_pre * sigma * up_pre).astype(BF16).astype(F32)
        gate_grad_rows = jnp.sum(hidden * pulled, axis=1, keepdims=True)
        gated = (hidden * gate).astype(BF16)
        grad_hidden = pulled * gate
        grad_gate = (grad_hidden * up_pre * sigma * (1.0 + gate_pre * (1.0 - sigma))).astype(BF16)
        grad_up = (grad_hidden * gate_pre * sigma).astype(BF16)
        grad_rows = (dot_nt(grad_gate, gate_w) + dot_nt(grad_up, up_w)).astype(BF16)
        coarse = gate_grad_rows.astype(BF16)
        fine = gate_grad_rows - coarse.astype(F32)
        tail = (coarse.astype(F32) * mine_coarse + fine * mine_fine).astype(BF16)
        grad_backs.append(collect(jnp.concatenate([grad_rows, tail], axis=1), s))
        kept.append((rows, gated, cot_rows[s], grad_gate, grad_up))
    for s in range(seqs):
        out_backs.append(collect(dot_nn(kept[s][1], down_w).astype(BF16), s))
    layer_out = jnp.stack(
        [(middles[s] + out_backs[s].astype(F32)).astype(BF16) for s in range(seqs)]
    )
    every = [jnp.concatenate([kept[s][i] for s in range(seqs)], axis=0) for i in range(5)]
    gate_grad = dot_tn(every[0], every[3])
    up_grad = dot_tn(every[0], every[4])
    down_grad = dot_tn(every[1], every[2])

    grad_mids, grad_spread = [], []
    router_grad = jnp.zeros((width, experts), F32)
    ffn_sum = jnp.zeros((width,), F32)
    for s in range(seqs):
        tail = grad_backs[s][:, width:].astype(F32)
        gates = gate_tables[s]
        grad_gates = tail[:, :experts] + tail[:, experts : 2 * experts]
        grad_logits = (
            gates * (grad_gates - jnp.sum(gates * grad_gates, axis=1, keepdims=True))
        ).astype(BF16)
        router_grad = router_grad + dot_tn(normed2s[s], grad_logits)
        grad_normed2 = grad_backs[s][:, :width].astype(F32) + dot_nt(grad_logits, router_weight)
        ffn_sum = ffn_sum + jnp.sum(grad_normed2 * mid_units[s], axis=0)
        grad_mid = cotangent[s].astype(F32) + rms_back(
            grad_normed2, mid_units[s], mid_scales[s], ffn_gain_row
        )
        grad_mids.append(grad_mid)
        grad_spread.append(plane_gather(grad_mid.astype(BF16), s, pair))
    grad_qkvs, grad_ins = [], []
    head_sums = jnp.zeros((2, HEAD_DIM), F32)
    for s in range(seqs):
        flat = grad_spread[s].reshape(seq_total, width)
        grad_attn = dot_nn(flat, out_local).astype(BF16).reshape(plane_ways, size, local_dim)
        grad_qkv, sums = attend_back(
            projected[s],
            tables,
            gains,
            segments[s],
            orders[s],
            lows[s],
            heads,
            attended[s],
            grad_attn,
            stats[s],
        )
        head_sums = head_sums + sums[:2]
        grad_qkv = grad_qkv.reshape(seq_total, local_dim + 2 * HEAD_DIM)
        grad_qkvs.append(grad_qkv)
        grad_normed = dot_nt(grad_qkv, qkv_local).astype(BF16)
        grad_normed = plane_reduce(grad_normed.reshape(plane_ways, size, width), s, pair)
        grad_in = rms_back(grad_normed.astype(F32), units[s], scales[s], attn_gain_row)
        grad_ins.append((grad_mids[s] + grad_in).astype(BF16))
    input_grad = jnp.stack(grad_ins)

    def shared_grad(lefts, rights):
        total = sum(
            dot_tn(a.reshape(seq_total, -1), b.reshape(seq_total, -1))
            for a, b in zip(lefts, rights)
        ).astype(BF16)
        total = lax.psum_scatter(total, "dp", scatter_dimension=0, tiled=True)
        return plane_exchange(total).reshape(plane_ways, weight_rows // plane_ways, -1)

    def side_by_side(pieces):
        return pieces.transpose(1, 0, 2).reshape(pieces.shape[1], -1)

    out_grad = side_by_side(shared_grad(grad_spread, attended)).astype(F32)
    pieces = shared_grad(spread, grad_qkvs).astype(F32)
    row_count = pieces.shape[1]

    def kv_columns(start):
        part = pieces[:, :, start : start + HEAD_DIM]
        return side_by_side(part.reshape(KV_HEADS, share, row_count, HEAD_DIM).sum(axis=1))

    qkv_grad = jnp.concatenate(
        [
            side_by_side(pieces[:, :, :local_dim]),
            kv_columns(local_dim),
            kv_columns(local_dim + HEAD_DIM),
        ],
        axis=1,
    )
    own_rows = lax.dynamic_slice(
        qkv_weight, (plane_index * row_count, 0), (row_count, qkv_weight.shape[1])
    )
    own_gain = lax.dynamic_slice(
        attn_gain, ((dp_index * plane_ways + plane_index) * row_count,), (row_count,)
    )
    attn_gain_grad = jnp.sum(own_rows.astype(F32) * qkv_grad, axis=1) / own_gain

    def every_reduce(parts):
        return jnp.sum(
            lax.all_to_all(parts, EVERY, split_axis=0, concat_axis=0, tiled=True), axis=0
        )

    devices = dp_ways * plane_ways
    small = every_reduce(
        jnp.concatenate(
            [router_grad.reshape(devices, -1), ffn_sum.reshape(devices, -1)], axis=1
        )
    )
    head_small = every_reduce(
        head_sums.reshape(2, devices, -1).transpose(1, 0, 2).reshape(devices, -1)
    )
    head_small = head_small.reshape(2, -1)
    cut = row_count * experts
    return (
        layer_out,
        input_grad,
        attn_gain_grad,
        qkv_grad,
        head_small[0],
        head_small[1],
        out_grad,
        small[cut:],
        small[:cut].reshape(row_count, experts),
        gate_grad[None],
        up_grad[None],
        down_grad[None],
    )


def solution(mesh):
    placed = (
        P("dp", PLANE, None),
        P("dp", None),
        P("dp", PLANE, None),
        P("dp", PLANE, None),
        P(),
        P("dp", None),
        P(),
        P(),
        P("dp", None),
        P(),
        P(),
        P(EVERY, None, None),
        P(EVERY, None, None),
        P(EVERY, None, None),
    )
    return jax.shard_map(
        body,
        mesh=mesh,
        in_specs=placed,
        out_specs=(
            P("dp", PLANE, None),
            P("dp", PLANE, None),
            P(EVERY),
            P(EVERY, None),
            P(EVERY),
            P(EVERY),
            P(EVERY, None),
            P(EVERY),
            P(EVERY, None),
            P(EVERY, None, None),
            P(EVERY, None, None),
            P(EVERY, None, None),
        ),
        check_vma=False,
    )
```

```python
import functools
import math

import jax
import jax.numpy as jnp
from jax import lax
from jax.experimental import pallas as pl
from jax.experimental.layout import Layout, with_layout_constraint
from jax.experimental.pallas import tpu as pltpu
from jax.sharding import PartitionSpec as P

Q_HEADS = 32
KV_HEADS = 4
HEAD_DIM = 128
EPSILON = 1e-06
NEG_FILL = -1e30
LOG2E = 1.4426950408889634
PLANE = ("blk", "head")
EVERY = ("dp", "blk", "head")
F32 = jnp.float32
BF16 = jnp.bfloat16


def dot_nn(a, b):
    return jnp.dot(a, b, preferred_element_type=F32)


def dot_nt(a, b):
    return lax.dot_general(a, b, (((1,), (1,)), ((), ())), preferred_element_type=F32)


def dot_tn(a, b):
    return lax.dot_general(a, b, (((0,), (0,)), ((), ())), preferred_element_type=F32)


def rms_parts(values):
    scale = lax.rsqrt(jnp.mean(values * values, axis=-1, keepdims=True) + EPSILON)
    return values * scale, scale


def rms_back(grad, unit, scale, gain_vec):
    scaled = grad * gain_vec
    return scale * (scaled - unit * jnp.mean(scaled * unit, axis=-1, keepdims=True))


def turn_head(unit, cosines, sines):
    return unit * cosines + pltpu.roll(unit, HEAD_DIM // 2, 1) * sines


def turn_back(grad, cosines, sines):
    return grad * cosines + pltpu.roll(grad * sines, HEAD_DIM // 2, 1)


def head_forward(raw, gain_row, cosines, sines):
    unit, scale = rms_parts(raw)
    return turn_head(unit * gain_row, cosines, sines), unit, scale


def fill_keys(heads, order_ref, qkv_ref, cos_ref, sin_ref, k_gain_ref, k_scr, v_scr):
    start = heads * HEAD_DIM
    if v_scr.shape[2] > HEAD_DIM:
        v_scr[:, :, HEAD_DIM:] = jnp.ones_like(v_scr[:, :, HEAD_DIM:])

    def one(block, carry):
        place = order_ref[block]
        raw = qkv_ref[place, :, start : start + HEAD_DIM]
        turned, _, _ = head_forward(raw, k_gain_ref[...], cos_ref[block], sin_ref[block])
        k_scr[block] = turned.astype(BF16)
        values = qkv_ref[place, :, start + HEAD_DIM : start + 2 * HEAD_DIM].astype(BF16)
        v_scr[block, :, :HEAD_DIM] = values
        return carry

    lax.fori_loop(0, qkv_ref.shape[0], one, 0)


def allowed_keys(row_seg, key_seg, row_block, key_block, heads):
    rows = lax.broadcasted_iota(jnp.int32, (row_seg.shape[0], key_seg.shape[1]), 0)
    cols = lax.broadcasted_iota(jnp.int32, (row_seg.shape[0], key_seg.shape[1]), 1)
    rows = rows + (row_block - key_block) * row_seg.shape[0]
    keep = jnp.where((row_seg == key_seg) & (cols <= rows), 0.0, NEG_FILL)
    return jnp.concatenate([keep] * heads, axis=0)


def attend_kernel(
    heads,
    score_scale,
    order_ref,
    low_ref,
    qkv_ref,
    cos_ref,
    sin_ref,
    q_gain_ref,
    k_gain_ref,
    seg_row_ref,
    seg_col_ref,
    attn_ref,
    stat_ref,
    k_scr,
    v_scr,
):
    block = pl.program_id(0)

    @pl.when(block == 0)
    def _():
        fill_keys(heads, order_ref, qkv_ref, cos_ref, sin_ref, k_gain_ref, k_scr, v_scr)

    place = order_ref[block]
    cosines, sines = cos_ref[block], sin_ref[block]
    rows = []
    for h in range(heads):
        raw = qkv_ref[place, :, h * HEAD_DIM : (h + 1) * HEAD_DIM]
        rows.append(head_forward(raw, q_gain_ref[...], cosines, sines)[0].astype(BF16))
    queries = jnp.concatenate(rows, axis=0)
    count = queries.shape[0]
    row_seg = seg_col_ref[block]

    def step(key_block, carry):
        scores = dot_nt(queries, k_scr[key_block]) * (score_scale * LOG2E)
        scores = scores + allowed_keys(row_seg, seg_row_ref[key_block], block, key_block, heads)
        return carry + dot_nn(jnp.exp2(scores).astype(BF16), v_scr[key_block])

    both = lax.fori_loop(
        low_ref[block], block + 1, step, jnp.zeros((count, 2 * HEAD_DIM), F32)
    )
    acc, total = both[:, :HEAD_DIM], both[:, HEAD_DIM:]
    acc = acc / total
    size = attn_ref.shape[1]
    for h in range(heads):
        attn_ref[0, :, h * HEAD_DIM : (h + 1) * HEAD_DIM] = acc[h * size : (h + 1) * size].astype(
            BF16
        )
    stat_ref[0] = jnp.log2(total)


def attend_back_kernel(
    heads,
    score_scale,
    order_ref,
    low_ref,
    qkv_ref,
    cos_ref,
    sin_ref,
    q_gain_ref,
    k_gain_ref,
    seg_row_ref,
    seg_col_ref,
    attn_ref,
    grad_ref,
    stat_ref,
    out_ref,
    gain_ref,
    k_scr,
    v_scr,
    dk_scr,
    dv_scr,
):
    block = pl.program_id(0)
    blocks = pl.num_programs(0)
    start = heads * HEAD_DIM

    @pl.when(block == 0)
    def _():
        fill_keys(heads, order_ref, qkv_ref, cos_ref, sin_ref, k_gain_ref, k_scr, v_scr)
        dk_scr[...] = jnp.zeros_like(dk_scr)
        dv_scr[...] = jnp.zeros_like(dv_scr)
        gain_ref[...] = jnp.zeros_like(gain_ref)

    place = order_ref[block]
    cosines, sines = cos_ref[block], sin_ref[block]
    rows, units, scales, grads, deltas = [], [], [], [], []
    for h in range(heads):
        raw = qkv_ref[place, :, h * HEAD_DIM : (h + 1) * HEAD_DIM]
        turned, unit, scale = head_forward(raw, q_gain_ref[...], cosines, sines)
        rows.append(turned.astype(BF16))
        units.append(unit)
        scales.append(scale)
        grad = grad_ref[0, :, h * HEAD_DIM : (h + 1) * HEAD_DIM]
        grads.append(grad)
        attn = attn_ref[0, :, h * HEAD_DIM : (h + 1) * HEAD_DIM]
        deltas.append(jnp.sum(grad.astype(F32) * attn.astype(F32), axis=1, keepdims=True))
    queries = jnp.concatenate(rows, axis=0)
    grad_rows = jnp.concatenate(grads, axis=0)
    delta = jnp.concatenate(deltas, axis=0)
    stat = stat_ref[0]
    row_seg = seg_col_ref[block]
    count = queries.shape[0]

    def step(key_block, acc):
        keys, values = k_scr[key_block], v_scr[key_block]
        scores = dot_nt(queries, keys) * (score_scale * LOG2E)
        scores = scores + allowed_keys(row_seg, seg_row_ref[key_block], block, key_block, heads)
        probs = jnp.exp2(scores - stat)
        grad_probs = dot_nt(grad_rows, values)
        grad_scores = (probs * (grad_probs - delta)).astype(BF16)
        dk_scr[key_block] += dot_tn(grad_scores, queries)
        dv_scr[key_block] += dot_tn(probs.astype(BF16), grad_rows)
        return acc + dot_nn(grad_scores, keys)

    acc = lax.fori_loop(
        low_ref[block], block + 1, step, jnp.zeros((count, HEAD_DIM), F32)
    )
    acc = acc * score_scale
    size = grad_ref.shape[1]
    gain_sum = jnp.zeros((1, HEAD_DIM), F32)
    for h in range(heads):
        grad = turn_back(acc[h * size : (h + 1) * size], cosines, sines)
        gain_sum = gain_sum + jnp.sum(grad * units[h], axis=0, keepdims=True)
        out_ref[place, :, h * HEAD_DIM : (h + 1) * HEAD_DIM] = rms_back(
            grad, units[h], scales[h], q_gain_ref[...]
        ).astype(BF16)
    gain_ref[0:1, :] += gain_sum

    @pl.when(block == blocks - 1)
    def _():
        def one(key_block, carry):
            spot = order_ref[key_block]
            raw = qkv_ref[spot, :, start : start + HEAD_DIM]
            unit, scale = rms_parts(raw)
            grad = turn_back(dk_scr[key_block] * score_scale, cos_ref[key_block], sin_ref[key_block])
            out_ref[spot, :, start : start + HEAD_DIM] = rms_back(
                grad, unit, scale, k_gain_ref[...]
            ).astype(BF16)
            out_ref[spot, :, start + HEAD_DIM : start + 2 * HEAD_DIM] = dv_scr[key_block].astype(
                BF16
            )
            return carry + jnp.sum(grad * unit, axis=0, keepdims=True)

        gain_ref[1:2, :] += lax.fori_loop(0, blocks, one, jnp.zeros((1, HEAD_DIM), F32))


def whole_block(shape):
    zeros = (0,) * len(shape)
    return pl.BlockSpec(shape, lambda block, order, low: zeros)


def row_block(shape):
    return pl.BlockSpec(shape, lambda block, order, low: (order[block], 0, 0))


def attention_inputs(qkv, tables, gains, segment):
    blocks, size, _ = qkv.shape
    rows = segment.reshape(blocks, 1, size)
    cols = segment.reshape(blocks, size, 1)
    arrays = (qkv, *tables, *gains, rows, cols)
    return arrays, [whole_block(a.shape) for a in arrays]


def attend(qkv, tables, gains, segment, order, low, heads):
    blocks, size, _ = qkv.shape
    arrays, specs = attention_inputs(qkv, tables, gains, segment)
    return pl.pallas_call(
        functools.partial(attend_kernel, heads, 1.0 / math.sqrt(HEAD_DIM)),
        grid_spec=pltpu.PrefetchScalarGridSpec(
            num_scalar_prefetch=2,
            grid=(blocks,),
            in_specs=specs,
            out_specs=[
                row_block((1, size, heads * HEAD_DIM)),
                row_block((1, heads * size, HEAD_DIM)),
            ],
            scratch_shapes=[
                pltpu.VMEM((blocks, size, HEAD_DIM), BF16),
                pltpu.VMEM((blocks, size, 2 * HEAD_DIM), BF16),
            ],
        ),
        out_shape=[
            jax.ShapeDtypeStruct((blocks, size, heads * HEAD_DIM), BF16),
            jax.ShapeDtypeStruct((blocks, heads * size, HEAD_DIM), F32),
        ],
        compiler_params=pltpu.CompilerParams(vmem_limit_bytes=48 * 2**20),
        cost_estimate=pl.CostEstimate(
            flops=2**24 * blocks * heads, bytes_accessed=qkv.size * 8, transcendentals=0
        ),
    )(order, low, *arrays)


def attend_back(qkv, tables, gains, segment, order, low, heads, attn, grad, stat):
    blocks, size, width = qkv.shape
    arrays, specs = attention_inputs(qkv, tables, gains, segment)
    return pl.pallas_call(
        functools.partial(attend_back_kernel, heads, 1.0 / math.sqrt(HEAD_DIM)),
        grid_spec=pltpu.PrefetchScalarGridSpec(
            num_scalar_prefetch=2,
            grid=(blocks,),
            in_specs=specs
            + [
                row_block((1, size, heads * HEAD_DIM)),
                row_block((1, size, heads * HEAD_DIM)),
                row_block((1, heads * size, HEAD_DIM)),
            ],
            out_specs=[whole_block((blocks, size, width)), whole_block((8, HEAD_DIM))],
            scratch_shapes=[pltpu.VMEM((blocks, size, HEAD_DIM), BF16)] * 2
            + [pltpu.VMEM((blocks, size, HEAD_DIM), F32)] * 2,
        ),
        out_shape=[
            jax.ShapeDtypeStruct((blocks, size, width), BF16),
            jax.ShapeDtypeStruct((8, HEAD_DIM), F32),
        ],
        compiler_params=pltpu.CompilerParams(vmem_limit_bytes=56 * 2**20),
        cost_estimate=pl.CostEstimate(
            flops=2**24 * blocks * heads * 2, bytes_accessed=qkv.size * 12, transcendentals=0
        ),
    )(order, low, *arrays, attn, grad, stat)


def expert_kernel(
    experts,
    expert_ref,
    rows_ref,
    gates_ref,
    cot_ref,
    gate_w_ref,
    up_w_ref,
    down_w_ref,
    gated_ref,
    grad_gate_ref,
    grad_up_ref,
    back_ref,
    out_ref,
):
    width = rows_ref.shape[1]
    rows = rows_ref[...]
    spots = lax.broadcasted_iota(jnp.int32, gates_ref.shape, 1)
    coarse_spot = spots == expert_ref[0]
    fine_spot = spots == expert_ref[0] + experts
    gate = jnp.sum(
        jnp.where(coarse_spot | fine_spot, gates_ref[...].astype(F32), 0.0), axis=1, keepdims=True
    )
    gate_pre = dot_nn(rows, gate_w_ref[...])
    up_pre = dot_nn(rows, up_w_ref[...])
    pulled = dot_nt(cot_ref[...], down_w_ref[...])
    sigma = 1.0 / (1.0 + jnp.exp(-gate_pre))
    swish = gate_pre * sigma
    hidden = (swish * up_pre).astype(BF16).astype(F32)
    gate_grad = jnp.sum(hidden * pulled, axis=1, keepdims=True)
    gated = (hidden * gate).astype(BF16)
    grad_hidden = pulled * gate
    grad_gate = (grad_hidden * up_pre * (sigma + swish * (1.0 - sigma))).astype(BF16)
    grad_up = (grad_hidden * swish).astype(BF16)
    gated_ref[...] = gated
    grad_gate_ref[...] = grad_gate
    grad_up_ref[...] = grad_up
    back_ref[:, :width] = (
        dot_nt(grad_gate, gate_w_ref[...]) + dot_nt(grad_up, up_w_ref[...])
    ).astype(BF16)
    coarse = gate_grad.astype(BF16).astype(F32)
    back_ref[:, width:] = jnp.where(
        coarse_spot, coarse, jnp.where(fine_spot, gate_grad - coarse, 0.0)
    ).astype(BF16)
    out_ref[...] = dot_nn(gated, down_w_ref[...]).astype(BF16)


def expert_pass(came, cot, gate_w, up_w, down_w, expert_id, experts):
    count, full = came.shape
    width, hidden = gate_w.shape
    block = max(b for b in range(16, 385, 16) if count % b == 0)
    extra = full - width

    def rows_of(columns, place=0):
        return pl.BlockSpec((block, columns), lambda i, e: (i, place))

    def kept(shape):
        return pl.BlockSpec(shape, lambda i, e: (0, 0), pipeline_mode=pl.Buffered(1))

    return pl.pallas_call(
        functools.partial(expert_kernel, experts),
        grid_spec=pltpu.PrefetchScalarGridSpec(
            num_scalar_prefetch=1,
            grid=(count // block,),
            in_specs=[
                rows_of(width),
                rows_of(extra, width // extra),
                rows_of(width),
                kept(gate_w.shape),
                kept(up_w.shape),
                kept(down_w.shape),
            ],
            out_specs=[rows_of(hidden)] * 3 + [rows_of(full), rows_of(width)],
        ),
        out_shape=[jax.ShapeDtypeStruct((count, hidden), BF16)] * 3
        + [
            jax.ShapeDtypeStruct((count, full), BF16),
            jax.ShapeDtypeStruct((count, width), BF16),
        ],
        compiler_params=pltpu.CompilerParams(vmem_limit_bytes=58 * 2**20),
        cost_estimate=pl.CostEstimate(
            flops=count * width * hidden * 3, bytes_accessed=count * width * 4, transcendentals=0
        ),
    )(expert_id.reshape(1), came, came, cot, gate_w, up_w, down_w)


def by_rows(array):
    return with_layout_constraint(array, Layout(major_to_minor=tuple(range(array.ndim))))


def ring_steps(ways):
    ring = list(range(1, ways, 2)) + list(range(0, ways, 2))[::-1]
    return [(ring[i], ring[(i + 1) % ways]) for i in range(ways)]


def line_gather(rows, ways):
    held, out = rows, [rows]
    for _ in range(ways - 1):
        held = lax.ppermute(held, "dp", ring_steps(ways))
        out.append(held)
    return jnp.concatenate(out, axis=0)


def ring_jumps(ways, count):
    ring = [a for a, _ in ring_steps(ways)]
    return [(ring[i], ring[(i + count) % ways]) for i in range(ways)]


def line_spread(rows, ways):
    blocks = [lax.ppermute(rows, "dp", ring_jumps(ways, k)) for k in range(1, ways)]
    return jnp.concatenate([rows] + blocks, axis=0)


def line_sum(parts, ways):
    size = parts.shape[0] // ways
    total = parts[:size].astype(F32)
    for k in range(1, ways):
        part = parts[k * size : (k + 1) * size]
        total = total + lax.ppermute(part, "dp", ring_jumps(ways, -k)).astype(F32)
    return total


def line_reduce(part, ways):
    back = [(b, a) for a, b in ring_steps(ways)]
    acc = part(ways - 1)
    for k in range(ways - 2, -1, -1):
        acc = lax.ppermute(acc, "dp", back)
        acc = yield (acc.astype(F32) + part(k).astype(F32)).astype(BF16)


def plane_gather_steps(rows, turn, pair):
    if not pair:
        yield lax.all_gather(rows, PLANE, axis=0, tiled=False)
        return
    first, second = plane_flips(turn)
    two = yield jnp.stack([rows, lax.ppermute(rows, PLANE, first)])
    four = yield jnp.concatenate([two, lax.ppermute(two, PLANE, second)])
    yield jnp.concatenate([four, lax.ppermute(four, PLANE, flips(2))])


def together(*moves):
    held = [next(move) for move in moves]
    while True:
        if len(held) > 1:
            held = [by_rows(h) for h in tie(*held)]
        after = []
        for move, value in zip(moves, held):
            try:
                after.append(move.send(value))
            except StopIteration:
                after.append(value)
        if all(a is b for a, b in zip(after, held)):
            return held
        held = after


def paired(blk_ways, head_ways):
    return blk_ways == 4 and head_ways == 2


def flips(bit):
    return [(i, i ^ bit) for i in range(8)]


def plane_flips(turn):
    return (flips(4), flips(1)) if turn % 2 == 0 else (flips(1), flips(4))


def plane_order(plane_index, plane_ways, turn, pair):
    blocks = jnp.arange(plane_ways, dtype=jnp.int32)
    if not pair:
        return blocks
    away = blocks ^ plane_index
    x, core, y = (away >> 2) & 1, (away >> 1) & 1, away & 1
    near, far = (x, y) if turn % 2 == 0 else (y, x)
    return (core * 4 + far * 2 + near).astype(jnp.int32)


def plane_reduce(product, turn, pair):
    if not pair:
        yield lax.psum_scatter(product(0, None), PLANE, scatter_dimension=0, tiled=False)
        return
    first, second = plane_flips(turn)
    away = lax.ppermute(product(4, 8), PLANE, flips(2))
    parts = yield (product(0, 4).astype(F32) + away.astype(F32)).astype(BF16)
    for half, move in ((2, second), (1, first)):
        came = lax.ppermute(parts[half:], PLANE, move)
        parts = (parts[:half].astype(F32) + came.astype(F32)).astype(BF16)
        if half > 1:
            parts = yield parts
    yield parts[0]


def tie(*arrays):
    return lax.optimization_barrier(arrays)


def every_exchange(rows):
    return lax.all_to_all(rows, EVERY, split_axis=0, concat_axis=0, tiled=True)


def plane_exchange(rows):
    return lax.all_to_all(rows, PLANE, split_axis=0, concat_axis=0, tiled=True)


def body(
    tokens,
    segments,
    routes,
    cotangent,
    attn_gain,
    qkv_weight,
    q_gain,
    k_gain,
    out_weight,
    ffn_gain,
    router_weight,
    gate_weight,
    up_weight,
    down_weight,
):
    seqs, size, width = tokens.shape
    dp_ways = lax.axis_size("dp")
    blk_ways = lax.axis_size("blk")
    head_ways = lax.axis_size("head")
    plane_ways = blk_ways * head_ways
    pair = paired(blk_ways, head_ways)
    dp_index = lax.axis_index("dp")
    plane_index = lax.axis_index("blk") * head_ways + lax.axis_index("head")
    seq_total = segments.shape[1]
    experts = router_weight.shape[1]
    top_count = routes.shape[2]
    capacity = (9 * size * top_count + 8 * experts - 1) // (8 * experts)
    query_dim = Q_HEADS * HEAD_DIM
    kv_dim = KV_HEADS * HEAD_DIM
    heads = Q_HEADS // plane_ways
    share = plane_ways // KV_HEADS
    kv_index = plane_index // share
    local_dim = heads * HEAD_DIM
    extra = -(-2 * experts // 128) * 128

    weight_rows = qkv_weight.shape[0]

    def columns(weight, start, count):
        return lax.dynamic_slice(weight, (0, start), (weight_rows, count))

    qkv_local = lax.all_gather(
        jnp.concatenate(
            [
                columns(qkv_weight, plane_index * local_dim, local_dim),
                columns(qkv_weight, query_dim + kv_index * HEAD_DIM, HEAD_DIM),
                columns(qkv_weight, query_dim + kv_dim + kv_index * HEAD_DIM, HEAD_DIM),
            ],
            axis=1,
        ),
        "dp",
        axis=0,
        tiled=True,
    )
    out_local = lax.all_gather(
        columns(out_weight, plane_index * local_dim, local_dim), "dp", axis=0, tiled=True
    )

    half = HEAD_DIM // 2
    frequency = 1000000.0 ** (-2.0 * jnp.arange(half, dtype=F32) / HEAD_DIM)
    angles = jnp.arange(seq_total, dtype=jnp.int32).astype(F32)[:, None] * frequency[None, :]
    cosines, sines = jnp.cos(angles), jnp.sin(angles)
    tables = (
        jnp.concatenate([cosines, cosines], axis=1).reshape(plane_ways, size, HEAD_DIM),
        jnp.concatenate([-sines, sines], axis=1).reshape(plane_ways, size, HEAD_DIM),
    )
    gains = (q_gain[None], k_gain[None])
    attn_gain_row, ffn_gain_row = attn_gain[None], ffn_gain[None]

    expert_ids = dp_index * plane_ways + jnp.arange(plane_ways, dtype=jnp.int32)
    before = (
        jnp.arange(size, dtype=jnp.int32)[:, None] > jnp.arange(size, dtype=jnp.int32)[None, :]
    ).astype(BF16)
    slot_ids = jnp.arange(dp_ways * capacity, dtype=jnp.int32)

    spots = jnp.array([[a for a, _ in ring_steps(dp_ways)].index(i) for i in range(dp_ways)], jnp.int32)
    ring_slots = (spots[dp_index] - spots) % dp_ways
    ring = jnp.array([a for a, _ in ring_steps(dp_ways)], jnp.int32)
    dp_index_of_slot = ring[(spots[dp_index] - jnp.arange(dp_ways)) % dp_ways]
    line_routes = line_gather(routes.reshape(1, seqs * size, top_count), dp_ways)
    line_routes = line_routes.reshape(dp_ways, seqs, size, top_count)

    def picks_of(s):
        seen = line_routes[:, s].reshape(dp_ways * size, top_count)
        chosen = jnp.any(seen[:, :, None] == expert_ids[None, None, :], axis=1)
        chosen = chosen.reshape(dp_ways, size, plane_ways)
        ranks = jnp.einsum(
            "ij,zje->zie", before, chosen.astype(BF16), preferred_element_type=F32
        ).astype(jnp.int32)
        ranks = ranks + jnp.arange(dp_ways, dtype=jnp.int32)[:, None, None] * capacity
        keys = jnp.where(chosen, ranks, -1)

        def table(keys):
            keys = keys.reshape(dp_ways * size, plane_ways).T
            picks = (keys[:, None, :] == slot_ids[None, :, None]).astype(BF16)
            return picks.reshape(plane_ways * dp_ways * capacity, dp_ways * size)

        return table(keys), table(jnp.take(keys, ring_slots, axis=0))

    picks, straight_picks = zip(*[picks_of(s) for s in range(seqs)])

    last = []

    def exchange(rows, move=plane_exchange):
        if last:
            rows, _ = tie(rows, last.pop())
        out = move(rows)
        last.append(out)
        return out

    def pack(line_rows, table):
        return dot_nn(table, line_rows).astype(BF16)

    def unpack(rows, s):
        return dot_tn(picks[s], rows).astype(BF16)

    orders, lows = [], []
    for s in range(seqs):
        blocks = segments[s].reshape(plane_ways, size)
        lows.append(
            jnp.sum(
                (blocks[None, :, size - 1] < blocks[:, None, 0]).astype(jnp.int32), axis=1
            ).astype(jnp.int32)
        )
        orders.append(plane_order(plane_index, plane_ways, s, pair))

    inputs, units, scales, spread = [], [], [], []
    for s in range(seqs):
        rows = tokens[s].astype(F32)
        unit, scale = rms_parts(rows)
        inputs.append(rows)
        units.append(unit)
        scales.append(scale)
        spread.append(plane_gather_steps((unit * attn_gain_row).astype(BF16), s, pair))
    *spread, qkv_local = tie(*together(*spread), qkv_local)
    spread = [by_rows(rows) for rows in spread]

    def times(left, right):
        def product(start, stop):
            rows = left[start:stop]
            count = rows.shape[0]
            out = dot_nt(rows.reshape(count * size, -1), right).astype(BF16)
            return out.reshape(count, size, width)

        return product

    lines, held = [], out_local
    for s in range(seqs):
        rows, held = tie(cotangent[s], held)
        held = line_spread(rows, dp_ways)
        lines.append(pack(held, picks[s]))
    projected, attended, stats, mixes = [], [], [], []
    for s in range(seqs):
        qkv = dot_nn(spread[s].reshape(seq_total, width), qkv_local)
        qkv = qkv.reshape(plane_ways, size, local_dim + 2 * HEAD_DIM)
        attn, stat = attend(qkv, tables, gains, segments[s], orders[s], lows[s], heads)
        projected.append(qkv)
        attended.append(attn)
        stats.append(stat)
        mixes.append(together(plane_reduce(times(attn, out_local), s, pair))[0])
    lines[0], *mixes = tie(lines[0], *mixes)
    cot_rows = [exchange(rows) for rows in lines]

    middles, normed2s, mid_units, mid_scales, gate_tables, came = [], [], [], [], [], []
    for s in range(seqs):
        middle = inputs[s] + mixes[s].astype(F32)
        unit, scale = rms_parts(middle)
        normed2 = (unit * ffn_gain_row).astype(BF16)
        logits = dot_nn(normed2, router_weight)
        chosen = jnp.any(
            routes[s][:, :, None] == jnp.arange(experts, dtype=jnp.int32)[None, None, :], axis=1
        )
        top = jnp.max(jnp.where(chosen, logits, -jnp.inf), axis=1, keepdims=True)
        powers = jnp.where(chosen, jnp.exp(jnp.where(chosen, logits - top, 0.0)), 0.0)
        gates = powers / jnp.sum(powers, axis=1, keepdims=True)
        coarse = gates.astype(BF16)
        fine = (gates - coarse.astype(F32)).astype(BF16)
        payload = [normed2, coarse, fine]
        if extra > 2 * experts:
            payload.append(jnp.zeros((size, extra - 2 * experts), BF16))
        middles.append(middle)
        normed2s.append(normed2)
        mid_units.append(unit)
        mid_scales.append(scale)
        gate_tables.append(gates)
        came.append(
            exchange(pack(line_gather(jnp.concatenate(payload, axis=1), dp_ways), picks[s]))
        )

    gate_w, up_w, down_w = gate_weight[0], up_weight[0], down_weight[0]
    expert_id = (dp_index * plane_ways + plane_index).astype(jnp.int32)
    kept, grad_lines, produced = [], [], []
    for s in range(seqs):
        gated, grad_gate, grad_up, back, out = expert_pass(
            came[s], cot_rows[s], gate_w, up_w, down_w, expert_id, experts
        )
        if s:
            back, grad_lines[-1] = tie(back, grad_lines[-1])
        grad_lines.append(exchange(back))
        produced.append(out)
        kept.append((came[s][:, :width], gated, cot_rows[s], grad_gate, grad_up))
    out_lines, grad_mids, reduced = [], [], []
    router_grad = jnp.zeros((width, experts), F32)
    ffn_sum = jnp.zeros((width,), F32)
    for s in range(seqs):
        back = unpack(grad_lines[s], s)
        if s == 0:
            back, kept = tie(back, kept)
        reduced.append(line_sum(back, dp_ways))
    out_lines.append(exchange(produced[0]))
    for s in range(seqs):
        tail = reduced[s][:, width:]
        gates = gate_tables[s]
        grad_gates = tail[:, :experts] + tail[:, experts : 2 * experts]
        grad_logits = (
            gates * (grad_gates - jnp.sum(gates * grad_gates, axis=1, keepdims=True))
        ).astype(BF16)
        router_grad = router_grad + dot_tn(normed2s[s], grad_logits)
        grad_normed2 = reduced[s][:, :width] + dot_nt(grad_logits, router_weight)
        ffn_sum = ffn_sum + jnp.sum(grad_normed2 * mid_units[s], axis=0)
        grad_mids.append(
            cotangent[s].astype(F32)
            + rms_back(grad_normed2, mid_units[s], mid_scales[s], ffn_gain_row)
        )

    gate_grad = sum(dot_tn(rows, grad) for rows, _, _, grad, _ in kept)
    up_grad = sum(dot_tn(rows, grad) for rows, _, _, _, grad in kept)
    down_grad = sum(dot_tn(gated, cot) for _, gated, cot, _, _ in kept)
    *grad_mids, out_lines[0], gate_grad, up_grad, down_grad = tie(
        *grad_mids, out_lines[0], gate_grad, up_grad, down_grad
    )
    grad_spread = together(
        *[plane_gather_steps(grad_mids[s].astype(BF16), s, pair) for s in range(seqs)]
    )
    devices = dp_ways * plane_ways

    def outcome(s):
        back = dot_tn(straight_picks[s], out_lines[s]).astype(BF16)
        back = lax.psum_scatter(back, "dp", scatter_dimension=0, tiled=True)
        return (middles[s] + back.astype(F32)).astype(BF16)

    for s in range(1, seqs):
        rows, *grad_spread = tie(produced[s], *grad_spread)
        grad_spread = [by_rows(g) for g in grad_spread]
        out_lines.append(exchange(rows))
    grad_qkvs, grad_ins = [], []
    head_sums = jnp.zeros((2, HEAD_DIM), F32)
    for s in range(seqs):
        flat = grad_spread[s].reshape(seq_total, width)
        grad_attn = dot_nn(flat, out_local).astype(BF16).reshape(plane_ways, size, local_dim)
        grad_qkv, sums = attend_back(
            projected[s],
            tables,
            gains,
            segments[s],
            orders[s],
            lows[s],
            heads,
            attended[s],
            grad_attn,
            stats[s],
        )
        head_sums = head_sums + sums[:2]
        grad_qkvs.append(grad_qkv)
    *grad_qkvs, out_lines[-1] = tie(*grad_qkvs, out_lines[-1])
    small = exchange(
        jnp.concatenate(
            [
                router_grad.reshape(devices, -1),
                ffn_sum.reshape(devices, -1),
                head_sums[0].reshape(devices, -1),
                head_sums[1].reshape(devices, -1),
            ],
            axis=1,
        ),
        every_exchange,
    )

    def total_over(lefts, rights):
        return sum(
            dot_tn(a.reshape(seq_total, -1), b.reshape(seq_total, -1))
            for a, b in zip(lefts, rights)
        ).astype(BF16)

    total = total_over(spread, grad_qkvs)
    *grad_normeds, qkv_rows = together(
        *[plane_reduce(times(grad_qkvs[s], qkv_local), s, pair) for s in range(seqs)],
        line_reduce(
            lambda k: lax.dynamic_slice_in_dim(
                total, dp_index_of_slot[k] * weight_rows, weight_rows
            ),
            dp_ways,
        ),
    )
    for s in range(seqs):
        grad_in = rms_back(grad_normeds[s].astype(F32), units[s], scales[s], attn_gain_row)
        grad_ins.append((grad_mids[s] + grad_in).astype(BF16))
    input_grad = jnp.stack(grad_ins)
    layer_out = jnp.stack([outcome(s) for s in range(seqs)])

    def rows_of_plane(total):
        return plane_exchange(total).reshape(plane_ways, weight_rows // plane_ways, -1)

    def side_by_side(pieces):
        return pieces.transpose(1, 0, 2).reshape(pieces.shape[1], -1)

    out_total = lax.psum_scatter(
        total_over(grad_spread, attended), "dp", scatter_dimension=0, tiled=True
    )
    out_grad = side_by_side(rows_of_plane(out_total)).astype(F32)
    pieces = rows_of_plane(qkv_rows).astype(F32)
    row_count = pieces.shape[1]

    def kv_columns(start):
        part = pieces[:, :, start : start + HEAD_DIM]
        return side_by_side(part.reshape(KV_HEADS, share, row_count, HEAD_DIM).sum(axis=1))

    qkv_grad = jnp.concatenate(
        [
            side_by_side(pieces[:, :, :local_dim]),
            kv_columns(local_dim),
            kv_columns(local_dim + HEAD_DIM),
        ],
        axis=1,
    )
    own_rows = lax.dynamic_slice(
        qkv_weight, (plane_index * row_count, 0), (row_count, qkv_weight.shape[1])
    )
    own_gain = lax.dynamic_slice(
        attn_gain, ((dp_index * plane_ways + plane_index) * row_count,), (row_count,)
    )
    attn_gain_grad = jnp.sum(own_rows.astype(F32) * qkv_grad, axis=1) / own_gain

    small = jnp.sum(small, axis=0)
    head_small = small[-2 * (HEAD_DIM // devices) :].reshape(2, -1)
    cut = row_count * experts
    return (
        layer_out,
        input_grad,
        attn_gain_grad,
        qkv_grad,
        head_small[0],
        head_small[1],
        out_grad,
        small[cut : cut + row_count],
        small[:cut].reshape(row_count, experts),
        gate_grad[None],
        up_grad[None],
        down_grad[None],
    )


def solution(mesh):
    placed = (
        P("dp", PLANE, None),
        P("dp", None),
        P("dp", PLANE, None),
        P("dp", PLANE, None),
        P(),
        P("dp", None),
        P(),
        P(),
        P("dp", None),
        P(),
        P(),
        P(EVERY, None, None),
        P(EVERY, None, None),
        P(EVERY, None, None),
    )
    return jax.shard_map(
        body,
        mesh=mesh,
        in_specs=placed,
        out_specs=(
            P("dp", PLANE, None),
            P("dp", PLANE, None),
            P(EVERY),
            P(EVERY, None),
            P(EVERY),
            P(EVERY),
            P(EVERY, None),
            P(EVERY),
            P(EVERY, None),
            P(EVERY, None, None),
            P(EVERY, None, None),
            P(EVERY, None, None),
        ),
        check_vma=False,
    )
```

```python
import functools
import math

import jax
import jax.numpy as jnp
from jax import lax
from jax.experimental import pallas as pl
from jax.experimental.layout import Layout, with_layout_constraint
from jax.experimental.pallas import tpu as pltpu
from jax.sharding import PartitionSpec as P

Q_HEADS = 32
KV_HEADS = 4
HEAD_DIM = 128
EPSILON = 1e-06
NEG_FILL = -1e30
LOG2E = 1.4426950408889634
SCORE_SCALE = LOG2E / math.sqrt(HEAD_DIM)
PLANE = ("blk", "head")
EVERY = ("dp", "blk", "head")
F32 = jnp.float32
BF16 = jnp.bfloat16


def dot_nn(a, b):
    return jnp.dot(a, b, preferred_element_type=F32)


def dot_nt(a, b):
    return lax.dot_general(a, b, (((1,), (1,)), ((), ())), preferred_element_type=F32)


def dot_tn(a, b):
    return lax.dot_general(a, b, (((0,), (0,)), ((), ())), preferred_element_type=F32)


def rms_parts(values):
    scale = lax.rsqrt(jnp.mean(values * values, axis=-1, keepdims=True) + EPSILON)
    return values * scale, scale


def rms_back(grad, unit, scale, gain_vec):
    scaled = grad * gain_vec
    return scale * (scaled - unit * jnp.mean(scaled * unit, axis=-1, keepdims=True))


def lane_sum(values):
    ones = jnp.ones((HEAD_DIM, HEAD_DIM), BF16)
    coarse = values.astype(BF16)
    fine = (values - coarse.astype(F32)).astype(BF16)
    return dot_nn(coarse, ones) + dot_nn(fine, ones)


def head_parts(values):
    scale = lax.rsqrt(lane_sum(values * values) * (1.0 / HEAD_DIM) + EPSILON)
    return values * scale, scale


def head_back(grad, unit, scale, gain_vec):
    scaled = grad * gain_vec
    return scale * (scaled - unit * (lane_sum(scaled * unit) * (1.0 / HEAD_DIM)))


def turn_head(unit, cosines, sines):
    return unit * cosines + pltpu.roll(unit, HEAD_DIM // 2, 1) * sines


def turn_back(grad, cosines, sines):
    return grad * cosines + pltpu.roll(grad * sines, HEAD_DIM // 2, 1)


def pair_of(refs, start):
    return jnp.concatenate([ref[0, :, start : start + HEAD_DIM] for ref in refs], axis=0)


def put_pair(ref, order_ref, pair, start, values):
    size = values.shape[0] // 2
    for i in range(2):
        ref[order_ref[2 * pair + i], :, start : start + HEAD_DIM] = values[
            i * size : (i + 1) * size
        ].astype(ref.dtype)


def add_keys(start, pair, qkv_refs, cosines, sines, k_gain_ref, k_scr, v_scr):
    raw = pair_of(qkv_refs, start)
    unit, _ = head_parts(raw)
    k_scr[pair] = turn_head(unit * k_gain_ref[...], cosines, sines).astype(BF16)
    v_scr[pair, :, :HEAD_DIM] = pair_of(qkv_refs, start + HEAD_DIM).astype(BF16)
    return raw


def hidden_keys(row_seg, key_seg, row_pair, key_pair):
    shape = (row_seg.shape[0], key_seg.shape[1])
    rows = lax.broadcasted_iota(jnp.int32, shape, 0) + (row_pair - key_pair) * shape[0]
    cols = lax.broadcasted_iota(jnp.int32, shape, 1)
    return jnp.where((row_seg == key_seg) & (cols <= rows), 0.0, NEG_FILL)


def attend_kernel(
    heads,
    order_ref,
    low_ref,
    qkv_even_ref,
    qkv_odd_ref,
    cos_ref,
    sin_ref,
    q_gain_ref,
    k_gain_ref,
    seg_row_ref,
    seg_col_ref,
    attn_ref,
    stat_ref,
    k_scr,
    v_scr,
    q_scr,
    acc_scr,
):
    pair = pl.program_id(0)

    qkv_refs = (qkv_even_ref, qkv_odd_ref)

    @pl.when(pair == 0)
    def _():
        v_scr[:, :, HEAD_DIM:] = jnp.ones_like(v_scr[:, :, HEAD_DIM:])

    cosines, sines = cos_ref[0], sin_ref[0]
    add_keys(heads * HEAD_DIM, pair, qkv_refs, cosines, sines, k_gain_ref, k_scr, v_scr)
    for h in range(heads):
        unit, _ = head_parts(pair_of(qkv_refs, h * HEAD_DIM))
        turned = turn_head(unit * q_gain_ref[...], cosines, sines)
        q_scr[h] = (turned * SCORE_SCALE).astype(BF16)
    acc_scr[...] = jnp.zeros_like(acc_scr)
    row_seg = seg_col_ref[0]

    def step(key_pair, carry):
        hide = hidden_keys(row_seg, seg_row_ref[key_pair], pair, key_pair)
        keys, values = k_scr[key_pair], v_scr[key_pair]
        for h in range(heads):
            weights = jnp.exp2(dot_nt(q_scr[h], keys) + hide).astype(BF16)
            acc_scr[h] += dot_nn(weights, values)
        return carry

    lax.fori_loop(low_ref[pair], pair + 1, step, 0)
    for h in range(heads):
        total = acc_scr[h, :, HEAD_DIM:]
        put_pair(attn_ref, order_ref, pair, h * HEAD_DIM, acc_scr[h, :, :HEAD_DIM] / total)
        stat_ref[0, h] = jnp.log2(total)


def attend_back_kernel(
    heads,
    order_ref,
    low_ref,
    qkv_even_ref,
    qkv_odd_ref,
    cos_ref,
    sin_ref,
    q_gain_ref,
    k_gain_ref,
    seg_row_ref,
    seg_col_ref,
    attn_even_ref,
    attn_odd_ref,
    grad_even_ref,
    grad_odd_ref,
    stat_ref,
    out_ref,
    gain_ref,
    k_scr,
    v_scr,
    dk_scr,
    dv_scr,
    q_scr,
    dq_scr,
    delta_scr,
    grad_scr,
    raw_scr,
    turn_scr,
):
    pair = pl.program_id(0)
    pairs = pl.num_programs(0)
    start = heads * HEAD_DIM

    @pl.when(pair == 0)
    def _():
        dk_scr[...] = jnp.zeros_like(dk_scr)
        dv_scr[...] = jnp.zeros_like(dv_scr)
        gain_ref[...] = jnp.zeros_like(gain_ref)

    qkv_refs = (qkv_even_ref, qkv_odd_ref)
    cosines, sines = cos_ref[0], sin_ref[0]
    raw_scr[pair] = add_keys(start, pair, qkv_refs, cosines, sines, k_gain_ref, k_scr, v_scr)
    turn_scr[0, pair] = cosines
    turn_scr[1, pair] = sines
    for h in range(heads):
        unit, _ = head_parts(pair_of(qkv_refs, h * HEAD_DIM))
        turned = turn_head(unit * q_gain_ref[...], cosines, sines)
        q_scr[h] = (turned * SCORE_SCALE).astype(BF16)
        grad = pair_of((grad_even_ref, grad_odd_ref), h * HEAD_DIM)
        attn = pair_of((attn_even_ref, attn_odd_ref), h * HEAD_DIM)
        grad_scr[h] = grad
        delta_scr[h] = lane_sum(grad.astype(F32) * attn.astype(F32))
    dq_scr[...] = jnp.zeros_like(dq_scr)
    row_seg = seg_col_ref[0]

    def step(key_pair, carry):
        hide = hidden_keys(row_seg, seg_row_ref[key_pair], pair, key_pair)
        keys, values = k_scr[key_pair], v_scr[key_pair]
        dk, dv = dk_scr[key_pair], dv_scr[key_pair]
        for h in range(heads):
            grad_rows = grad_scr[h]
            stat = jnp.concatenate([stat_ref[0, h]] * 2, axis=1)
            delta = jnp.concatenate([delta_scr[h]] * 2, axis=1)
            probs = jnp.exp2(dot_nt(q_scr[h], keys) + (hide - stat))
            grad_scores = (probs * (dot_nt(grad_rows, values) - delta)).astype(BF16)
            dk = dk + dot_tn(grad_scores, q_scr[h])
            dv = dv + dot_tn(probs.astype(BF16), grad_rows)
            dq_scr[h] += dot_nn(grad_scores, keys)
        dk_scr[key_pair] = dk
        dv_scr[key_pair] = dv
        return carry

    lax.fori_loop(low_ref[pair], pair + 1, step, 0)
    gain_sum = jnp.zeros((1, HEAD_DIM), F32)
    for h in range(heads):
        unit, scale = head_parts(pair_of(qkv_refs, h * HEAD_DIM))
        grad = turn_back(dq_scr[h] * (SCORE_SCALE / LOG2E), cosines, sines)
        gain_sum = gain_sum + jnp.sum(grad * unit, axis=0, keepdims=True)
        put_pair(
            out_ref, order_ref, pair, h * HEAD_DIM, head_back(grad, unit, scale, q_gain_ref[...])
        )
    gain_ref[0:1, :] += gain_sum

    @pl.when(pair == pairs - 1)
    def _():
        def one(key_pair, carry):
            unit, scale = head_parts(raw_scr[key_pair])
            grad = turn_back(
                dk_scr[key_pair] * (1.0 / LOG2E), turn_scr[0, key_pair], turn_scr[1, key_pair]
            )
            put_pair(
                out_ref, order_ref, key_pair, start, head_back(grad, unit, scale, k_gain_ref[...])
            )
            put_pair(out_ref, order_ref, key_pair, start + HEAD_DIM, dv_scr[key_pair])
            return carry + jnp.sum(grad * unit, axis=0, keepdims=True)

        gain_ref[1:2, :] += lax.fori_loop(0, pairs, one, jnp.zeros((1, HEAD_DIM), F32))


def whole_block(shape):
    zeros = (0,) * len(shape)
    return pl.BlockSpec(shape, lambda pair, order, low: zeros)


def stat_block(heads, rows):
    return pl.BlockSpec((1, heads, rows, HEAD_DIM), lambda pair, order, low: (pair, 0, 0, 0))


def pair_block(shape):
    return pl.BlockSpec((1, *shape), lambda pair, order, low: (pair, 0, 0))


def ordered_blocks(shape):
    return [
        pl.BlockSpec((1, *shape), lambda pair, order, low, i=i: (order[2 * pair + i], 0, 0))
        for i in range(2)
    ]


def attention_inputs(qkv, tables, gains, segment):
    blocks, size, width = qkv.shape
    tables = [table.reshape(blocks // 2, 2 * size, HEAD_DIM) for table in tables]
    rows = segment.reshape(blocks // 2, 1, 2 * size)
    cols = segment.reshape(blocks // 2, 2 * size, 1)
    specs = (
        ordered_blocks((size, width))
        + [pair_block((2 * size, HEAD_DIM))] * 2
        + [whole_block(gain.shape) for gain in gains]
        + [whole_block(rows.shape), pair_block((2 * size, 1))]
    )
    return (qkv, qkv, *tables, *gains, rows, cols), specs


def attend(qkv, tables, gains, segment, order, low, heads):
    blocks, size, _ = qkv.shape
    pairs, rows = blocks // 2, 2 * size
    arrays, specs = attention_inputs(qkv, tables, gains, segment)
    return pl.pallas_call(
        functools.partial(attend_kernel, heads),
        grid_spec=pltpu.PrefetchScalarGridSpec(
            num_scalar_prefetch=2,
            grid=(pairs,),
            in_specs=specs,
            out_specs=[
                whole_block((blocks, size, heads * HEAD_DIM)),
                stat_block(heads, rows),
            ],
            scratch_shapes=[
                pltpu.VMEM((pairs, rows, HEAD_DIM), BF16),
                pltpu.VMEM((pairs, rows, 2 * HEAD_DIM), BF16),
                pltpu.VMEM((heads, rows, HEAD_DIM), BF16),
                pltpu.VMEM((heads, rows, 2 * HEAD_DIM), F32),
            ],
        ),
        out_shape=[
            jax.ShapeDtypeStruct((blocks, size, heads * HEAD_DIM), BF16),
            jax.ShapeDtypeStruct((pairs, heads, rows, HEAD_DIM), F32),
        ],
        compiler_params=pltpu.CompilerParams(vmem_limit_bytes=48 * 2**20),
        cost_estimate=pl.CostEstimate(
            flops=2**24 * blocks * heads, bytes_accessed=qkv.size * 8, transcendentals=0
        ),
    )(order, low, *arrays)


def attend_back(qkv, tables, gains, segment, order, low, heads, attn, grad, stat):
    blocks, size, width = qkv.shape
    pairs, rows = blocks // 2, 2 * size
    arrays, specs = attention_inputs(qkv, tables, gains, segment)
    return pl.pallas_call(
        functools.partial(attend_back_kernel, heads),
        grid_spec=pltpu.PrefetchScalarGridSpec(
            num_scalar_prefetch=2,
            grid=(pairs,),
            in_specs=specs
            + ordered_blocks((size, heads * HEAD_DIM)) * 2
            + [stat_block(heads, rows)],
            out_specs=[whole_block((blocks, size, width)), whole_block((8, HEAD_DIM))],
            scratch_shapes=[pltpu.VMEM((pairs, rows, HEAD_DIM), BF16)] * 2
            + [pltpu.VMEM((pairs, rows, HEAD_DIM), F32)] * 2
            + [
                pltpu.VMEM((heads, rows, HEAD_DIM), BF16),
                pltpu.VMEM((heads, rows, HEAD_DIM), F32),
                pltpu.VMEM((heads, rows, HEAD_DIM), F32),
                pltpu.VMEM((heads, rows, HEAD_DIM), BF16),
                pltpu.VMEM((pairs, rows, HEAD_DIM), F32),
                pltpu.VMEM((2, pairs, rows, HEAD_DIM), F32),
            ],
        ),
        out_shape=[
            jax.ShapeDtypeStruct((blocks, size, width), BF16),
            jax.ShapeDtypeStruct((8, HEAD_DIM), F32),
        ],
        compiler_params=pltpu.CompilerParams(vmem_limit_bytes=56 * 2**20),
        cost_estimate=pl.CostEstimate(
            flops=2**24 * blocks * heads * 2, bytes_accessed=qkv.size * 12, transcendentals=0
        ),
    )(order, low, *arrays, attn, attn, grad, grad, stat)


def project_kernel(counts, normed, *refs):
    pieces, (gain_ref, weight_ref, out_ref, rows_ref) = refs[: len(counts)], refs[len(counts) :]
    block = pl.program_id(0)
    rows = pieces[-1][0]
    place = sum(counts) - counts[-1]
    for ref, count in zip(pieces[-2::-1], counts[-2::-1]):
        rows = jnp.where(block < place, ref[0], rows)
        place = place - count
    if normed:
        unit, _ = rms_parts(rows.astype(F32))
        rows = (unit * gain_ref[...]).astype(BF16)
    rows_ref[0] = rows
    out_ref[0] = dot_nn(rows, weight_ref[...]).astype(out_ref.dtype)


def project(pieces, gain, weight, normed, out_type):
    counts = [piece.shape[0] for piece in pieces]
    _, size, width = pieces[0].shape
    blocks, columns = sum(counts), weight.shape[1]

    def piece_spec(first, count):
        return pl.BlockSpec(
            (1, size, width), lambda i: (jnp.clip(i - first, 0, count - 1), 0, 0)
        )

    firsts = [sum(counts[:i]) for i in range(len(counts))]
    return pl.pallas_call(
        functools.partial(project_kernel, counts, normed),
        grid=(blocks,),
        in_specs=[piece_spec(first, count) for first, count in zip(firsts, counts)]
        + [
            pl.BlockSpec(gain.shape, lambda i: (0, 0)),
            pl.BlockSpec(weight.shape, lambda i: (0, 0), pipeline_mode=pl.Buffered(1)),
        ],
        out_specs=[
            pl.BlockSpec((1, size, columns), lambda i: (i, 0, 0)),
            pl.BlockSpec((1, size, width), lambda i: (i, 0, 0)),
        ],
        out_shape=[
            jax.ShapeDtypeStruct((blocks, size, columns), out_type),
            jax.ShapeDtypeStruct((blocks, size, width), BF16),
        ],
        compiler_params=pltpu.CompilerParams(vmem_limit_bytes=32 * 2**20),
        cost_estimate=pl.CostEstimate(
            flops=blocks * size * width * columns, bytes_accessed=weight.size, transcendentals=0
        ),
    )(*pieces, gain, weight)


def expert_kernel(
    experts,
    expert_ref,
    rows_ref,
    gates_ref,
    cot_ref,
    gate_w_ref,
    up_w_ref,
    down_w_ref,
    gated_ref,
    grad_gate_ref,
    grad_up_ref,
    back_ref,
    out_ref,
):
    width = rows_ref.shape[1]
    rows = rows_ref[...]
    spots = lax.broadcasted_iota(jnp.int32, gates_ref.shape, 1)
    coarse_spot = spots == expert_ref[0]
    fine_spot = spots == expert_ref[0] + experts
    gate = jnp.sum(
        jnp.where(coarse_spot | fine_spot, gates_ref[...].astype(F32), 0.0), axis=1, keepdims=True
    )
    gate_pre = dot_nn(rows, gate_w_ref[...])
    up_pre = dot_nn(rows, up_w_ref[...])
    pulled = dot_nt(cot_ref[...], down_w_ref[...])
    sigma = 1.0 / (1.0 + jnp.exp(-gate_pre))
    swish = gate_pre * sigma
    hidden = (swish * up_pre).astype(BF16).astype(F32)
    gate_grad = jnp.sum(hidden * pulled, axis=1, keepdims=True)
    gated = (hidden * gate).astype(BF16)
    grad_hidden = pulled * gate
    grad_gate = (grad_hidden * up_pre * (sigma + swish * (1.0 - sigma))).astype(BF16)
    grad_up = (grad_hidden * swish).astype(BF16)
    gated_ref[...] = gated
    grad_gate_ref[...] = grad_gate
    grad_up_ref[...] = grad_up
    back_ref[:, :width] = (
        dot_nt(grad_gate, gate_w_ref[...]) + dot_nt(grad_up, up_w_ref[...])
    ).astype(BF16)
    coarse = gate_grad.astype(BF16).astype(F32)
    back_ref[:, width:] = jnp.where(
        coarse_spot, coarse, jnp.where(fine_spot, gate_grad - coarse, 0.0)
    ).astype(BF16)
    out_ref[...] = dot_nn(gated, down_w_ref[...]).astype(BF16)


def expert_pass(came, cot, gate_w, up_w, down_w, expert_id, experts):
    count, full = came.shape
    width, hidden = gate_w.shape
    block = max(b for b in range(16, 385, 16) if count % b == 0)
    extra = full - width

    def rows_of(columns, place=0):
        return pl.BlockSpec((block, columns), lambda i, e: (i, place))

    def kept(shape):
        return pl.BlockSpec(shape, lambda i, e: (0, 0), pipeline_mode=pl.Buffered(1))

    return pl.pallas_call(
        functools.partial(expert_kernel, experts),
        grid_spec=pltpu.PrefetchScalarGridSpec(
            num_scalar_prefetch=1,
            grid=(count // block,),
            in_specs=[
                rows_of(width),
                rows_of(extra, width // extra),
                rows_of(width),
                kept(gate_w.shape),
                kept(up_w.shape),
                kept(down_w.shape),
            ],
            out_specs=[rows_of(hidden)] * 3 + [rows_of(full), rows_of(width)],
        ),
        out_shape=[jax.ShapeDtypeStruct((count, hidden), BF16)] * 3
        + [
            jax.ShapeDtypeStruct((count, full), BF16),
            jax.ShapeDtypeStruct((count, width), BF16),
        ],
        compiler_params=pltpu.CompilerParams(vmem_limit_bytes=58 * 2**20),
        cost_estimate=pl.CostEstimate(
            flops=count * width * hidden * 3, bytes_accessed=count * width * 4, transcendentals=0
        ),
    )(expert_id.reshape(1), came, came, cot, gate_w, up_w, down_w)


def by_rows(array):
    return with_layout_constraint(array, Layout(major_to_minor=tuple(range(array.ndim))))


def ring_steps(ways):
    ring = list(range(1, ways, 2)) + list(range(0, ways, 2))[::-1]
    return [(ring[i], ring[(i + 1) % ways]) for i in range(ways)]


def line_gather(rows, ways):
    held, out = rows, [rows]
    for _ in range(ways - 1):
        held = lax.ppermute(held, "dp", ring_steps(ways))
        out.append(held)
    return jnp.concatenate(out, axis=0)


def ring_jumps(ways, count):
    ring = [a for a, _ in ring_steps(ways)]
    return [(ring[i], ring[(i + count) % ways]) for i in range(ways)]


def line_spread(rows, ways):
    blocks = [lax.ppermute(rows, "dp", ring_jumps(ways, k)) for k in range(1, ways)]
    return jnp.concatenate([rows] + blocks, axis=0)


def line_sum(parts, ways):
    size = parts.shape[0] // ways
    total = parts[:size].astype(F32)
    for k in range(1, ways):
        part = parts[k * size : (k + 1) * size]
        total = total + lax.ppermute(part, "dp", ring_jumps(ways, -k)).astype(F32)
    return total


def line_reduce(part, ways):
    back = [(b, a) for a, b in ring_steps(ways)]
    acc = part(ways - 1)
    for k in range(ways - 2, -1, -1):
        acc = lax.ppermute(acc, "dp", back)
        acc = yield (acc.astype(F32) + part(k).astype(F32)).astype(BF16)


def plane_gather_steps(rows, turn, pair):
    if not pair:
        yield [lax.all_gather(rows, PLANE, axis=0, tiled=False)]
        return
    first, second = plane_flips(turn)
    two = yield jnp.stack([rows, lax.ppermute(rows, PLANE, first)])
    four = yield jnp.concatenate([two, lax.ppermute(two, PLANE, second)])
    yield [four, lax.ppermute(four, PLANE, flips(2))]


def together(*moves):
    held, going = [next(move) for move in moves], True
    while going:
        if len(held) > 1:
            held = jax.tree.map(by_rows, list(tie(*held)))
        going = False
        for i, move in enumerate(moves):
            try:
                held[i] = move.send(held[i])
                going = True
            except StopIteration:
                continue
    return held


def paired(blk_ways, head_ways):
    return blk_ways == 4 and head_ways == 2


def flips(bit):
    return [(i, i ^ bit) for i in range(8)]


def plane_flips(turn):
    return (flips(4), flips(1)) if turn % 2 == 0 else (flips(1), flips(4))


def plane_order(plane_index, plane_ways, turn, pair):
    blocks = jnp.arange(plane_ways, dtype=jnp.int32)
    if not pair:
        return blocks
    away = blocks ^ plane_index
    x, core, y = (away >> 2) & 1, (away >> 1) & 1, away & 1
    near, far = (x, y) if turn % 2 == 0 else (y, x)
    return (core * 4 + far * 2 + near).astype(jnp.int32)


def plane_reduce(product, turn, pair):
    if not pair:
        yield lax.psum_scatter(product(0, None), PLANE, scatter_dimension=0, tiled=False)
        return
    first, second = plane_flips(turn)
    away = lax.ppermute(product(4, 8), PLANE, flips(2))
    parts = yield (product(0, 4).astype(F32) + away.astype(F32)).astype(BF16)
    for half, move in ((2, second), (1, first)):
        came = lax.ppermute(parts[half:], PLANE, move)
        parts = (parts[:half].astype(F32) + came.astype(F32)).astype(BF16)
        if half > 1:
            parts = yield parts
    yield parts[0]


def tie(*arrays):
    return lax.optimization_barrier(arrays)


def every_exchange(rows):
    return lax.all_to_all(rows, EVERY, split_axis=0, concat_axis=0, tiled=True)


def plane_exchange(rows):
    return lax.all_to_all(rows, PLANE, split_axis=0, concat_axis=0, tiled=True)


def body(
    tokens,
    segments,
    routes,
    cotangent,
    attn_gain,
    qkv_weight,
    q_gain,
    k_gain,
    out_weight,
    ffn_gain,
    router_weight,
    gate_weight,
    up_weight,
    down_weight,
):
    seqs, size, width = tokens.shape
    dp_ways = lax.axis_size("dp")
    blk_ways = lax.axis_size("blk")
    head_ways = lax.axis_size("head")
    plane_ways = blk_ways * head_ways
    pair = paired(blk_ways, head_ways)
    dp_index = lax.axis_index("dp")
    plane_index = lax.axis_index("blk") * head_ways + lax.axis_index("head")
    seq_total = segments.shape[1]
    experts = router_weight.shape[1]
    top_count = routes.shape[2]
    capacity = (9 * size * top_count + 8 * experts - 1) // (8 * experts)
    query_dim = Q_HEADS * HEAD_DIM
    kv_dim = KV_HEADS * HEAD_DIM
    heads = Q_HEADS // plane_ways
    share = plane_ways // KV_HEADS
    kv_index = plane_index // share
    local_dim = heads * HEAD_DIM
    extra = -(-2 * experts // 128) * 128

    weight_rows = qkv_weight.shape[0]

    def columns(weight, start, count):
        return lax.dynamic_slice(weight, (0, start), (weight_rows, count))

    qkv_local = lax.all_gather(
        jnp.concatenate(
            [
                columns(qkv_weight, plane_index * local_dim, local_dim),
                columns(qkv_weight, query_dim + kv_index * HEAD_DIM, HEAD_DIM),
                columns(qkv_weight, query_dim + kv_dim + kv_index * HEAD_DIM, HEAD_DIM),
            ],
            axis=1,
        ),
        "dp",
        axis=0,
        tiled=True,
    )

    half = HEAD_DIM // 2
    frequency = 1000000.0 ** (-2.0 * jnp.arange(half, dtype=F32) / HEAD_DIM)
    angles = jnp.arange(seq_total, dtype=jnp.int32).astype(F32)[:, None] * frequency[None, :]
    cosines, sines = jnp.cos(angles), jnp.sin(angles)
    tables = (
        jnp.concatenate([cosines, cosines], axis=1).reshape(plane_ways, size, HEAD_DIM),
        jnp.concatenate([-sines, sines], axis=1).reshape(plane_ways, size, HEAD_DIM),
    )
    gains = (q_gain[None], k_gain[None])
    attn_gain_row, ffn_gain_row = attn_gain[None], ffn_gain[None]

    expert_ids = dp_index * plane_ways + jnp.arange(plane_ways, dtype=jnp.int32)
    before = (
        jnp.arange(size, dtype=jnp.int32)[:, None] > jnp.arange(size, dtype=jnp.int32)[None, :]
    ).astype(BF16)
    slot_ids = jnp.arange(dp_ways * capacity, dtype=jnp.int32)

    spots = jnp.array([[a for a, _ in ring_steps(dp_ways)].index(i) for i in range(dp_ways)], jnp.int32)
    ring_slots = (spots[dp_index] - spots) % dp_ways
    ring = jnp.array([a for a, _ in ring_steps(dp_ways)], jnp.int32)
    dp_index_of_slot = ring[(spots[dp_index] - jnp.arange(dp_ways)) % dp_ways]
    def route_steps():
        yield lows[0]
        yield line_routes

    line_routes = line_spread(routes.reshape(1, seqs * size, top_count), dp_ways)

    def picks_of(s):
        seen = line_routes.reshape(dp_ways, seqs, size, top_count)[:, s]
        seen = seen.reshape(dp_ways * size, top_count)
        chosen = jnp.any(seen[:, :, None] == expert_ids[None, None, :], axis=1)
        chosen = chosen.reshape(dp_ways, size, plane_ways)
        ranks = jnp.einsum(
            "ij,zje->zie", before, chosen.astype(BF16), preferred_element_type=F32
        ).astype(jnp.int32)
        ranks = ranks + jnp.arange(dp_ways, dtype=jnp.int32)[:, None, None] * capacity
        keys = jnp.where(chosen, ranks, -1)

        def table(keys):
            keys = keys.reshape(dp_ways * size, plane_ways).T
            picks = (keys[:, None, :] == slot_ids[None, :, None]).astype(BF16)
            return picks.reshape(plane_ways * dp_ways * capacity, dp_ways * size)

        return table(keys), table(jnp.take(keys, ring_slots, axis=0))


    last = []

    def exchange(rows, move=plane_exchange):
        if last:
            rows, _ = tie(rows, last.pop())
        out = move(rows)
        last.append(out)
        return out

    def pack(line_rows, table):
        return dot_nn(table, line_rows).astype(BF16)

    def unpack(rows, s):
        return dot_tn(picks[s], rows).astype(BF16)

    orders, lows = [], []
    for s in range(seqs):
        blocks = segments[s].reshape(plane_ways // 2, 2 * size)
        lows.append(
            jnp.sum(
                (blocks[None, :, -1] < blocks[:, None, 0]).astype(jnp.int32), axis=1
            ).astype(jnp.int32)
        )
        orders.append(plane_order(plane_index, plane_ways, s, pair))

    inputs, units, scales = [], [], []
    moves = []
    for s in range(seqs):
        rows = tokens[s].astype(F32)
        unit, scale = rms_parts(rows)
        inputs.append(rows)
        units.append(unit)
        scales.append(scale)
        moves.append(plane_gather_steps(tokens[s], s, pair))
    *pieces, line_routes = together(*moves, route_steps())
    picks, straight_picks = zip(*[picks_of(s) for s in range(seqs)])
    pieces, qkv_local = tie(pieces, qkv_local)
    out_columns, qkv_local = tie(
        columns(out_weight, plane_index * local_dim, local_dim), qkv_local
    )
    out_local = lax.all_gather(out_columns, "dp", axis=0, tiled=True)
    pieces = jax.tree.map(by_rows, pieces)

    def times(left, right):
        def product(start, stop):
            rows = left[start:stop]
            count = rows.shape[0]
            out = dot_nt(rows.reshape(count * size, -1), right).astype(BF16)
            return out.reshape(count, size, width)

        return product

    lines, held = [], out_local
    for s in range(seqs):
        rows, held = tie(cotangent[s], held)
        held = line_spread(rows, dp_ways)
        lines.append(held)
    projected, attended, stats, mixes, spread = [], [], [], [], []
    for s in range(seqs):
        qkv, rows = project(pieces[s], attn_gain_row, qkv_local, True, F32)
        spread.append(rows)
        attn, stat = attend(qkv, tables, gains, segments[s], orders[s], lows[s], heads)
        projected.append(qkv)
        attended.append(attn)
        stats.append(stat)
        mixes.append(plane_reduce(times(attn, out_local), s, pair))

    def pack_steps():
        mark = yield lows[0]
        mark = yield mark
        rows, _ = tie(lines[0], mark)
        yield pack(rows, picks[0])

    *mixes, packed = together(*mixes, pack_steps())
    packed, *mixes = tie(packed, *mixes)
    cot_rows = [exchange(packed)]

    middles, normed2s, mid_units, mid_scales, gate_tables, came = [], [], [], [], [], []
    for s in range(seqs):
        middle = inputs[s] + mixes[s].astype(F32)
        unit, scale = rms_parts(middle)
        normed2 = (unit * ffn_gain_row).astype(BF16)
        logits = dot_nn(normed2, router_weight)
        chosen = jnp.any(
            routes[s][:, :, None] == jnp.arange(experts, dtype=jnp.int32)[None, None, :], axis=1
        )
        top = jnp.max(jnp.where(chosen, logits, -jnp.inf), axis=1, keepdims=True)
        powers = jnp.where(chosen, jnp.exp(jnp.where(chosen, logits - top, 0.0)), 0.0)
        gates = powers / jnp.sum(powers, axis=1, keepdims=True)
        coarse = gates.astype(BF16)
        fine = (gates - coarse.astype(F32)).astype(BF16)
        payload = [normed2, coarse, fine]
        if extra > 2 * experts:
            payload.append(jnp.zeros((size, extra - 2 * experts), BF16))
        middles.append(middle)
        normed2s.append(normed2)
        mid_units.append(unit)
        mid_scales.append(scale)
        gate_tables.append(gates)
        line = line_gather(jnp.concatenate(payload, axis=1), dp_ways)
        if s:
            cot_rows.append(exchange(pack(lines[s], picks[s])))
        came.append(exchange(pack(line, picks[s])))

    gate_w, up_w, down_w = gate_weight[0], up_weight[0], down_weight[0]
    expert_id = (dp_index * plane_ways + plane_index).astype(jnp.int32)
    kept, grad_lines, produced = [], [], []
    for s in range(seqs):
        gated, grad_gate, grad_up, back, out = expert_pass(
            came[s], cot_rows[s], gate_w, up_w, down_w, expert_id, experts
        )
        if s:
            back, grad_lines[-1] = tie(back, grad_lines[-1])
        grad_lines.append(exchange(back))
        produced.append(out)
        kept.append((came[s][:, :width], gated, cot_rows[s], grad_gate, grad_up))
    out_lines, grad_mids, reduced = [], [], []
    router_grad = jnp.zeros((width, experts), F32)
    ffn_sum = jnp.zeros((width,), F32)
    for s in range(seqs):
        back = unpack(grad_lines[s], s)
        if s == 0:
            back, kept = tie(back, kept)
        reduced.append(line_sum(back, dp_ways))
    out_lines.append(exchange(produced[0]))
    for s in range(seqs):
        tail = reduced[s][:, width:]
        gates = gate_tables[s]
        grad_gates = tail[:, :experts] + tail[:, experts : 2 * experts]
        grad_logits = (
            gates * (grad_gates - jnp.sum(gates * grad_gates, axis=1, keepdims=True))
        ).astype(BF16)
        router_grad = router_grad + dot_tn(normed2s[s], grad_logits)
        grad_normed2 = reduced[s][:, :width] + dot_nt(grad_logits, router_weight)
        ffn_sum = ffn_sum + jnp.sum(grad_normed2 * mid_units[s], axis=0)
        grad_mids.append(
            cotangent[s].astype(F32)
            + rms_back(grad_normed2, mid_units[s], mid_scales[s], ffn_gain_row)
        )

    gate_grad = sum(dot_tn(rows, grad) for rows, _, _, grad, _ in kept)
    up_grad = sum(dot_tn(rows, grad) for rows, _, _, _, grad in kept)
    down_grad = sum(dot_tn(gated, cot) for _, gated, cot, _, _ in kept)
    *grad_mids, out_lines[0], gate_grad, up_grad, down_grad = tie(
        *grad_mids, out_lines[0], gate_grad, up_grad, down_grad
    )
    devices = dp_ways * plane_ways

    def small_steps():
        rows = yield jnp.concatenate(
            [router_grad.reshape(devices, -1), ffn_sum.reshape(devices, -1)], axis=1
        )
        yield exchange(rows, every_exchange)

    outcome_lines = []

    def outcome_steps():
        rows = yield out_lines[0]
        outcome_lines.append(dot_tn(straight_picks[0], rows).astype(BF16))
        yield outcome_lines[0]

    *pieces, small, _ = together(
        *[plane_gather_steps(grad_mids[s].astype(BF16), s, pair) for s in range(seqs)],
        small_steps(),
        outcome_steps(),
    )
    pieces, small = tie(pieces, small)
    pieces = jax.tree.map(by_rows, pieces)

    def outcome(s):
        if s == len(outcome_lines):
            outcome_lines.append(dot_tn(straight_picks[s], out_lines[s]).astype(BF16))
        back = outcome_lines[s]
        back = lax.psum_scatter(back, "dp", scatter_dimension=0, tiled=True)
        return (middles[s] + back.astype(F32)).astype(BF16)

    for s in range(1, seqs):
        rows, pieces = tie(produced[s], pieces)
        pieces = jax.tree.map(by_rows, pieces)
        out_lines.append(exchange(rows))
    grad_spread = []
    grad_qkvs, grad_ins = [], []
    head_sums = jnp.zeros((2, HEAD_DIM), F32)
    for s in range(seqs):
        grad_attn, rows = project(pieces[s], ffn_gain_row, out_local, False, BF16)
        grad_spread.append(rows)
        grad_qkv, sums = attend_back(
            projected[s],
            tables,
            gains,
            segments[s],
            orders[s],
            lows[s],
            heads,
            attended[s],
            grad_attn,
            stats[s],
        )
        head_sums = head_sums + sums[:2]
        grad_qkvs.append(grad_qkv)
    *grad_qkvs, out_lines[-1] = tie(*grad_qkvs, out_lines[-1])
    head_small = exchange(
        jnp.concatenate(
            [head_sums[0].reshape(devices, -1), head_sums[1].reshape(devices, -1)], axis=1
        ),
        every_exchange,
    )

    def total_over(lefts, rights):
        return sum(
            dot_tn(a.reshape(seq_total, -1), b.reshape(seq_total, -1))
            for a, b in zip(lefts, rights)
        ).astype(BF16)

    total = total_over(spread, grad_qkvs)
    def rows_of_plane(total):
        return plane_exchange(total).reshape(plane_ways, weight_rows // plane_ways, -1)

    out_total = lax.psum_scatter(
        total_over(grad_spread, attended), "dp", scatter_dimension=0, tiled=True
    )
    out_rows = rows_of_plane(out_total)
    sums = [plane_reduce(times(grad_qkvs[s], qkv_local), s, pair) for s in range(seqs)]
    ring_sum = line_reduce(
        lambda k: lax.dynamic_slice_in_dim(
            total, dp_index_of_slot[k] * weight_rows, weight_rows
        ),
        dp_ways,
    )
    held, qkv_rows = [next(move) for move in sums], next(ring_sum)
    qkv_rows, head_small = tie(qkv_rows, head_small)
    for turn in range(dp_ways - 1):
        qkv_rows = ring_sum.send(qkv_rows) if turn else qkv_rows
        if pair and turn:
            qkv_rows, *held = tie(qkv_rows, *held)
            held = [move.send(by_rows(h)) for move, h in zip(sums, held)]
        if turn == 1:
            qkv_rows, out_rows = tie(qkv_rows, out_rows)
    grad_normeds = held

    for s in range(seqs):
        grad_in = rms_back(grad_normeds[s].astype(F32), units[s], scales[s], attn_gain_row)
        grad_ins.append((grad_mids[s] + grad_in).astype(BF16))
    input_grad = jnp.stack(grad_ins)
    layer_out = jnp.stack([outcome(s) for s in range(seqs)])

    def side_by_side(pieces):
        return pieces.transpose(1, 0, 2).reshape(pieces.shape[1], -1)

    out_grad = side_by_side(out_rows).astype(F32)
    pieces = rows_of_plane(qkv_rows).astype(F32)
    row_count = pieces.shape[1]

    def kv_columns(start):
        part = pieces[:, :, start : start + HEAD_DIM]
        return side_by_side(part.reshape(KV_HEADS, share, row_count, HEAD_DIM).sum(axis=1))

    qkv_grad = jnp.concatenate(
        [
            side_by_side(pieces[:, :, :local_dim]),
            kv_columns(local_dim),
            kv_columns(local_dim + HEAD_DIM),
        ],
        axis=1,
    )
    own_rows = lax.dynamic_slice(
        qkv_weight, (plane_index * row_count, 0), (row_count, qkv_weight.shape[1])
    )
    own_gain = lax.dynamic_slice(
        attn_gain, ((dp_index * plane_ways + plane_index) * row_count,), (row_count,)
    )
    attn_gain_grad = jnp.sum(own_rows.astype(F32) * qkv_grad, axis=1) / own_gain

    small = jnp.sum(small, axis=0)
    head_small = jnp.sum(head_small, axis=0).reshape(2, -1)
    cut = row_count * experts
    return (
        layer_out,
        input_grad,
        attn_gain_grad,
        qkv_grad,
        head_small[0],
        head_small[1],
        out_grad,
        small[cut : cut + row_count],
        small[:cut].reshape(row_count, experts),
        gate_grad[None],
        up_grad[None],
        down_grad[None],
    )


def solution(mesh):
    placed = (
        P("dp", PLANE, None),
        P("dp", None),
        P("dp", PLANE, None),
        P("dp", PLANE, None),
        P(),
        P("dp", None),
        P(),
        P(),
        P("dp", None),
        P(),
        P(),
        P(EVERY, None, None),
        P(EVERY, None, None),
        P(EVERY, None, None),
    )
    return jax.shard_map(
        body,
        mesh=mesh,
        in_specs=placed,
        out_specs=(
            P("dp", PLANE, None),
            P("dp", PLANE, None),
            P(EVERY),
            P(EVERY, None),
            P(EVERY),
            P(EVERY),
            P(EVERY, None),
            P(EVERY),
            P(EVERY, None),
            P(EVERY, None, None),
            P(EVERY, None, None),
            P(EVERY, None, None),
        ),
        check_vma=False,
    )
```

```python
import functools
import math

import jax
import jax.numpy as jnp
from jax import lax
from jax.experimental import pallas as pl
from jax.experimental.layout import Layout, with_layout_constraint
from jax.experimental.pallas import tpu as pltpu
from jax.sharding import PartitionSpec as P

Q_HEADS = 32
KV_HEADS = 4
HEAD_DIM = 128
EPSILON = 1e-06
NEG_FILL = -1e30
LOG2E = 1.4426950408889634
SCORE_SCALE = LOG2E / math.sqrt(HEAD_DIM)
PLANE = ("blk", "head")
EVERY = ("dp", "blk", "head")
F32 = jnp.float32
BF16 = jnp.bfloat16


def dot_nn(a, b):
    return jnp.dot(a, b, preferred_element_type=F32)


def dot_nt(a, b):
    return lax.dot_general(a, b, (((1,), (1,)), ((), ())), preferred_element_type=F32)


def dot_tn(a, b):
    return lax.dot_general(a, b, (((0,), (0,)), ((), ())), preferred_element_type=F32)


def rms_parts(values):
    scale = lax.rsqrt(jnp.mean(values * values, axis=-1, keepdims=True) + EPSILON)
    return values * scale, scale


def rms_back(grad, unit, scale, gain_vec):
    scaled = grad * gain_vec
    return scale * (scaled - unit * jnp.mean(scaled * unit, axis=-1, keepdims=True))


def lane_sum(values):
    ones = jnp.ones((HEAD_DIM, HEAD_DIM), BF16)
    coarse = values.astype(BF16)
    fine = (values - coarse.astype(F32)).astype(BF16)
    return dot_nn(coarse, ones) + dot_nn(fine, ones)


def head_parts(values):
    scale = lax.rsqrt(lane_sum(values * values) * (1.0 / HEAD_DIM) + EPSILON)
    return values * scale, scale


def head_back(grad, unit, scale, gain_vec):
    scaled = grad * gain_vec
    return scale * (scaled - unit * (lane_sum(scaled * unit) * (1.0 / HEAD_DIM)))


def turn_head(unit, cosines, sines):
    return unit * cosines + pltpu.roll(unit, HEAD_DIM // 2, 1) * sines


def turn_back(grad, cosines, sines):
    return grad * cosines + pltpu.roll(grad * sines, HEAD_DIM // 2, 1)


def pair_of(refs, start):
    return jnp.concatenate([ref[0, :, start : start + HEAD_DIM] for ref in refs], axis=0)


def put_pair(ref, order_ref, pair, start, values):
    size = values.shape[0] // 2
    for i in range(2):
        ref[order_ref[2 * pair + i], :, start : start + HEAD_DIM] = values[
            i * size : (i + 1) * size
        ].astype(ref.dtype)


def add_keys(start, pair, qkv_refs, cosines, sines, k_gain_ref, k_scr, v_scr):
    raw = pair_of(qkv_refs, start)
    unit, _ = head_parts(raw)
    k_scr[pair] = turn_head(unit * k_gain_ref[...], cosines, sines).astype(BF16)
    v_scr[pair, :, :HEAD_DIM] = pair_of(qkv_refs, start + HEAD_DIM).astype(BF16)
    return raw


def hidden_keys(row_seg, key_seg, row_pair, key_pair):
    shape = (row_seg.shape[0], key_seg.shape[1])
    rows = lax.broadcasted_iota(jnp.int32, shape, 0) + (row_pair - key_pair) * shape[0]
    cols = lax.broadcasted_iota(jnp.int32, shape, 1)
    return jnp.where((row_seg == key_seg) & (cols <= rows), 0.0, NEG_FILL)


def attend_kernel(
    heads,
    order_ref,
    low_ref,
    qkv_even_ref,
    qkv_odd_ref,
    cos_ref,
    sin_ref,
    q_gain_ref,
    k_gain_ref,
    seg_row_ref,
    seg_col_ref,
    attn_ref,
    stat_ref,
    k_scr,
    v_scr,
    q_scr,
    acc_scr,
):
    pair = pl.program_id(0)

    qkv_refs = (qkv_even_ref, qkv_odd_ref)

    @pl.when(pair == 0)
    def _():
        v_scr[:, :, HEAD_DIM:] = jnp.ones_like(v_scr[:, :, HEAD_DIM:])

    cosines, sines = cos_ref[0], sin_ref[0]
    add_keys(heads * HEAD_DIM, pair, qkv_refs, cosines, sines, k_gain_ref, k_scr, v_scr)
    for h in range(heads):
        unit, _ = head_parts(pair_of(qkv_refs, h * HEAD_DIM))
        turned = turn_head(unit * q_gain_ref[...], cosines, sines)
        q_scr[h] = (turned * SCORE_SCALE).astype(BF16)
    acc_scr[...] = jnp.zeros_like(acc_scr)
    row_seg = seg_col_ref[0]

    def step(key_pair, carry):
        hide = hidden_keys(row_seg, seg_row_ref[key_pair], pair, key_pair)
        keys, values = k_scr[key_pair], v_scr[key_pair]
        for h in range(heads):
            weights = jnp.exp2(dot_nt(q_scr[h], keys) + hide).astype(BF16)
            acc_scr[h] += dot_nn(weights, values)
        return carry

    lax.fori_loop(low_ref[pair], pair + 1, step, 0)
    for h in range(heads):
        total = acc_scr[h, :, HEAD_DIM:]
        put_pair(attn_ref, order_ref, pair, h * HEAD_DIM, acc_scr[h, :, :HEAD_DIM] / total)
        stat_ref[0, h] = jnp.log2(total)


def attend_back_kernel(
    heads,
    order_ref,
    low_ref,
    qkv_even_ref,
    qkv_odd_ref,
    cos_ref,
    sin_ref,
    q_gain_ref,
    k_gain_ref,
    seg_row_ref,
    seg_col_ref,
    attn_even_ref,
    attn_odd_ref,
    grad_even_ref,
    grad_odd_ref,
    stat_ref,
    out_ref,
    gain_ref,
    k_scr,
    v_scr,
    dk_scr,
    dv_scr,
    q_scr,
    dq_scr,
    delta_scr,
    grad_scr,
    raw_scr,
    turn_scr,
):
    pair = pl.program_id(0)
    pairs = pl.num_programs(0)
    start = heads * HEAD_DIM

    @pl.when(pair == 0)
    def _():
        dk_scr[...] = jnp.zeros_like(dk_scr)
        dv_scr[...] = jnp.zeros_like(dv_scr)
        gain_ref[...] = jnp.zeros_like(gain_ref)

    qkv_refs = (qkv_even_ref, qkv_odd_ref)
    cosines, sines = cos_ref[0], sin_ref[0]
    raw_scr[pair] = add_keys(start, pair, qkv_refs, cosines, sines, k_gain_ref, k_scr, v_scr)
    turn_scr[0, pair] = cosines
    turn_scr[1, pair] = sines
    for h in range(heads):
        unit, _ = head_parts(pair_of(qkv_refs, h * HEAD_DIM))
        turned = turn_head(unit * q_gain_ref[...], cosines, sines)
        q_scr[h] = (turned * SCORE_SCALE).astype(BF16)
        grad = pair_of((grad_even_ref, grad_odd_ref), h * HEAD_DIM)
        attn = pair_of((attn_even_ref, attn_odd_ref), h * HEAD_DIM)
        grad_scr[h] = grad
        delta_scr[h] = lane_sum(grad.astype(F32) * attn.astype(F32))
    dq_scr[...] = jnp.zeros_like(dq_scr)
    row_seg = seg_col_ref[0]

    def step(key_pair, carry):
        hide = hidden_keys(row_seg, seg_row_ref[key_pair], pair, key_pair)
        keys, values = k_scr[key_pair], v_scr[key_pair]
        dk, dv = dk_scr[key_pair], dv_scr[key_pair]
        for h in range(heads):
            grad_rows = grad_scr[h]
            stat = jnp.concatenate([stat_ref[0, h]] * 2, axis=1)
            delta = jnp.concatenate([delta_scr[h]] * 2, axis=1)
            probs = jnp.exp2(dot_nt(q_scr[h], keys) + (hide - stat))
            grad_scores = (probs * (dot_nt(grad_rows, values) - delta)).astype(BF16)
            dk = dk + dot_tn(grad_scores, q_scr[h])
            dv = dv + dot_tn(probs.astype(BF16), grad_rows)
            dq_scr[h] += dot_nn(grad_scores, keys)
        dk_scr[key_pair] = dk
        dv_scr[key_pair] = dv
        return carry

    lax.fori_loop(low_ref[pair], pair + 1, step, 0)
    gain_sum = jnp.zeros((1, HEAD_DIM), F32)
    for h in range(heads):
        unit, scale = head_parts(pair_of(qkv_refs, h * HEAD_DIM))
        grad = turn_back(dq_scr[h] * (SCORE_SCALE / LOG2E), cosines, sines)
        gain_sum = gain_sum + jnp.sum(grad * unit, axis=0, keepdims=True)
        put_pair(
            out_ref, order_ref, pair, h * HEAD_DIM, head_back(grad, unit, scale, q_gain_ref[...])
        )
    gain_ref[0:1, :] += gain_sum

    @pl.when(pair == pairs - 1)
    def _():
        def one(key_pair, carry):
            unit, scale = head_parts(raw_scr[key_pair])
            grad = turn_back(
                dk_scr[key_pair] * (1.0 / LOG2E), turn_scr[0, key_pair], turn_scr[1, key_pair]
            )
            put_pair(
                out_ref, order_ref, key_pair, start, head_back(grad, unit, scale, k_gain_ref[...])
            )
            put_pair(out_ref, order_ref, key_pair, start + HEAD_DIM, dv_scr[key_pair])
            return carry + jnp.sum(grad * unit, axis=0, keepdims=True)

        gain_ref[1:2, :] += lax.fori_loop(0, pairs, one, jnp.zeros((1, HEAD_DIM), F32))


def whole_block(shape):
    zeros = (0,) * len(shape)
    return pl.BlockSpec(shape, lambda pair, order, low: zeros)


def stat_block(heads, rows):
    return pl.BlockSpec((1, heads, rows, HEAD_DIM), lambda pair, order, low: (pair, 0, 0, 0))


def pair_block(shape):
    return pl.BlockSpec((1, *shape), lambda pair, order, low: (pair, 0, 0))


def ordered_blocks(shape):
    return [
        pl.BlockSpec((1, *shape), lambda pair, order, low, i=i: (order[2 * pair + i], 0, 0))
        for i in range(2)
    ]


def attention_inputs(qkv, tables, gains, segment):
    blocks, size, width = qkv.shape
    tables = [table.reshape(blocks // 2, 2 * size, HEAD_DIM) for table in tables]
    rows = segment.reshape(blocks // 2, 1, 2 * size)
    cols = segment.reshape(blocks // 2, 2 * size, 1)
    specs = (
        ordered_blocks((size, width))
        + [pair_block((2 * size, HEAD_DIM))] * 2
        + [whole_block(gain.shape) for gain in gains]
        + [whole_block(rows.shape), pair_block((2 * size, 1))]
    )
    return (qkv, qkv, *tables, *gains, rows, cols), specs


def attend(qkv, tables, gains, segment, order, low, heads):
    blocks, size, _ = qkv.shape
    pairs, rows = blocks // 2, 2 * size
    arrays, specs = attention_inputs(qkv, tables, gains, segment)
    return pl.pallas_call(
        functools.partial(attend_kernel, heads),
        grid_spec=pltpu.PrefetchScalarGridSpec(
            num_scalar_prefetch=2,
            grid=(pairs,),
            in_specs=specs,
            out_specs=[
                whole_block((blocks, size, heads * HEAD_DIM)),
                stat_block(heads, rows),
            ],
            scratch_shapes=[
                pltpu.VMEM((pairs, rows, HEAD_DIM), BF16),
                pltpu.VMEM((pairs, rows, 2 * HEAD_DIM), BF16),
                pltpu.VMEM((heads, rows, HEAD_DIM), BF16),
                pltpu.VMEM((heads, rows, 2 * HEAD_DIM), F32),
            ],
        ),
        out_shape=[
            jax.ShapeDtypeStruct((blocks, size, heads * HEAD_DIM), BF16),
            jax.ShapeDtypeStruct((pairs, heads, rows, HEAD_DIM), F32),
        ],
        compiler_params=pltpu.CompilerParams(vmem_limit_bytes=48 * 2**20),
        cost_estimate=pl.CostEstimate(
            flops=2**24 * blocks * heads, bytes_accessed=qkv.size * 8, transcendentals=0
        ),
    )(order, low, *arrays)


def attend_back(qkv, tables, gains, segment, order, low, heads, attn, grad, stat):
    blocks, size, width = qkv.shape
    pairs, rows = blocks // 2, 2 * size
    arrays, specs = attention_inputs(qkv, tables, gains, segment)
    return pl.pallas_call(
        functools.partial(attend_back_kernel, heads),
        grid_spec=pltpu.PrefetchScalarGridSpec(
            num_scalar_prefetch=2,
            grid=(pairs,),
            in_specs=specs
            + ordered_blocks((size, heads * HEAD_DIM)) * 2
            + [stat_block(heads, rows)],
            out_specs=[whole_block((blocks, size, width)), whole_block((8, HEAD_DIM))],
            scratch_shapes=[pltpu.VMEM((pairs, rows, HEAD_DIM), BF16)] * 2
            + [pltpu.VMEM((pairs, rows, HEAD_DIM), F32)] * 2
            + [
                pltpu.VMEM((heads, rows, HEAD_DIM), BF16),
                pltpu.VMEM((heads, rows, HEAD_DIM), F32),
                pltpu.VMEM((heads, rows, HEAD_DIM), F32),
                pltpu.VMEM((heads, rows, HEAD_DIM), BF16),
                pltpu.VMEM((pairs, rows, HEAD_DIM), F32),
                pltpu.VMEM((2, pairs, rows, HEAD_DIM), F32),
            ],
        ),
        out_shape=[
            jax.ShapeDtypeStruct((blocks, size, width), BF16),
            jax.ShapeDtypeStruct((8, HEAD_DIM), F32),
        ],
        compiler_params=pltpu.CompilerParams(vmem_limit_bytes=56 * 2**20),
        cost_estimate=pl.CostEstimate(
            flops=2**24 * blocks * heads * 2, bytes_accessed=qkv.size * 12, transcendentals=0
        ),
    )(order, low, *arrays, attn, attn, grad, grad, stat)


def project_kernel(counts, normed, *refs):
    pieces, (gain_ref, weight_ref, out_ref, rows_ref) = refs[: len(counts)], refs[len(counts) :]
    block = pl.program_id(0)
    rows = pieces[-1][0]
    place = sum(counts) - counts[-1]
    for ref, count in zip(pieces[-2::-1], counts[-2::-1]):
        rows = jnp.where(block < place, ref[0], rows)
        place = place - count
    if normed:
        unit, _ = rms_parts(rows.astype(F32))
        rows = (unit * gain_ref[...]).astype(BF16)
    rows_ref[0] = rows
    out_ref[0] = dot_nn(rows, weight_ref[...]).astype(out_ref.dtype)


def project(pieces, gain, weight, normed, out_type):
    counts = [piece.shape[0] for piece in pieces]
    _, size, width = pieces[0].shape
    blocks, columns = sum(counts), weight.shape[1]

    def piece_spec(first, count):
        return pl.BlockSpec(
            (1, size, width), lambda i: (jnp.clip(i - first, 0, count - 1), 0, 0)
        )

    firsts = [sum(counts[:i]) for i in range(len(counts))]
    return pl.pallas_call(
        functools.partial(project_kernel, counts, normed),
        grid=(blocks,),
        in_specs=[piece_spec(first, count) for first, count in zip(firsts, counts)]
        + [
            pl.BlockSpec(gain.shape, lambda i: (0, 0)),
            pl.BlockSpec(weight.shape, lambda i: (0, 0), pipeline_mode=pl.Buffered(1)),
        ],
        out_specs=[
            pl.BlockSpec((1, size, columns), lambda i: (i, 0, 0)),
            pl.BlockSpec((1, size, width), lambda i: (i, 0, 0)),
        ],
        out_shape=[
            jax.ShapeDtypeStruct((blocks, size, columns), out_type),
            jax.ShapeDtypeStruct((blocks, size, width), BF16),
        ],
        compiler_params=pltpu.CompilerParams(vmem_limit_bytes=32 * 2**20),
        cost_estimate=pl.CostEstimate(
            flops=blocks * size * width * columns, bytes_accessed=weight.size, transcendentals=0
        ),
    )(*pieces, gain, weight)


def expert_kernel(
    experts,
    expert_ref,
    rows_ref,
    gates_ref,
    cot_ref,
    gate_w_ref,
    up_w_ref,
    down_w_ref,
    gated_ref,
    grad_gate_ref,
    grad_up_ref,
    back_ref,
    out_ref,
):
    width = rows_ref.shape[1]
    rows = rows_ref[...]
    spots = lax.broadcasted_iota(jnp.int32, gates_ref.shape, 1)
    coarse_spot = spots == expert_ref[0]
    fine_spot = spots == expert_ref[0] + experts
    gate = jnp.sum(
        jnp.where(coarse_spot | fine_spot, gates_ref[...].astype(F32), 0.0), axis=1, keepdims=True
    )
    gate_pre = dot_nn(rows, gate_w_ref[...])
    up_pre = dot_nn(rows, up_w_ref[...])
    pulled = dot_nt(cot_ref[...], down_w_ref[...])
    sigma = 1.0 / (1.0 + jnp.exp(-gate_pre))
    swish = gate_pre * sigma
    hidden = (swish * up_pre).astype(BF16).astype(F32)
    gate_grad = jnp.sum(hidden * pulled, axis=1, keepdims=True)
    gated = (hidden * gate).astype(BF16)
    grad_hidden = pulled * gate
    grad_gate = (grad_hidden * up_pre * (sigma + swish * (1.0 - sigma))).astype(BF16)
    grad_up = (grad_hidden * swish).astype(BF16)
    gated_ref[...] = gated
    grad_gate_ref[...] = grad_gate
    grad_up_ref[...] = grad_up
    back_ref[:, :width] = (
        dot_nt(grad_gate, gate_w_ref[...]) + dot_nt(grad_up, up_w_ref[...])
    ).astype(BF16)
    coarse = gate_grad.astype(BF16).astype(F32)
    back_ref[:, width:] = jnp.where(
        coarse_spot, coarse, jnp.where(fine_spot, gate_grad - coarse, 0.0)
    ).astype(BF16)
    out_ref[...] = dot_nn(gated, down_w_ref[...]).astype(BF16)


def expert_pass(came, cot, gate_w, up_w, down_w, expert_id, experts):
    count, full = came.shape
    width, hidden = gate_w.shape
    block = max(b for b in range(16, 385, 16) if count % b == 0)
    extra = full - width

    def rows_of(columns, place=0):
        return pl.BlockSpec((block, columns), lambda i, e: (i, place))

    def kept(shape):
        return pl.BlockSpec(shape, lambda i, e: (0, 0), pipeline_mode=pl.Buffered(1))

    return pl.pallas_call(
        functools.partial(expert_kernel, experts),
        grid_spec=pltpu.PrefetchScalarGridSpec(
            num_scalar_prefetch=1,
            grid=(count // block,),
            in_specs=[
                rows_of(width),
                rows_of(extra, width // extra),
                rows_of(width),
                kept(gate_w.shape),
                kept(up_w.shape),
                kept(down_w.shape),
            ],
            out_specs=[rows_of(hidden)] * 3 + [rows_of(full), rows_of(width)],
        ),
        out_shape=[jax.ShapeDtypeStruct((count, hidden), BF16)] * 3
        + [
            jax.ShapeDtypeStruct((count, full), BF16),
            jax.ShapeDtypeStruct((count, width), BF16),
        ],
        compiler_params=pltpu.CompilerParams(vmem_limit_bytes=58 * 2**20),
        cost_estimate=pl.CostEstimate(
            flops=count * width * hidden * 3, bytes_accessed=count * width * 4, transcendentals=0
        ),
    )(expert_id.reshape(1), came, came, cot, gate_w, up_w, down_w)


def by_rows(array):
    return with_layout_constraint(array, Layout(major_to_minor=tuple(range(array.ndim))))


def ring_steps(ways):
    ring = list(range(1, ways, 2)) + list(range(0, ways, 2))[::-1]
    return [(ring[i], ring[(i + 1) % ways]) for i in range(ways)]


def line_gather(rows, ways):
    held, out = rows, [rows]
    for _ in range(ways - 1):
        held = lax.ppermute(held, "dp", ring_steps(ways))
        out.append(held)
    return jnp.concatenate(out, axis=0)


def ring_jumps(ways, count):
    ring = [a for a, _ in ring_steps(ways)]
    return [(ring[i], ring[(i + count) % ways]) for i in range(ways)]


def line_spread(rows, ways):
    blocks = [lax.ppermute(rows, "dp", ring_jumps(ways, k)) for k in range(1, ways)]
    return jnp.concatenate([rows] + blocks, axis=0)


def line_sum(parts, ways):
    size = parts.shape[0] // ways
    total = parts[:size].astype(F32)
    for k in range(1, ways):
        part = parts[k * size : (k + 1) * size]
        total = total + lax.ppermute(part, "dp", ring_jumps(ways, -k)).astype(F32)
    return total


def line_reduce(part, ways):
    back = [(b, a) for a, b in ring_steps(ways)]
    acc = part(ways - 1)
    for k in range(ways - 2, -1, -1):
        acc = lax.ppermute(acc, "dp", back)
        acc = yield (acc.astype(F32) + part(k).astype(F32)).astype(BF16)


def plane_gather_steps(rows, turn, pair):
    if not pair:
        yield [lax.all_gather(rows, PLANE, axis=0, tiled=False)]
        return
    first, second = plane_flips(turn)
    two = yield jnp.stack([rows, lax.ppermute(rows, PLANE, first)])
    four = yield jnp.concatenate([two, lax.ppermute(two, PLANE, second)])
    yield [four, lax.ppermute(four, PLANE, flips(2))]


def together(*moves):
    held, going = [next(move) for move in moves], True
    while going:
        if len(held) > 1:
            held = jax.tree.map(by_rows, list(tie(*held)))
        going = False
        for i, move in enumerate(moves):
            try:
                held[i] = move.send(held[i])
                going = True
            except StopIteration:
                continue
    return held


def paired(blk_ways, head_ways):
    return blk_ways == 4 and head_ways == 2


def flips(bit):
    return [(i, i ^ bit) for i in range(8)]


def plane_flips(turn):
    return (flips(4), flips(1)) if turn % 2 == 0 else (flips(1), flips(4))


def plane_order(plane_index, plane_ways, turn, pair):
    blocks = jnp.arange(plane_ways, dtype=jnp.int32)
    if not pair:
        return blocks
    away = blocks ^ plane_index
    x, core, y = (away >> 2) & 1, (away >> 1) & 1, away & 1
    near, far = (x, y) if turn % 2 == 0 else (y, x)
    return (core * 4 + far * 2 + near).astype(jnp.int32)


def plane_reduce(product, turn, pair):
    if not pair:
        yield lax.psum_scatter(product(0, None), PLANE, scatter_dimension=0, tiled=False)
        return
    first, second = plane_flips(turn)
    away = lax.ppermute(product(4, 8), PLANE, flips(2))
    parts = yield (product(0, 4).astype(F32) + away.astype(F32)).astype(BF16)
    for half, move in ((2, second), (1, first)):
        came = lax.ppermute(parts[half:], PLANE, move)
        parts = (parts[:half].astype(F32) + came.astype(F32)).astype(BF16)
        if half > 1:
            parts = yield parts
    yield parts[0]


def tie(*arrays):
    return lax.optimization_barrier(arrays)


def every_exchange(rows):
    return lax.all_to_all(rows, EVERY, split_axis=0, concat_axis=0, tiled=True)


def plane_exchange(rows):
    return lax.all_to_all(rows, PLANE, split_axis=0, concat_axis=0, tiled=True)


def body(
    tokens,
    segments,
    routes,
    cotangent,
    attn_gain,
    qkv_weight,
    q_gain,
    k_gain,
    out_weight,
    ffn_gain,
    router_weight,
    gate_weight,
    up_weight,
    down_weight,
):
    seqs, size, width = tokens.shape
    dp_ways = lax.axis_size("dp")
    blk_ways = lax.axis_size("blk")
    head_ways = lax.axis_size("head")
    plane_ways = blk_ways * head_ways
    pair = paired(blk_ways, head_ways)
    dp_index = lax.axis_index("dp")
    plane_index = lax.axis_index("blk") * head_ways + lax.axis_index("head")
    seq_total = segments.shape[1]
    experts = router_weight.shape[1]
    top_count = routes.shape[2]
    capacity = (9 * size * top_count + 8 * experts - 1) // (8 * experts)
    query_dim = Q_HEADS * HEAD_DIM
    kv_dim = KV_HEADS * HEAD_DIM
    heads = Q_HEADS // plane_ways
    share = plane_ways // KV_HEADS
    kv_index = plane_index // share
    local_dim = heads * HEAD_DIM
    extra = -(-2 * experts // 128) * 128

    weight_rows = qkv_weight.shape[0]

    def columns(weight, start, count):
        return lax.dynamic_slice(weight, (0, start), (weight_rows, count))

    qkv_local = lax.all_gather(
        jnp.concatenate(
            [
                columns(qkv_weight, plane_index * local_dim, local_dim),
                columns(qkv_weight, query_dim + kv_index * HEAD_DIM, HEAD_DIM),
                columns(qkv_weight, query_dim + kv_dim + kv_index * HEAD_DIM, HEAD_DIM),
            ],
            axis=1,
        ),
        "dp",
        axis=0,
        tiled=True,
    )

    half = HEAD_DIM // 2
    frequency = 1000000.0 ** (-2.0 * jnp.arange(half, dtype=F32) / HEAD_DIM)
    angles = jnp.arange(seq_total, dtype=jnp.int32).astype(F32)[:, None] * frequency[None, :]
    cosines, sines = jnp.cos(angles), jnp.sin(angles)
    tables = (
        jnp.concatenate([cosines, cosines], axis=1).reshape(plane_ways, size, HEAD_DIM),
        jnp.concatenate([-sines, sines], axis=1).reshape(plane_ways, size, HEAD_DIM),
    )
    gains = (q_gain[None], k_gain[None])
    attn_gain_row, ffn_gain_row = attn_gain[None], ffn_gain[None]

    expert_ids = dp_index * plane_ways + jnp.arange(plane_ways, dtype=jnp.int32)
    before = (
        jnp.arange(size, dtype=jnp.int32)[:, None] > jnp.arange(size, dtype=jnp.int32)[None, :]
    ).astype(BF16)
    slot_ids = jnp.arange(dp_ways * capacity, dtype=jnp.int32)

    spots = jnp.array([[a for a, _ in ring_steps(dp_ways)].index(i) for i in range(dp_ways)], jnp.int32)
    ring_slots = (spots[dp_index] - spots) % dp_ways
    ring = jnp.array([a for a, _ in ring_steps(dp_ways)], jnp.int32)
    dp_index_of_slot = ring[(spots[dp_index] - jnp.arange(dp_ways)) % dp_ways]
    def route_steps():
        yield lows[0]
        yield line_routes

    line_routes = line_spread(routes.reshape(1, seqs * size, top_count), dp_ways)

    def picks_of(s):
        seen = line_routes.reshape(dp_ways, seqs, size, top_count)[:, s]
        seen = seen.reshape(dp_ways * size, top_count)
        chosen = jnp.any(seen[:, :, None] == expert_ids[None, None, :], axis=1)
        chosen = chosen.reshape(dp_ways, size, plane_ways)
        ranks = jnp.einsum(
            "ij,zje->zie", before, chosen.astype(BF16), preferred_element_type=F32
        ).astype(jnp.int32)
        ranks = ranks + jnp.arange(dp_ways, dtype=jnp.int32)[:, None, None] * capacity
        keys = jnp.where(chosen, ranks, -1)

        def table(keys):
            keys = keys.reshape(dp_ways * size, plane_ways).T
            picks = (keys[:, None, :] == slot_ids[None, :, None]).astype(BF16)
            return picks.reshape(plane_ways * dp_ways * capacity, dp_ways * size)

        return table(keys), table(jnp.take(keys, ring_slots, axis=0))


    last = []

    def exchange(rows, move=plane_exchange):
        if last:
            rows, _ = tie(rows, last.pop())
        out = move(rows)
        last.append(out)
        return out

    def pack(line_rows, table):
        return dot_nn(table, line_rows).astype(BF16)

    def unpack(rows, s):
        return dot_tn(picks[s], rows).astype(BF16)

    orders, lows = [], []
    for s in range(seqs):
        blocks = segments[s].reshape(plane_ways // 2, 2 * size)
        lows.append(
            jnp.sum(
                (blocks[None, :, -1] < blocks[:, None, 0]).astype(jnp.int32), axis=1
            ).astype(jnp.int32)
        )
        orders.append(plane_order(plane_index, plane_ways, s, pair))

    inputs, units, scales = [], [], []
    moves = []
    for s in range(seqs):
        rows = tokens[s].astype(F32)
        unit, scale = rms_parts(rows)
        inputs.append(rows)
        units.append(unit)
        scales.append(scale)
        moves.append(plane_gather_steps(tokens[s], s, pair))
    *pieces, line_routes = together(*moves, route_steps())
    picks, straight_picks = zip(*[picks_of(s) for s in range(seqs)])
    pieces, qkv_local = tie(pieces, qkv_local)
    out_columns, qkv_local = tie(
        columns(out_weight, plane_index * local_dim, local_dim), qkv_local
    )
    out_local = lax.all_gather(out_columns, "dp", axis=0, tiled=True)
    pieces = jax.tree.map(by_rows, pieces)

    def times(left, right):
        def product(start, stop):
            rows = left[start:stop]
            count = rows.shape[0]
            out = dot_nt(rows.reshape(count * size, -1), right).astype(BF16)
            return out.reshape(count, size, width)

        return product

    lines, held = [], out_local
    for s in range(seqs):
        rows, held = tie(cotangent[s], held)
        held = line_spread(rows, dp_ways)
        lines.append(held)
    projected, attended, stats, mixes, spread = [], [], [], [], []
    for s in range(seqs):
        qkv, rows = project(pieces[s], attn_gain_row, qkv_local, True, F32)
        spread.append(rows)
        attn, stat = attend(qkv, tables, gains, segments[s], orders[s], lows[s], heads)
        projected.append(qkv)
        attended.append(attn)
        stats.append(stat)
        mixes.append(plane_reduce(times(attn, out_local), s, pair))

    def pack_steps():
        mark = yield lows[0]
        mark = yield mark
        rows, _ = tie(lines[0], mark)
        yield pack(rows, picks[0])

    *mixes, packed = together(*mixes, pack_steps())
    packed, *mixes = tie(packed, *mixes)
    cot_rows = [exchange(packed)]

    middles, normed2s, mid_units, mid_scales, gate_tables, came = [], [], [], [], [], []
    for s in range(seqs):
        middle = inputs[s] + mixes[s].astype(F32)
        unit, scale = rms_parts(middle)
        normed2 = (unit * ffn_gain_row).astype(BF16)
        logits = dot_nn(normed2, router_weight)
        chosen = jnp.any(
            routes[s][:, :, None] == jnp.arange(experts, dtype=jnp.int32)[None, None, :], axis=1
        )
        top = jnp.max(jnp.where(chosen, logits, -jnp.inf), axis=1, keepdims=True)
        powers = jnp.where(chosen, jnp.exp(jnp.where(chosen, logits - top, 0.0)), 0.0)
        gates = powers / jnp.sum(powers, axis=1, keepdims=True)
        coarse = gates.astype(BF16)
        fine = (gates - coarse.astype(F32)).astype(BF16)
        payload = [normed2, coarse, fine]
        if extra > 2 * experts:
            payload.append(jnp.zeros((size, extra - 2 * experts), BF16))
        middles.append(middle)
        normed2s.append(normed2)
        mid_units.append(unit)
        mid_scales.append(scale)
        gate_tables.append(gates)
        line = line_gather(jnp.concatenate(payload, axis=1), dp_ways)
        if s:
            cot_rows.append(exchange(pack(lines[s], picks[s])))
        came.append(exchange(pack(line, picks[s])))

    gate_w, up_w, down_w = gate_weight[0], up_weight[0], down_weight[0]
    expert_id = (dp_index * plane_ways + plane_index).astype(jnp.int32)
    kept, grad_lines, produced = [], [], []
    for s in range(seqs):
        gated, grad_gate, grad_up, back, out = expert_pass(
            came[s], cot_rows[s], gate_w, up_w, down_w, expert_id, experts
        )
        if s:
            back, grad_lines[-1] = tie(back, grad_lines[-1])
        grad_lines.append(exchange(back))
        produced.append(out)
        kept.append((came[s][:, :width], gated, cot_rows[s], grad_gate, grad_up))
    out_lines, grad_mids, reduced = [], [], []
    router_grad = jnp.zeros((width, experts), F32)
    ffn_sum = jnp.zeros((width,), F32)
    for s in range(seqs):
        back = unpack(grad_lines[s], s)
        if s == 0:
            back, kept = tie(back, kept)
        reduced.append(line_sum(back, dp_ways))
    out_lines.append(exchange(produced[0]))
    for s in range(seqs):
        tail = reduced[s][:, width:]
        gates = gate_tables[s]
        grad_gates = tail[:, :experts] + tail[:, experts : 2 * experts]
        grad_logits = (
            gates * (grad_gates - jnp.sum(gates * grad_gates, axis=1, keepdims=True))
        ).astype(BF16)
        router_grad = router_grad + dot_tn(normed2s[s], grad_logits)
        grad_normed2 = reduced[s][:, :width] + dot_nt(grad_logits, router_weight)
        ffn_sum = ffn_sum + jnp.sum(grad_normed2 * mid_units[s], axis=0)
        grad_mids.append(
            cotangent[s].astype(F32)
            + rms_back(grad_normed2, mid_units[s], mid_scales[s], ffn_gain_row)
        )

    gate_grad = sum(dot_tn(rows, grad) for rows, _, _, grad, _ in kept)
    up_grad = sum(dot_tn(rows, grad) for rows, _, _, _, grad in kept)
    down_grad = sum(dot_tn(gated, cot) for _, gated, cot, _, _ in kept)
    *grad_mids, out_lines[0], gate_grad, up_grad, down_grad = tie(
        *grad_mids, out_lines[0], gate_grad, up_grad, down_grad
    )
    devices = dp_ways * plane_ways

    def small_steps():
        rows = yield jnp.concatenate(
            [router_grad.reshape(devices, -1), ffn_sum.reshape(devices, -1)], axis=1
        )
        yield exchange(rows, every_exchange)

    outcome_lines = []

    def outcome_steps():
        outcome_lines.append(dot_tn(straight_picks[0], out_lines[0]).astype(BF16))
        yield outcome_lines[0]

    *pieces, small, _ = together(
        *[plane_gather_steps(grad_mids[s].astype(BF16), s, pair) for s in range(seqs)],
        small_steps(),
        outcome_steps(),
    )
    pieces, small = tie(pieces, small)
    pieces = jax.tree.map(by_rows, pieces)

    def outcome(s):
        if s == len(outcome_lines):
            outcome_lines.append(dot_tn(straight_picks[s], out_lines[s]).astype(BF16))
        back = outcome_lines[s]
        back = lax.psum_scatter(back, "dp", scatter_dimension=0, tiled=True)
        return (middles[s] + back.astype(F32)).astype(BF16)

    for s in range(1, seqs):
        rows, pieces = tie(produced[s], pieces)
        pieces = jax.tree.map(by_rows, pieces)
        out_lines.append(exchange(rows))
    grad_spread, layer_outs = [], [outcome(0)]
    grad_qkvs, grad_ins = [], []
    head_sums = jnp.zeros((2, HEAD_DIM), F32)
    for s in range(seqs):
        grad_attn, rows = project(pieces[s], ffn_gain_row, out_local, False, BF16)
        if s == 0:
            grad_attn, layer_outs[0] = tie(grad_attn, layer_outs[0])
        grad_spread.append(rows)
        grad_qkv, sums = attend_back(
            projected[s],
            tables,
            gains,
            segments[s],
            orders[s],
            lows[s],
            heads,
            attended[s],
            grad_attn,
            stats[s],
        )
        head_sums = head_sums + sums[:2]
        grad_qkvs.append(grad_qkv)
    *grad_qkvs, out_lines[-1] = tie(*grad_qkvs, out_lines[-1])
    head_small = exchange(
        jnp.concatenate(
            [head_sums[0].reshape(devices, -1), head_sums[1].reshape(devices, -1)], axis=1
        ),
        every_exchange,
    )

    def total_over(lefts, rights):
        return sum(
            dot_tn(a.reshape(seq_total, -1), b.reshape(seq_total, -1))
            for a, b in zip(lefts, rights)
        ).astype(BF16)

    total = total_over(spread, grad_qkvs)
    def rows_of_plane(total):
        return plane_exchange(total).reshape(plane_ways, weight_rows // plane_ways, -1)

    out_total = lax.psum_scatter(
        total_over(grad_spread, attended), "dp", scatter_dimension=0, tiled=True
    )
    out_rows = rows_of_plane(out_total)
    sums = [plane_reduce(times(grad_qkvs[s], qkv_local), s, pair) for s in range(seqs)]
    ring_sum = line_reduce(
        lambda k: lax.dynamic_slice_in_dim(
            total, dp_index_of_slot[k] * weight_rows, weight_rows
        ),
        dp_ways,
    )
    held, qkv_rows = [next(move) for move in sums], next(ring_sum)
    qkv_rows, head_small = tie(qkv_rows, head_small)
    for turn in range(dp_ways - 1):
        qkv_rows = ring_sum.send(qkv_rows) if turn else qkv_rows
        if pair and turn:
            qkv_rows, *held = tie(qkv_rows, *held)
            held = [move.send(by_rows(h)) for move, h in zip(sums, held)]
        if turn == 1:
            qkv_rows, out_rows = tie(qkv_rows, out_rows)
    grad_normeds = held

    for s in range(seqs):
        grad_in = rms_back(grad_normeds[s].astype(F32), units[s], scales[s], attn_gain_row)
        grad_ins.append((grad_mids[s] + grad_in).astype(BF16))
    input_grad = jnp.stack(grad_ins)
    layer_out = jnp.stack(layer_outs + [outcome(s) for s in range(1, seqs)])

    def side_by_side(pieces):
        return pieces.transpose(1, 0, 2).reshape(pieces.shape[1], -1)

    out_grad = side_by_side(out_rows).astype(F32)
    pieces = rows_of_plane(qkv_rows).astype(F32)
    row_count = pieces.shape[1]

    def kv_columns(start):
        part = pieces[:, :, start : start + HEAD_DIM]
        return side_by_side(part.reshape(KV_HEADS, share, row_count, HEAD_DIM).sum(axis=1))

    qkv_grad = jnp.concatenate(
        [
            side_by_side(pieces[:, :, :local_dim]),
            kv_columns(local_dim),
            kv_columns(local_dim + HEAD_DIM),
        ],
        axis=1,
    )
    own_rows = lax.dynamic_slice(
        qkv_weight, (plane_index * row_count, 0), (row_count, qkv_weight.shape[1])
    )
    own_gain = lax.dynamic_slice(
        attn_gain, ((dp_index * plane_ways + plane_index) * row_count,), (row_count,)
    )
    attn_gain_grad = jnp.sum(own_rows.astype(F32) * qkv_grad, axis=1) / own_gain

    small = jnp.sum(small, axis=0)
    head_small = jnp.sum(head_small, axis=0).reshape(2, -1)
    cut = row_count * experts
    return (
        layer_out,
        input_grad,
        attn_gain_grad,
        qkv_grad,
        head_small[0],
        head_small[1],
        out_grad,
        small[cut : cut + row_count],
        small[:cut].reshape(row_count, experts),
        gate_grad[None],
        up_grad[None],
        down_grad[None],
    )


def solution(mesh):
    placed = (
        P("dp", PLANE, None),
        P("dp", None),
        P("dp", PLANE, None),
        P("dp", PLANE, None),
        P(),
        P("dp", None),
        P(),
        P(),
        P("dp", None),
        P(),
        P(),
        P(EVERY, None, None),
        P(EVERY, None, None),
        P(EVERY, None, None),
    )
    return jax.shard_map(
        body,
        mesh=mesh,
        in_specs=placed,
        out_specs=(
            P("dp", PLANE, None),
            P("dp", PLANE, None),
            P(EVERY),
            P(EVERY, None),
            P(EVERY),
            P(EVERY),
            P(EVERY, None),
            P(EVERY),
            P(EVERY, None),
            P(EVERY, None, None),
            P(EVERY, None, None),
            P(EVERY, None, None),
        ),
        check_vma=False,
    )
```

```python
import functools
import math

import jax
import jax.numpy as jnp
from jax import lax
from jax.experimental import pallas as pl
from jax.experimental.layout import Layout, with_layout_constraint
from jax.experimental.pallas import tpu as pltpu
from jax.sharding import PartitionSpec as P

Q_HEADS = 32
KV_HEADS = 4
HEAD_DIM = 128
EPSILON = 1e-06
NEG_FILL = -1e30
LOG2E = 1.4426950408889634
SCORE_SCALE = LOG2E / math.sqrt(HEAD_DIM)
PLANE = ("blk", "head")
EVERY = ("dp", "blk", "head")
F32 = jnp.float32
BF16 = jnp.bfloat16


def dot_nn(a, b):
    return jnp.dot(a, b, preferred_element_type=F32)


def dot_nt(a, b):
    return lax.dot_general(a, b, (((1,), (1,)), ((), ())), preferred_element_type=F32)


def dot_tn(a, b):
    return lax.dot_general(a, b, (((0,), (0,)), ((), ())), preferred_element_type=F32)


def rms_parts(values):
    scale = lax.rsqrt(jnp.mean(values * values, axis=-1, keepdims=True) + EPSILON)
    return values * scale, scale


def rms_back(grad, unit, scale, gain_vec):
    scaled = grad * gain_vec
    return scale * (scaled - unit * jnp.mean(scaled * unit, axis=-1, keepdims=True))


def lane_sum(values):
    ones = jnp.ones((HEAD_DIM, HEAD_DIM), BF16)
    coarse = values.astype(BF16)
    fine = (values - coarse.astype(F32)).astype(BF16)
    return dot_nn(coarse, ones) + dot_nn(fine, ones)


def head_parts(values):
    scale = lax.rsqrt(lane_sum(values * values) * (1.0 / HEAD_DIM) + EPSILON)
    return values * scale, scale


def head_back(grad, unit, scale, gain_vec):
    scaled = grad * gain_vec
    return scale * (scaled - unit * (lane_sum(scaled * unit) * (1.0 / HEAD_DIM)))


def turn_head(unit, cosines, sines):
    return unit * cosines + pltpu.roll(unit, HEAD_DIM // 2, 1) * sines


def turn_back(grad, cosines, sines):
    return grad * cosines + pltpu.roll(grad * sines, HEAD_DIM // 2, 1)


def pair_of(refs, start):
    return jnp.concatenate([ref[0, :, start : start + HEAD_DIM] for ref in refs], axis=0)


def put_pair(ref, order_ref, pair, start, values):
    size = values.shape[0] // 2
    for i in range(2):
        ref[order_ref[2 * pair + i], :, start : start + HEAD_DIM] = values[
            i * size : (i + 1) * size
        ].astype(ref.dtype)


def add_keys(start, pair, qkv_refs, cosines, sines, k_gain_ref, k_scr, v_scr):
    raw = pair_of(qkv_refs, start)
    unit, _ = head_parts(raw)
    k_scr[pair] = turn_head(unit * k_gain_ref[...], cosines, sines).astype(BF16)
    v_scr[pair, :, :HEAD_DIM] = pair_of(qkv_refs, start + HEAD_DIM).astype(BF16)
    return raw


def hidden_keys(row_seg, key_seg, row_pair, key_pair):
    shape = (row_seg.shape[0], key_seg.shape[1])
    rows = lax.broadcasted_iota(jnp.int32, shape, 0) + (row_pair - key_pair) * shape[0]
    cols = lax.broadcasted_iota(jnp.int32, shape, 1)
    return jnp.where((row_seg == key_seg) & (cols <= rows), 0.0, NEG_FILL)


def attend_kernel(
    heads,
    order_ref,
    low_ref,
    qkv_even_ref,
    qkv_odd_ref,
    cos_ref,
    sin_ref,
    q_gain_ref,
    k_gain_ref,
    seg_row_ref,
    seg_col_ref,
    attn_ref,
    stat_ref,
    k_scr,
    v_scr,
    q_scr,
    acc_scr,
):
    pair = pl.program_id(0)

    qkv_refs = (qkv_even_ref, qkv_odd_ref)

    @pl.when(pair == 0)
    def _():
        v_scr[:, :, HEAD_DIM:] = jnp.ones_like(v_scr[:, :, HEAD_DIM:])

    cosines, sines = cos_ref[0], sin_ref[0]
    add_keys(heads * HEAD_DIM, pair, qkv_refs, cosines, sines, k_gain_ref, k_scr, v_scr)
    for h in range(heads):
        unit, _ = head_parts(pair_of(qkv_refs, h * HEAD_DIM))
        turned = turn_head(unit * q_gain_ref[...], cosines, sines)
        q_scr[h] = (turned * SCORE_SCALE).astype(BF16)
    acc_scr[...] = jnp.zeros_like(acc_scr)
    row_seg = seg_col_ref[0]

    def step(key_pair, carry):
        hide = hidden_keys(row_seg, seg_row_ref[key_pair], pair, key_pair)
        keys, values = k_scr[key_pair], v_scr[key_pair]
        for h in range(heads):
            weights = jnp.exp2(dot_nt(q_scr[h], keys) + hide).astype(BF16)
            acc_scr[h] += dot_nn(weights, values)
        return carry

    lax.fori_loop(low_ref[pair], pair + 1, step, 0)
    for h in range(heads):
        total = acc_scr[h, :, HEAD_DIM:]
        put_pair(attn_ref, order_ref, pair, h * HEAD_DIM, acc_scr[h, :, :HEAD_DIM] / total)
        stat_ref[0, h] = jnp.log2(total)


def attend_back_kernel(
    heads,
    order_ref,
    low_ref,
    qkv_even_ref,
    qkv_odd_ref,
    cos_ref,
    sin_ref,
    q_gain_ref,
    k_gain_ref,
    seg_row_ref,
    seg_col_ref,
    attn_even_ref,
    attn_odd_ref,
    grad_even_ref,
    grad_odd_ref,
    stat_ref,
    out_ref,
    gain_ref,
    k_scr,
    v_scr,
    dk_scr,
    dv_scr,
    q_scr,
    dq_scr,
    delta_scr,
    grad_scr,
    raw_scr,
    turn_scr,
):
    pair = pl.program_id(0)
    pairs = pl.num_programs(0)
    start = heads * HEAD_DIM

    @pl.when(pair == 0)
    def _():
        dk_scr[...] = jnp.zeros_like(dk_scr)
        dv_scr[...] = jnp.zeros_like(dv_scr)
        gain_ref[...] = jnp.zeros_like(gain_ref)

    qkv_refs = (qkv_even_ref, qkv_odd_ref)
    cosines, sines = cos_ref[0], sin_ref[0]
    raw_scr[pair] = add_keys(start, pair, qkv_refs, cosines, sines, k_gain_ref, k_scr, v_scr)
    turn_scr[0, pair] = cosines
    turn_scr[1, pair] = sines
    for h in range(heads):
        unit, _ = head_parts(pair_of(qkv_refs, h * HEAD_DIM))
        turned = turn_head(unit * q_gain_ref[...], cosines, sines)
        q_scr[h] = (turned * SCORE_SCALE).astype(BF16)
        grad = pair_of((grad_even_ref, grad_odd_ref), h * HEAD_DIM)
        attn = pair_of((attn_even_ref, attn_odd_ref), h * HEAD_DIM)
        grad_scr[h] = grad
        delta_scr[h] = lane_sum(grad.astype(F32) * attn.astype(F32))
    dq_scr[...] = jnp.zeros_like(dq_scr)
    row_seg = seg_col_ref[0]

    def step(key_pair, carry):
        hide = hidden_keys(row_seg, seg_row_ref[key_pair], pair, key_pair)
        keys, values = k_scr[key_pair], v_scr[key_pair]
        dk, dv = dk_scr[key_pair], dv_scr[key_pair]
        for h in range(heads):
            grad_rows = grad_scr[h]
            stat = jnp.concatenate([stat_ref[0, h]] * 2, axis=1)
            delta = jnp.concatenate([delta_scr[h]] * 2, axis=1)
            probs = jnp.exp2(dot_nt(q_scr[h], keys) + (hide - stat))
            grad_scores = (probs * (dot_nt(grad_rows, values) - delta)).astype(BF16)
            dk = dk + dot_tn(grad_scores, q_scr[h])
            dv = dv + dot_tn(probs.astype(BF16), grad_rows)
            dq_scr[h] += dot_nn(grad_scores, keys)
        dk_scr[key_pair] = dk
        dv_scr[key_pair] = dv
        return carry

    lax.fori_loop(low_ref[pair], pair + 1, step, 0)
    gain_sum = jnp.zeros((1, HEAD_DIM), F32)
    for h in range(heads):
        unit, scale = head_parts(pair_of(qkv_refs, h * HEAD_DIM))
        grad = turn_back(dq_scr[h] * (SCORE_SCALE / LOG2E), cosines, sines)
        gain_sum = gain_sum + jnp.sum(grad * unit, axis=0, keepdims=True)
        put_pair(
            out_ref, order_ref, pair, h * HEAD_DIM, head_back(grad, unit, scale, q_gain_ref[...])
        )
    gain_ref[0:1, :] += gain_sum

    @pl.when(pair == pairs - 1)
    def _():
        def one(key_pair, carry):
            unit, scale = head_parts(raw_scr[key_pair])
            grad = turn_back(
                dk_scr[key_pair] * (1.0 / LOG2E), turn_scr[0, key_pair], turn_scr[1, key_pair]
            )
            put_pair(
                out_ref, order_ref, key_pair, start, head_back(grad, unit, scale, k_gain_ref[...])
            )
            put_pair(out_ref, order_ref, key_pair, start + HEAD_DIM, dv_scr[key_pair])
            return carry + jnp.sum(grad * unit, axis=0, keepdims=True)

        gain_ref[1:2, :] += lax.fori_loop(0, pairs, one, jnp.zeros((1, HEAD_DIM), F32))


def whole_block(shape):
    zeros = (0,) * len(shape)
    return pl.BlockSpec(shape, lambda pair, order, low: zeros)


def stat_block(heads, rows):
    return pl.BlockSpec((1, heads, rows, HEAD_DIM), lambda pair, order, low: (pair, 0, 0, 0))


def pair_block(shape):
    return pl.BlockSpec((1, *shape), lambda pair, order, low: (pair, 0, 0))


def ordered_blocks(shape):
    return [
        pl.BlockSpec((1, *shape), lambda pair, order, low, i=i: (order[2 * pair + i], 0, 0))
        for i in range(2)
    ]


def attention_inputs(qkv, tables, gains, segment):
    blocks, size, width = qkv.shape
    tables = [table.reshape(blocks // 2, 2 * size, HEAD_DIM) for table in tables]
    rows = segment.reshape(blocks // 2, 1, 2 * size)
    cols = segment.reshape(blocks // 2, 2 * size, 1)
    specs = (
        ordered_blocks((size, width))
        + [pair_block((2 * size, HEAD_DIM))] * 2
        + [whole_block(gain.shape) for gain in gains]
        + [whole_block(rows.shape), pair_block((2 * size, 1))]
    )
    return (qkv, qkv, *tables, *gains, rows, cols), specs


def attend(qkv, tables, gains, segment, order, low, heads):
    blocks, size, _ = qkv.shape
    pairs, rows = blocks // 2, 2 * size
    arrays, specs = attention_inputs(qkv, tables, gains, segment)
    return pl.pallas_call(
        functools.partial(attend_kernel, heads),
        grid_spec=pltpu.PrefetchScalarGridSpec(
            num_scalar_prefetch=2,
            grid=(pairs,),
            in_specs=specs,
            out_specs=[
                whole_block((blocks, size, heads * HEAD_DIM)),
                stat_block(heads, rows),
            ],
            scratch_shapes=[
                pltpu.VMEM((pairs, rows, HEAD_DIM), BF16),
                pltpu.VMEM((pairs, rows, 2 * HEAD_DIM), BF16),
                pltpu.VMEM((heads, rows, HEAD_DIM), BF16),
                pltpu.VMEM((heads, rows, 2 * HEAD_DIM), F32),
            ],
        ),
        out_shape=[
            jax.ShapeDtypeStruct((blocks, size, heads * HEAD_DIM), BF16),
            jax.ShapeDtypeStruct((pairs, heads, rows, HEAD_DIM), F32),
        ],
        compiler_params=pltpu.CompilerParams(vmem_limit_bytes=48 * 2**20),
        cost_estimate=pl.CostEstimate(
            flops=2**24 * blocks * heads, bytes_accessed=qkv.size * 8, transcendentals=0
        ),
    )(order, low, *arrays)


def attend_back(qkv, tables, gains, segment, order, low, heads, attn, grad, stat):
    blocks, size, width = qkv.shape
    pairs, rows = blocks // 2, 2 * size
    arrays, specs = attention_inputs(qkv, tables, gains, segment)
    return pl.pallas_call(
        functools.partial(attend_back_kernel, heads),
        grid_spec=pltpu.PrefetchScalarGridSpec(
            num_scalar_prefetch=2,
            grid=(pairs,),
            in_specs=specs
            + ordered_blocks((size, heads * HEAD_DIM)) * 2
            + [stat_block(heads, rows)],
            out_specs=[whole_block((blocks, size, width)), whole_block((8, HEAD_DIM))],
            scratch_shapes=[pltpu.VMEM((pairs, rows, HEAD_DIM), BF16)] * 2
            + [pltpu.VMEM((pairs, rows, HEAD_DIM), F32)] * 2
            + [
                pltpu.VMEM((heads, rows, HEAD_DIM), BF16),
                pltpu.VMEM((heads, rows, HEAD_DIM), F32),
                pltpu.VMEM((heads, rows, HEAD_DIM), F32),
                pltpu.VMEM((heads, rows, HEAD_DIM), BF16),
                pltpu.VMEM((pairs, rows, HEAD_DIM), F32),
                pltpu.VMEM((2, pairs, rows, HEAD_DIM), F32),
            ],
        ),
        out_shape=[
            jax.ShapeDtypeStruct((blocks, size, width), BF16),
            jax.ShapeDtypeStruct((8, HEAD_DIM), F32),
        ],
        compiler_params=pltpu.CompilerParams(vmem_limit_bytes=56 * 2**20),
        cost_estimate=pl.CostEstimate(
            flops=2**24 * blocks * heads * 2, bytes_accessed=qkv.size * 12, transcendentals=0
        ),
    )(order, low, *arrays, attn, attn, grad, grad, stat)


def project_kernel(counts, normed, *refs):
    pieces, (gain_ref, weight_ref, out_ref, rows_ref) = refs[: len(counts)], refs[len(counts) :]
    block = pl.program_id(0)
    rows = pieces[-1][0]
    place = sum(counts) - counts[-1]
    for ref, count in zip(pieces[-2::-1], counts[-2::-1]):
        rows = jnp.where(block < place, ref[0], rows)
        place = place - count
    if normed:
        unit, _ = rms_parts(rows.astype(F32))
        rows = (unit * gain_ref[...]).astype(BF16)
    rows_ref[0] = rows
    out_ref[0] = dot_nn(rows, weight_ref[...]).astype(out_ref.dtype)


def project(pieces, gain, weight, normed, out_type):
    counts = [piece.shape[0] for piece in pieces]
    _, size, width = pieces[0].shape
    blocks, columns = sum(counts), weight.shape[1]

    def piece_spec(first, count):
        return pl.BlockSpec(
            (1, size, width), lambda i: (jnp.clip(i - first, 0, count - 1), 0, 0)
        )

    firsts = [sum(counts[:i]) for i in range(len(counts))]
    return pl.pallas_call(
        functools.partial(project_kernel, counts, normed),
        grid=(blocks,),
        in_specs=[piece_spec(first, count) for first, count in zip(firsts, counts)]
        + [
            pl.BlockSpec(gain.shape, lambda i: (0, 0)),
            pl.BlockSpec(weight.shape, lambda i: (0, 0), pipeline_mode=pl.Buffered(1)),
        ],
        out_specs=[
            pl.BlockSpec((1, size, columns), lambda i: (i, 0, 0)),
            pl.BlockSpec((1, size, width), lambda i: (i, 0, 0)),
        ],
        out_shape=[
            jax.ShapeDtypeStruct((blocks, size, columns), out_type),
            jax.ShapeDtypeStruct((blocks, size, width), BF16),
        ],
        compiler_params=pltpu.CompilerParams(vmem_limit_bytes=32 * 2**20),
        cost_estimate=pl.CostEstimate(
            flops=blocks * size * width * columns, bytes_accessed=weight.size, transcendentals=0
        ),
    )(*pieces, gain, weight)


def expert_kernel(
    experts,
    expert_ref,
    rows_ref,
    gates_ref,
    cot_ref,
    gate_w_ref,
    up_w_ref,
    down_w_ref,
    gated_ref,
    grad_gate_ref,
    grad_up_ref,
    back_ref,
    out_ref,
):
    width = rows_ref.shape[1]
    rows = rows_ref[...]
    spots = lax.broadcasted_iota(jnp.int32, gates_ref.shape, 1)
    coarse_spot = spots == expert_ref[0]
    fine_spot = spots == expert_ref[0] + experts
    gate = jnp.sum(
        jnp.where(coarse_spot | fine_spot, gates_ref[...].astype(F32), 0.0), axis=1, keepdims=True
    )
    gate_pre = dot_nn(rows, gate_w_ref[...])
    up_pre = dot_nn(rows, up_w_ref[...])
    pulled = dot_nt(cot_ref[...], down_w_ref[...])
    sigma = 1.0 / (1.0 + jnp.exp(-gate_pre))
    swish = gate_pre * sigma
    hidden = (swish * up_pre).astype(BF16).astype(F32)
    gate_grad = jnp.sum(hidden * pulled, axis=1, keepdims=True)
    gated = (hidden * gate).astype(BF16)
    grad_hidden = pulled * gate
    grad_gate = (grad_hidden * up_pre * (sigma + swish * (1.0 - sigma))).astype(BF16)
    grad_up = (grad_hidden * swish).astype(BF16)
    gated_ref[...] = gated
    grad_gate_ref[...] = grad_gate
    grad_up_ref[...] = grad_up
    back_ref[:, :width] = (
        dot_nt(grad_gate, gate_w_ref[...]) + dot_nt(grad_up, up_w_ref[...])
    ).astype(BF16)
    coarse = gate_grad.astype(BF16).astype(F32)
    back_ref[:, width:] = jnp.where(
        coarse_spot, coarse, jnp.where(fine_spot, gate_grad - coarse, 0.0)
    ).astype(BF16)
    out_ref[...] = dot_nn(gated, down_w_ref[...]).astype(BF16)


def expert_pass(came, cot, gate_w, up_w, down_w, expert_id, experts):
    count, full = came.shape
    width, hidden = gate_w.shape
    block = max(b for b in range(16, 385, 16) if count % b == 0)
    extra = full - width

    def rows_of(columns, place=0):
        return pl.BlockSpec((block, columns), lambda i, e: (i, place))

    def kept(shape):
        return pl.BlockSpec(shape, lambda i, e: (0, 0), pipeline_mode=pl.Buffered(1))

    return pl.pallas_call(
        functools.partial(expert_kernel, experts),
        grid_spec=pltpu.PrefetchScalarGridSpec(
            num_scalar_prefetch=1,
            grid=(count // block,),
            in_specs=[
                rows_of(width),
                rows_of(extra, width // extra),
                rows_of(width),
                kept(gate_w.shape),
                kept(up_w.shape),
                kept(down_w.shape),
            ],
            out_specs=[rows_of(hidden)] * 3 + [rows_of(full), rows_of(width)],
        ),
        out_shape=[jax.ShapeDtypeStruct((count, hidden), BF16)] * 3
        + [
            jax.ShapeDtypeStruct((count, full), BF16),
            jax.ShapeDtypeStruct((count, width), BF16),
        ],
        compiler_params=pltpu.CompilerParams(vmem_limit_bytes=58 * 2**20),
        cost_estimate=pl.CostEstimate(
            flops=count * width * hidden * 3, bytes_accessed=count * width * 4, transcendentals=0
        ),
    )(expert_id.reshape(1), came, came, cot, gate_w, up_w, down_w)


def by_rows(array):
    return with_layout_constraint(array, Layout(major_to_minor=tuple(range(array.ndim))))


def ring_steps(ways):
    ring = list(range(1, ways, 2)) + list(range(0, ways, 2))[::-1]
    return [(ring[i], ring[(i + 1) % ways]) for i in range(ways)]


def line_gather(rows, ways):
    held, out = rows, [rows]
    for _ in range(ways - 1):
        held = lax.ppermute(held, "dp", ring_steps(ways))
        out.append(held)
    return jnp.concatenate(out, axis=0)


def ring_jumps(ways, count):
    ring = [a for a, _ in ring_steps(ways)]
    return [(ring[i], ring[(i + count) % ways]) for i in range(ways)]


def line_spread(rows, ways):
    blocks = [lax.ppermute(rows, "dp", ring_jumps(ways, k)) for k in range(1, ways)]
    return jnp.concatenate([rows] + blocks, axis=0)


def line_sum(parts, ways):
    size = parts.shape[0] // ways
    total = parts[:size].astype(F32)
    for k in range(1, ways):
        part = parts[k * size : (k + 1) * size]
        total = total + lax.ppermute(part, "dp", ring_jumps(ways, -k)).astype(F32)
    return total


def line_reduce(part, ways):
    back = [(b, a) for a, b in ring_steps(ways)]
    acc = part(ways - 1)
    for k in range(ways - 2, -1, -1):
        acc = lax.ppermute(acc, "dp", back)
        acc = yield (acc.astype(F32) + part(k).astype(F32)).astype(BF16)


def plane_gather_steps(rows, turn, pair):
    if not pair:
        yield [lax.all_gather(rows, PLANE, axis=0, tiled=False)]
        return
    first, second = plane_flips(turn)
    two = yield jnp.stack([rows, lax.ppermute(rows, PLANE, first)])
    four = yield jnp.concatenate([two, lax.ppermute(two, PLANE, second)])
    yield [four, lax.ppermute(four, PLANE, flips(2))]


def together(*moves):
    held, going = [next(move) for move in moves], True
    while going:
        if len(held) > 1:
            held = jax.tree.map(by_rows, list(tie(*held)))
        going = False
        for i, move in enumerate(moves):
            try:
                held[i] = move.send(held[i])
                going = True
            except StopIteration:
                continue
    return held


def paired(blk_ways, head_ways):
    return blk_ways == 4 and head_ways == 2


def flips(bit):
    return [(i, i ^ bit) for i in range(8)]


def plane_flips(turn):
    return (flips(4), flips(1)) if turn % 2 == 0 else (flips(1), flips(4))


def plane_order(plane_index, plane_ways, turn, pair):
    blocks = jnp.arange(plane_ways, dtype=jnp.int32)
    if not pair:
        return blocks
    away = blocks ^ plane_index
    x, core, y = (away >> 2) & 1, (away >> 1) & 1, away & 1
    near, far = (x, y) if turn % 2 == 0 else (y, x)
    return (core * 4 + far * 2 + near).astype(jnp.int32)


def plane_reduce(product, turn, pair):
    if not pair:
        yield lax.psum_scatter(product(0, None), PLANE, scatter_dimension=0, tiled=False)
        return
    first, second = plane_flips(turn)
    away = lax.ppermute(product(4, 8), PLANE, flips(2))
    parts = yield (product(0, 4).astype(F32) + away.astype(F32)).astype(BF16)
    for half, move in ((2, second), (1, first)):
        came = lax.ppermute(parts[half:], PLANE, move)
        parts = (parts[:half].astype(F32) + came.astype(F32)).astype(BF16)
        if half > 1:
            parts = yield parts
    yield parts[0]


def tie(*arrays):
    return lax.optimization_barrier(arrays)


def every_exchange(rows):
    return lax.all_to_all(rows, EVERY, split_axis=0, concat_axis=0, tiled=True)


def plane_exchange(rows):
    return lax.all_to_all(rows, PLANE, split_axis=0, concat_axis=0, tiled=True)


def body(
    tokens,
    segments,
    routes,
    cotangent,
    attn_gain,
    qkv_weight,
    q_gain,
    k_gain,
    out_weight,
    ffn_gain,
    router_weight,
    gate_weight,
    up_weight,
    down_weight,
):
    seqs, size, width = tokens.shape
    dp_ways = lax.axis_size("dp")
    blk_ways = lax.axis_size("blk")
    head_ways = lax.axis_size("head")
    plane_ways = blk_ways * head_ways
    pair = paired(blk_ways, head_ways)
    dp_index = lax.axis_index("dp")
    plane_index = lax.axis_index("blk") * head_ways + lax.axis_index("head")
    seq_total = segments.shape[1]
    experts = router_weight.shape[1]
    top_count = routes.shape[2]
    capacity = (9 * size * top_count + 8 * experts - 1) // (8 * experts)
    query_dim = Q_HEADS * HEAD_DIM
    kv_dim = KV_HEADS * HEAD_DIM
    heads = Q_HEADS // plane_ways
    share = plane_ways // KV_HEADS
    kv_index = plane_index // share
    local_dim = heads * HEAD_DIM
    extra = -(-2 * experts // 128) * 128

    weight_rows = qkv_weight.shape[0]

    def columns(weight, start, count):
        return lax.dynamic_slice(weight, (0, start), (weight_rows, count))

    qkv_local = lax.all_gather(
        jnp.concatenate(
            [
                columns(qkv_weight, plane_index * local_dim, local_dim),
                columns(qkv_weight, query_dim + kv_index * HEAD_DIM, HEAD_DIM),
                columns(qkv_weight, query_dim + kv_dim + kv_index * HEAD_DIM, HEAD_DIM),
            ],
            axis=1,
        ),
        "dp",
        axis=0,
        tiled=True,
    )

    half = HEAD_DIM // 2
    frequency = 1000000.0 ** (-2.0 * jnp.arange(half, dtype=F32) / HEAD_DIM)
    angles = jnp.arange(seq_total, dtype=jnp.int32).astype(F32)[:, None] * frequency[None, :]
    cosines, sines = jnp.cos(angles), jnp.sin(angles)
    tables = (
        jnp.concatenate([cosines, cosines], axis=1).reshape(plane_ways, size, HEAD_DIM),
        jnp.concatenate([-sines, sines], axis=1).reshape(plane_ways, size, HEAD_DIM),
    )
    gains = (q_gain[None], k_gain[None])
    attn_gain_row, ffn_gain_row = attn_gain[None], ffn_gain[None]

    expert_ids = dp_index * plane_ways + jnp.arange(plane_ways, dtype=jnp.int32)
    before = (
        jnp.arange(size, dtype=jnp.int32)[:, None] > jnp.arange(size, dtype=jnp.int32)[None, :]
    ).astype(BF16)
    slot_ids = jnp.arange(dp_ways * capacity, dtype=jnp.int32)

    spots = jnp.array([[a for a, _ in ring_steps(dp_ways)].index(i) for i in range(dp_ways)], jnp.int32)
    ring_slots = (spots[dp_index] - spots) % dp_ways
    ring = jnp.array([a for a, _ in ring_steps(dp_ways)], jnp.int32)
    dp_index_of_slot = ring[(spots[dp_index] - jnp.arange(dp_ways)) % dp_ways]
    def route_steps():
        yield lows[0]
        yield line_routes

    line_routes = line_spread(routes.reshape(1, seqs * size, top_count), dp_ways)

    def picks_of(s):
        seen = line_routes.reshape(dp_ways, seqs, size, top_count)[:, s]
        seen = seen.reshape(dp_ways * size, top_count)
        chosen = jnp.any(seen[:, :, None] == expert_ids[None, None, :], axis=1)
        chosen = chosen.reshape(dp_ways, size, plane_ways)
        ranks = jnp.einsum(
            "ij,zje->zie", before, chosen.astype(BF16), preferred_element_type=F32
        ).astype(jnp.int32)
        ranks = ranks + jnp.arange(dp_ways, dtype=jnp.int32)[:, None, None] * capacity
        keys = jnp.where(chosen, ranks, -1)

        def table(keys):
            keys = keys.reshape(dp_ways * size, plane_ways).T
            picks = (keys[:, None, :] == slot_ids[None, :, None]).astype(BF16)
            return picks.reshape(plane_ways * dp_ways * capacity, dp_ways * size)

        return table(keys), table(jnp.take(keys, ring_slots, axis=0))


    last = []

    def exchange(rows, move=plane_exchange):
        if last:
            rows, _ = tie(rows, last.pop())
        out = move(rows)
        last.append(out)
        return out

    def pack(line_rows, table):
        return dot_nn(table, line_rows).astype(BF16)

    def unpack(rows, s):
        return dot_tn(picks[s], rows).astype(BF16)

    orders, lows = [], []
    for s in range(seqs):
        blocks = segments[s].reshape(plane_ways // 2, 2 * size)
        lows.append(
            jnp.sum(
                (blocks[None, :, -1] < blocks[:, None, 0]).astype(jnp.int32), axis=1
            ).astype(jnp.int32)
        )
        orders.append(plane_order(plane_index, plane_ways, s, pair))

    inputs, units, scales = [], [], []
    moves = []
    for s in range(seqs):
        rows = tokens[s].astype(F32)
        unit, scale = rms_parts(rows)
        inputs.append(rows)
        units.append(unit)
        scales.append(scale)
        moves.append(plane_gather_steps(tokens[s], s, pair))
    *pieces, line_routes = together(*moves, route_steps())
    picks, straight_picks = zip(*[picks_of(s) for s in range(seqs)])
    pieces, qkv_local = tie(pieces, qkv_local)
    out_columns, qkv_local = tie(
        columns(out_weight, plane_index * local_dim, local_dim), qkv_local
    )
    out_local = lax.all_gather(out_columns, "dp", axis=0, tiled=True)
    pieces = jax.tree.map(by_rows, pieces)

    def times(left, right):
        def product(start, stop):
            rows = left[start:stop]
            count = rows.shape[0]
            out = dot_nt(rows.reshape(count * size, -1), right).astype(BF16)
            return out.reshape(count, size, width)

        return product

    lines, held = [], out_local
    for s in range(seqs):
        rows, held = tie(cotangent[s], held)
        held = line_spread(rows, dp_ways)
        lines.append(held)
    projected, attended, stats, mixes, spread = [], [], [], [], []
    for s in range(seqs):
        qkv, rows = project(pieces[s], attn_gain_row, qkv_local, True, F32)
        spread.append(rows)
        attn, stat = attend(qkv, tables, gains, segments[s], orders[s], lows[s], heads)
        projected.append(qkv)
        attended.append(attn)
        stats.append(stat)
        mixes.append(plane_reduce(times(attn, out_local), s, pair))

    def pack_steps():
        mark = yield lows[0]
        mark = yield mark
        rows, _ = tie(lines[0], mark)
        yield pack(rows, picks[0])

    *mixes, packed = together(*mixes, pack_steps())
    packed, *mixes = tie(packed, *mixes)
    cot_rows = [exchange(packed)]

    middles, normed2s, mid_units, mid_scales, gate_tables, came = [], [], [], [], [], []
    for s in range(seqs):
        middle = inputs[s] + mixes[s].astype(F32)
        unit, scale = rms_parts(middle)
        normed2 = (unit * ffn_gain_row).astype(BF16)
        logits = dot_nn(normed2, router_weight)
        chosen = jnp.any(
            routes[s][:, :, None] == jnp.arange(experts, dtype=jnp.int32)[None, None, :], axis=1
        )
        top = jnp.max(jnp.where(chosen, logits, -jnp.inf), axis=1, keepdims=True)
        powers = jnp.where(chosen, jnp.exp(jnp.where(chosen, logits - top, 0.0)), 0.0)
        gates = powers / jnp.sum(powers, axis=1, keepdims=True)
        coarse = gates.astype(BF16)
        fine = (gates - coarse.astype(F32)).astype(BF16)
        payload = [normed2, coarse, fine]
        if extra > 2 * experts:
            payload.append(jnp.zeros((size, extra - 2 * experts), BF16))
        middles.append(middle)
        normed2s.append(normed2)
        mid_units.append(unit)
        mid_scales.append(scale)
        gate_tables.append(gates)
        line = line_gather(jnp.concatenate(payload, axis=1), dp_ways)
        if s:
            cot_rows.append(exchange(pack(lines[s], picks[s])))
        came.append(exchange(pack(line, picks[s])))

    gate_w, up_w, down_w = gate_weight[0], up_weight[0], down_weight[0]
    expert_id = (dp_index * plane_ways + plane_index).astype(jnp.int32)
    kept, grad_lines, produced = [], [], []
    for s in range(seqs):
        gated, grad_gate, grad_up, back, out = expert_pass(
            came[s], cot_rows[s], gate_w, up_w, down_w, expert_id, experts
        )
        if s:
            back, grad_lines[-1] = tie(back, grad_lines[-1])
        grad_lines.append(exchange(back))
        produced.append(out)
        kept.append((came[s][:, :width], gated, cot_rows[s], grad_gate, grad_up))
    out_lines, grad_mids, reduced = [], [], []
    router_grad = jnp.zeros((width, experts), F32)
    ffn_sum = jnp.zeros((width,), F32)
    for s in range(seqs):
        back = unpack(grad_lines[s], s)
        if s == 0:
            back, kept = tie(back, kept)
        reduced.append(line_sum(back, dp_ways))
    out_lines.append(exchange(produced[0]))
    for s in range(seqs):
        tail = reduced[s][:, width:]
        gates = gate_tables[s]
        grad_gates = tail[:, :experts] + tail[:, experts : 2 * experts]
        grad_logits = (
            gates * (grad_gates - jnp.sum(gates * grad_gates, axis=1, keepdims=True))
        ).astype(BF16)
        router_grad = router_grad + dot_tn(normed2s[s], grad_logits)
        grad_normed2 = reduced[s][:, :width] + dot_nt(grad_logits, router_weight)
        ffn_sum = ffn_sum + jnp.sum(grad_normed2 * mid_units[s], axis=0)
        grad_mids.append(
            cotangent[s].astype(F32)
            + rms_back(grad_normed2, mid_units[s], mid_scales[s], ffn_gain_row)
        )

    gate_grad = sum(dot_tn(rows, grad) for rows, _, _, grad, _ in kept)
    up_grad = sum(dot_tn(rows, grad) for rows, _, _, _, grad in kept)
    down_grad = sum(dot_tn(gated, cot) for _, gated, cot, _, _ in kept)
    grad_sends = [grad_mid.astype(BF16) for grad_mid in grad_mids]
    *grad_sends, out_lines[0], gate_grad, up_grad, down_grad = tie(
        *grad_sends, out_lines[0], gate_grad, up_grad, down_grad
    )
    devices = dp_ways * plane_ways

    def small_steps():
        rows = yield jnp.concatenate(
            [router_grad.reshape(devices, -1), ffn_sum.reshape(devices, -1)], axis=1
        )
        yield exchange(rows, every_exchange)

    outcome_lines = []

    def outcome_steps():
        outcome_lines.append(dot_tn(straight_picks[0], out_lines[0]).astype(BF16))
        yield outcome_lines[0]

    *pieces, small, _ = together(
        *[plane_gather_steps(by_rows(grad_sends[s]), s, pair) for s in range(seqs)],
        small_steps(),
        outcome_steps(),
    )
    pieces, small = tie(pieces, small)
    pieces = jax.tree.map(by_rows, pieces)

    def outcome(s):
        if s == len(outcome_lines):
            outcome_lines.append(dot_tn(straight_picks[s], out_lines[s]).astype(BF16))
        back = outcome_lines[s]
        back = lax.psum_scatter(back, "dp", scatter_dimension=0, tiled=True)
        return (middles[s] + back.astype(F32)).astype(BF16)

    for s in range(1, seqs):
        rows, pieces = tie(produced[s], pieces)
        pieces = jax.tree.map(by_rows, pieces)
        out_lines.append(exchange(rows))
    grad_spread, layer_outs = [], [outcome(0)]
    grad_qkvs, grad_ins = [], []
    head_sums = jnp.zeros((2, HEAD_DIM), F32)
    for s in range(seqs):
        grad_attn, rows = project(pieces[s], ffn_gain_row, out_local, False, BF16)
        if s == 0:
            grad_attn, layer_outs[0] = tie(grad_attn, layer_outs[0])
        grad_spread.append(rows)
        grad_qkv, sums = attend_back(
            projected[s],
            tables,
            gains,
            segments[s],
            orders[s],
            lows[s],
            heads,
            attended[s],
            grad_attn,
            stats[s],
        )
        head_sums = head_sums + sums[:2]
        grad_qkvs.append(grad_qkv)
    *grad_qkvs, out_lines[-1] = tie(*grad_qkvs, out_lines[-1])
    head_small = exchange(
        jnp.concatenate(
            [head_sums[0].reshape(devices, -1), head_sums[1].reshape(devices, -1)], axis=1
        ),
        every_exchange,
    )

    def total_over(lefts, rights):
        return sum(
            dot_tn(a.reshape(seq_total, -1), b.reshape(seq_total, -1))
            for a, b in zip(lefts, rights)
        ).astype(BF16)

    total = total_over(spread, grad_qkvs)
    def rows_of_plane(total):
        return plane_exchange(total).reshape(plane_ways, weight_rows // plane_ways, -1)

    out_total = lax.psum_scatter(
        total_over(grad_spread, attended), "dp", scatter_dimension=0, tiled=True
    )
    out_rows = rows_of_plane(out_total)
    sums = [plane_reduce(times(grad_qkvs[s], qkv_local), s, pair) for s in range(seqs)]
    ring_sum = line_reduce(
        lambda k: lax.dynamic_slice_in_dim(
            total, dp_index_of_slot[k] * weight_rows, weight_rows
        ),
        dp_ways,
    )
    held, qkv_rows = [next(move) for move in sums], next(ring_sum)
    qkv_rows, head_small = tie(qkv_rows, head_small)
    for turn in range(dp_ways - 1):
        qkv_rows = ring_sum.send(qkv_rows) if turn else qkv_rows
        if pair and turn == dp_ways - 2:
            _, *held = tie(qkv_rows, *held)
        elif pair and turn:
            qkv_rows, *held = tie(qkv_rows, *held)
        if pair and turn:
            held = [move.send(by_rows(h)) for move, h in zip(sums, held)]
        if turn == 1:
            qkv_rows, out_rows = tie(qkv_rows, out_rows)
    grad_normeds = held

    for s in range(seqs):
        grad_in = rms_back(grad_normeds[s].astype(F32), units[s], scales[s], attn_gain_row)
        grad_ins.append((grad_mids[s] + grad_in).astype(BF16))
    input_grad = jnp.stack(grad_ins)
    layer_out = jnp.stack(layer_outs + [outcome(s) for s in range(1, seqs)])

    def side_by_side(pieces):
        return pieces.transpose(1, 0, 2).reshape(pieces.shape[1], -1)

    out_grad = side_by_side(out_rows).astype(F32)
    pieces = rows_of_plane(qkv_rows).astype(F32)
    row_count = pieces.shape[1]

    def kv_columns(start):
        part = pieces[:, :, start : start + HEAD_DIM]
        return side_by_side(part.reshape(KV_HEADS, share, row_count, HEAD_DIM).sum(axis=1))

    qkv_grad = jnp.concatenate(
        [
            side_by_side(pieces[:, :, :local_dim]),
            kv_columns(local_dim),
            kv_columns(local_dim + HEAD_DIM),
        ],
        axis=1,
    )
    own_rows = lax.dynamic_slice(
        qkv_weight, (plane_index * row_count, 0), (row_count, qkv_weight.shape[1])
    )
    own_gain = lax.dynamic_slice(
        attn_gain, ((dp_index * plane_ways + plane_index) * row_count,), (row_count,)
    )
    attn_gain_grad = jnp.sum(own_rows.astype(F32) * qkv_grad, axis=1) / own_gain

    small = jnp.sum(small, axis=0)
    head_small = jnp.sum(head_small, axis=0).reshape(2, -1)
    cut = row_count * experts
    return (
        layer_out,
        input_grad,
        attn_gain_grad,
        qkv_grad,
        head_small[0],
        head_small[1],
        out_grad,
        small[cut : cut + row_count],
        small[:cut].reshape(row_count, experts),
        gate_grad[None],
        up_grad[None],
        down_grad[None],
    )


def solution(mesh):
    placed = (
        P("dp", PLANE, None),
        P("dp", None),
        P("dp", PLANE, None),
        P("dp", PLANE, None),
        P(),
        P("dp", None),
        P(),
        P(),
        P("dp", None),
        P(),
        P(),
        P(EVERY, None, None),
        P(EVERY, None, None),
        P(EVERY, None, None),
    )
    return jax.shard_map(
        body,
        mesh=mesh,
        in_specs=placed,
        out_specs=(
            P("dp", PLANE, None),
            P("dp", PLANE, None),
            P(EVERY),
            P(EVERY, None),
            P(EVERY),
            P(EVERY),
            P(EVERY, None),
            P(EVERY),
            P(EVERY, None),
            P(EVERY, None, None),
            P(EVERY, None, None),
            P(EVERY, None, None),
        ),
        check_vma=False,
    )
```
